32 devices in a mesh: dp: 4 (over z), fsdp: 8 (over y, x, core).
Axes of the slice: x: 2, y: 2, z: 4, core: 2. Of those that a mesh axis runs over, the one named last changes fastest.
Arguments:
- long_x: float32 [32, 1024, 768], P(('dp', 'fsdp')), may hold values from -6 to 6
- short_x: float32 [32, 512, 768], P(('dp', 'fsdp')), may hold values from -6 to 6
- long_len: int32 [32], P(('dp', 'fsdp')), may hold values from 256 to 1024
- short_len: int32 [32], P(('dp', 'fsdp')), may hold values from 128 to 512
- expert_ids: int32 [49152, 1], P(('dp', 'fsdp')), may hold values from 0 to 7; in each aligned block of 1536 rows (0 to 1535, 1536 to 3071, ...) at most 256 rows name the same one
- ln1_gain: bfloat16 [768], P(('dp', 'fsdp')), may hold values from 0.5 to 1.5
- ln1_bias: bfloat16 [768], P(('dp', 'fsdp')), may hold values from -1.5 to 1.5
- w_qkv: bfloat16 [768, 2304], P(('dp', 'fsdp')), may hold values from -0.21875 to 0.21875
- w_proj: bfloat16 [768, 768], P(None, ('dp', 'fsdp')), may hold values from -1.75 to 1.75
- ln2_gain: bfloat16 [768], P(('dp', 'fsdp')), may hold values from 0.5 to 1.5
- ln2_bias: bfloat16 [768], P(('dp', 'fsdp')), may hold values from -1.5 to 1.5
- w_up: bfloat16 [8, 768, 3072], P('fsdp', None, 'dp'), may hold values from -0.21875 to 0.21875
- w_down: bfloat16 [8, 3072, 768], P('fsdp', 'dp'), may hold values from -0.109375 to 0.109375
- long_cot: float32 [32, 1024, 768], P(('dp', 'fsdp')), may hold values from -6 to 6
- short_cot: float32 [32, 512, 768], P(('dp', 'fsdp')), may hold values from -6 to 6
Outputs:
- long_out: float32 [32, 1024, 768], P(('dp', 'fsdp'))
- short_out: float32 [32, 512, 768], P(('dp', 'fsdp'))
- long_grad: float32 [32, 1024, 768], P(('dp', 'fsdp'))
- short_grad: float32 [32, 512, 768], P(('dp', 'fsdp'))
- grad_ln1_gain: float32 [768], P(('dp', 'fsdp'))
- grad_ln1_bias: float32 [768], P(('dp', 'fsdp'))
- grad_qkv: float32 [768, 2304], P(('dp', 'fsdp'))
- grad_proj: float32 [768, 768], P(None, ('dp', 'fsdp'))
- grad_ln2_gain: float32 [768], P(('dp', 'fsdp'))
- grad_ln2_bias: float32 [768], P(('dp', 'fsdp'))
- grad_up: float32 [8, 768, 3072], P('fsdp', None, 'dp')
- grad_down: float32 [8, 3072, 768], P('fsdp', 'dp')
The draws below stay inside these ranges and needn't reach their ends.
Inputs may be any that keep to these rules, and one draw needn't show every extreme that they name: `expert_ids`: in each aligned block of 1536 rows (the token slots of one device), no expert is named by more than 256 rows.
All inputs are finite; a program needn't handle non-finite values.
Results may differ from the reference program's by a relative error of at most 0.012.
Values may be sent and summed in bfloat16 or wider, within the bound.
A program may use at most 320 MiB of HBM per device.

```python
import math
import jax
import jax.numpy as jnp
import numpy as np
from jax import lax

D = 768
HEADS = 12
HEAD_DIM = 64
FF = 3072
LONG = 1024
SHORT = 512
EXPERTS = 8
TOK_DEV = 1536
CAP = 256
NLONG = 32
NSHORT = 32
TOKENS = 49152
N_DP = 4
N_FSDP = 8


def plant(drawn, key, smallest, top_value):
    shape = drawn.shape
    place = [jax.random.randint(jax.random.fold_in(key, axis), (), 0, shape[axis]) for axis in range(len(shape))]
    drawn = drawn.at[tuple(place)].set(smallest)
    longest = shape.index(max(shape))
    place[longest] = (place[longest] + 1) % shape[longest]
    return drawn.at[tuple(place)].set(top_value)


def spiked(values, key, source, target, shards_of, factor):
    def block_of(dim):
        return (jnp.arange(values.shape[dim]) // (values.shape[dim] // shards_of)).reshape((-1,) + (1,) * (values.ndim - 1 - dim))

    first = jax.random.permutation(key, shards_of)[block_of(target)]
    far = (block_of(target) + shards_of // 2) % shards_of
    return jnp.where((block_of(source) == first) | (block_of(source) == far), factor * values, values)


def levels(key, shape, pieces, smallest, top_value):
    level = 1.0
    for dim, blocks in pieces:
        steps = jax.random.uniform(jax.random.fold_in(jax.random.fold_in(key, 6), dim), (blocks,), jnp.float32, smallest / len(pieces), top_value / len(pieces))
        level = level * jnp.repeat(jnp.exp(steps), shape[dim] // blocks).reshape((-1,) + (1,) * (len(shape) - 1 - dim))
    return level


def deal_out(stream_key, own, number, rows, count, top, bound, lean):
    order = jax.random.permutation(stream_key, count)
    packed, ordinary = shares(count, rows * top, bound, lean, True), shares(count, rows * top, bound, lean, False)
    places = jnp.arange(count)

    def named(sizes, turn):
        used = int((sizes > 0).sum())
        fixed = max(1, used // 4)
        shifted = fixed + (places - fixed + turn * (used - fixed)) % max(1, count - fixed)
        return jnp.zeros((count,), jnp.int32).at[order[jnp.where(places < fixed, places, shifted)]].set(jnp.asarray(sizes, jnp.int32))

    sizes = jnp.where(number % 4 == 0, named(packed, number // 4), named(ordinary, number - number // 4 - 1))
    mixed = jax.random.permutation(jax.random.fold_in(own, 3), count)
    giver, taker = mixed[0:count // 2 * 2:2], mixed[1:count // 2 * 2:2]
    room = jnp.minimum(sizes[giver] - 1, bound - sizes[taker]) // 2
    room = jnp.where((giver == order[0]) | (taker == order[0]) | (sizes[taker] == 0), 0, jnp.maximum(room, 0))
    shifted = jax.random.randint(jax.random.fold_in(own, 4), (count // 2,), 0, 1 << 20) % (room + 1)
    sizes = sizes.at[giver].add(-shifted).at[taker].add(shifted)
    items = jnp.searchsorted(jnp.cumsum(sizes), jnp.arange(rows * top), side="right").astype(jnp.int32)
    listing = items.reshape(top, rows).T
    listing = listing[jax.random.permutation(jax.random.fold_in(own, 1), rows)]
    turn = jax.random.randint(jax.random.fold_in(own, 2), (rows, 1), 0, top)
    return jnp.take_along_axis(listing, (jnp.arange(top)[None, :] + turn) % top, axis=1)


def shares(amount, total, reach, skew, full):
    portions = [(1 << 20) // math.isqrt(grade ** skew) + 1 for grade in range(1, amount + 1)]
    largest = reach if full else min(reach, max(-(-total // amount), total * portions[0] // sum(portions)))
    least = 1 if total - largest >= amount - 1 else 0
    holding, rest = [largest] + [least] * (amount - 1), total - largest - least * (amount - 1)
    while rest > 0:
        movable = [i for i in range(1, amount) if holding[i] < largest] or [i for i in range(1, amount) if holding[i] < reach]
        whole, left = sum([portions[i] for i in movable]), rest
        for i in movable:
            extra = min(reach - holding[i], max(1, left * portions[i] // whole), rest)
            holding[i] = holding[i] + extra
            rest = rest - extra
    return np.array(holding)


def gaussian(own_key, shape, deviation, bound, shards=(), kind=jnp.bfloat16):
    values = jax.random.normal(own_key, shape, jnp.float32) * deviation
    if len(shards) > 0:
        values = levels(own_key, shape, shards, -0.22, 0.18) * values
    return jnp.clip(values, min=-bound, max=bound).astype(kind)


def noise_with(stream_key, shape, deviation, most, cuts, heavy, held_as=jnp.bfloat16):
    drawn = deviation * jax.random.normal(stream_key, shape, jnp.float32)
    if cuts:
        drawn = drawn * levels(stream_key, shape, cuts, -0.22, 0.18)
    return jnp.clip(spiked(drawn, jax.random.fold_in(stream_key, 3), *heavy), -most, most).astype(held_as)


def setup_inputs(seed: int = 0) -> dict:
    key_of = jax.random.split(jax.random.key(seed), 16)
    long_x = gaussian(key_of[0], (NLONG, LONG, D), 1.0, 6.0, ((0, 32),), jnp.float32)
    short_x = gaussian(key_of[1], (NSHORT, SHORT, D), 1.0, 6.0, ((0, 32),), jnp.float32)
    long_len = plant(jax.random.randint(key_of[2], (NLONG,), LONG // 4, LONG + 1), jax.random.fold_in(key_of[2], 1), LONG // 4, LONG).astype(jnp.int32)
    short_len = plant(jax.random.randint(key_of[3], (NSHORT,), SHORT // 4, SHORT + 1), jax.random.fold_in(key_of[3], 1), SHORT // 4, SHORT).astype(jnp.int32)
    expert_ids_keys = jax.random.split(jax.random.fold_in(key_of[4], 1), TOKENS // TOK_DEV)
    expert_ids_turns = jax.random.permutation(jax.random.fold_in(key_of[4], 3), TOKENS // TOK_DEV)
    expert_ids = jax.vmap(lambda own, number: deal_out(jax.random.fold_in(key_of[4], 2), own, number, TOK_DEV, EXPERTS, 1, CAP, 1))(expert_ids_keys, expert_ids_turns).reshape((TOKENS, 1))
    ln1_gain = jnp.clip(1.0 + 0.1 * jax.random.normal(key_of[5], (D,), jnp.float32), 0.5, 1.5).astype(jnp.bfloat16)
    ln1_bias = gaussian(key_of[6], (D,), 0.3, 1.5, ((0, 32),))
    w_qkv = gaussian(key_of[7], (D, 3 * D), D ** -0.5, 0.21875, ((0, 32),))
    w_proj = gaussian(key_of[8], (D, D), (D // 64) ** -0.5, 1.75, ((1, 32),))
    ln2_gain = jnp.clip(1.0 + 0.1 * jax.random.normal(key_of[9], (D,), jnp.float32), 0.5, 1.5).astype(jnp.bfloat16)
    ln2_bias = gaussian(key_of[10], (D,), 0.3, 1.5, ((0, 32),))
    w_up = gaussian(key_of[11], (EXPERTS, D, FF), D ** -0.5, 0.21875, ((0, 8), (2, 4)))
    w_down = gaussian(key_of[12], (EXPERTS, FF, D), FF ** -0.5, 0.109375, ((0, 8), (1, 4)))
    long_cot = noise_with(key_of[13], (NLONG, LONG, D), 1.0, 6.0, ((0, 32),), (0, 2, 32, 2.75), jnp.float32)
    short_cot = noise_with(key_of[14], (NSHORT, SHORT, D), 1.0, 6.0, ((0, 32),), (0, 2, 32, 2.75), jnp.float32)
    return {"long_x": long_x, "short_x": short_x, "long_len": long_len, "short_len": short_len, "expert_ids": expert_ids, "ln1_gain": ln1_gain, "ln1_bias": ln1_bias, "w_qkv": w_qkv, "w_proj": w_proj, "ln2_gain": ln2_gain, "ln2_bias": ln2_bias, "w_up": w_up, "w_down": w_down, "long_cot": long_cot, "short_cot": short_cot}


EPSILON = 1e-05
MASKED = -1e+30
HIGHEST = lax.Precision.HIGHEST

@jax.custom_vjp
def low(v):
    return lax.optimization_barrier(v.astype(jnp.bfloat16)).astype(jnp.float32)

@jax.custom_vjp
def low_back(v):
    return v

def low_keep(v):
    return (low(v), None)

def low_pass(kept, grad):
    return (grad,)

def back_keep(v):
    return (v, None)

def back_low(kept, grad):
    return (low(grad),)
low.defvjp(low_keep, low_pass)
low_back.defvjp(back_keep, back_low)

def product(left, right):
    return jnp.dot(left, right, precision=HIGHEST, preferred_element_type=jnp.float32)

def layer_norm(inputs, norm_gain, norm_bias):
    average = lax.optimization_barrier(jnp.mean(inputs, -1, keepdims=True))
    centred = inputs - average
    variance = lax.optimization_barrier(jnp.mean(centred * centred, -1, keepdims=True))
    return centred * lax.rsqrt(variance + EPSILON) * norm_gain + norm_bias

def attend(query_key_value, length):
    row_count = query_key_value.shape[0]
    split_parts = query_key_value.reshape(row_count, 3, HEADS, HEAD_DIM)
    queries, keys_all, values = (split_parts[:, 0], split_parts[:, 1], split_parts[:, 2])
    scores = jnp.einsum('qhc,khc->hqk', queries, keys_all, precision=HIGHEST, preferred_element_type=jnp.float32)
    scores = low_back(scores * HEAD_DIM ** (-0.5))
    position = jnp.arange(row_count, dtype=jnp.int32)
    allowed = (position[None, :] <= position[:, None]) & (position[None, :] < length)
    scores = jnp.where(allowed[None], scores, MASKED)
    highest = lax.optimization_barrier(jnp.max(scores, -1, keepdims=True))
    exponent = jnp.exp(scores - highest)
    probability = low(exponent / lax.optimization_barrier(jnp.sum(exponent, -1, keepdims=True)))
    expert_mixture = jnp.einsum('hqk,khc->qhc', probability, values, precision=HIGHEST, preferred_element_type=jnp.float32)
    return expert_mixture.reshape(row_count, HEADS * HEAD_DIM)

def mix_tokens(inputs, length, dense_set):
    first_gain, first_bias, query_key_value_weight, output_projection_weight, second_gain, second_bias = dense_set
    block_input_rows = low(layer_norm(inputs, first_gain, first_bias))
    query_key_value = low(low_back(product(block_input_rows, query_key_value_weight)))
    expert_mixture = low(low_back(attend(query_key_value, length)))
    hidden = inputs + low_back(product(expert_mixture, output_projection_weight))
    return (hidden, low(low_back(layer_norm(hidden, second_gain, second_bias))))

def reference(long_x, short_x, long_len, short_len, expert_ids, ln1_gain, ln1_bias, w_qkv, w_proj, ln2_gain, ln2_bias, w_up, w_down, long_cot, short_cot):
    blocks = N_DP * N_FSDP
    chosen_all = expert_ids[:, 0].reshape(blocks, -1)
    long_lens = long_len.reshape(blocks, -1)
    short_lens = short_len.reshape(blocks, -1)

    def forward(long_in, short_in, first_gain, first_bias, query_key_value_weight, output_projection_weight, second_gain, second_bias, up_weight, down_weight):
        dense_set = (first_gain, first_bias, query_key_value_weight, output_projection_weight, second_gain, second_bias)

        def device_block(inputs):
            long_rows, short_rows, long_length, short_length, chosen = inputs

            def one_sequence(seq_rows, seq_length):
                return mix_tokens(seq_rows, seq_length, dense_set)
            long_hidden, long_normed = jax.vmap(one_sequence)(long_rows, long_length)
            short_hidden, short_normed = jax.vmap(one_sequence)(short_rows, short_length)
            hidden = jnp.concatenate([long_hidden.reshape(-1, D), short_hidden.reshape(-1, D)], 0)
            normed = jnp.concatenate([long_normed.reshape(-1, D), short_normed.reshape(-1, D)], 0)
            onehot = (chosen[:, None] == jnp.arange(EXPERTS, dtype=jnp.int32)[None, :]).astype(jnp.int32)
            slot_rank = lax.optimization_barrier(jnp.sum(jnp.cumsum(onehot, 0) * onehot, 1)) - 1
            buffer = jnp.zeros((EXPERTS, CAP, D), jnp.float32).at[chosen, slot_rank].set(normed)
            pre_act = low_back(jnp.einsum('ecd,edf->ecf', buffer, up_weight, precision=HIGHEST, preferred_element_type=jnp.float32))
            activated = low(jax.nn.gelu(pre_act))
            result = low(low_back(jnp.einsum('ecf,efd->ecd', activated, down_weight, precision=HIGHEST, preferred_element_type=jnp.float32)))
            output = hidden + result[chosen, slot_rank]
            long_count = long_rows.shape[0] * long_rows.shape[1]
            return (output[:long_count].reshape(long_rows.shape), output[long_count:].reshape(short_rows.shape))
        outputs = lax.map(jax.checkpoint(device_block), (long_in.reshape(blocks, -1, LONG, D), short_in.reshape(blocks, -1, SHORT, D), long_lens, short_lens, chosen_all))
        return (outputs[0].reshape(long_in.shape), outputs[1].reshape(short_in.shape))
    weights = tuple((item.astype(jnp.float32) for item in (ln1_gain, ln1_bias, w_qkv, w_proj, ln2_gain, ln2_bias, w_up, w_down)))
    outputs, pullback = jax.vjp(forward, long_x, short_x, *weights)
    grads = pullback((long_cot, short_cot))
    return (outputs[0], outputs[1], grads[0], grads[1], grads[2], grads[3], grads[4], grads[5], grads[6], grads[7], grads[8], grads[9])
```

```python
import functools

import jax
import jax.numpy as jnp
from jax import lax
from jax.experimental import pallas as pl
from jax.experimental.pallas import tpu as pltpu
from jax.sharding import PartitionSpec as P

MESH = pl.DeviceIdType.MESH
HEAD_DIM = 64
EPSILON = 1e-05
MASKED = -1e30
BF16 = jnp.bfloat16
F32 = jnp.float32
LANES = 128
ROWS = 512
BLOCK = 256
VMEM_LIMIT = 60 * 2**20

NN = (((1,), (0,)), ((), ()))
NT = (((1,), (1,)), ((), ()))
TN = (((0,), (0,)), ((), ()))


def dot(a, b, dims=NN, precision=None):
    return lax.dot_general(a, b, dims, preferred_element_type=F32, precision=precision)


def params(**extra):
    return pltpu.CompilerParams(vmem_limit_bytes=VMEM_LIMIT, **extra)


def cost(flops, moved, exps=0):
    return pl.CostEstimate(flops=int(flops), bytes_accessed=int(moved), transcendentals=int(exps))


def constant(shape):
    return pl.BlockSpec(shape, lambda *_: (0,) * len(shape), pipeline_mode=pl.Buffered(1))


def norm_parts(inputs):
    average = jnp.mean(inputs, -1, keepdims=True)
    centred = inputs - average
    inv_scale = lax.rsqrt(jnp.mean(centred * centred, -1, keepdims=True) + EPSILON)
    return centred * inv_scale, inv_scale


def norm_back(grad_normed, normed, inv_scale):
    centre_term = jnp.mean(grad_normed, -1, keepdims=True)
    slope_term = jnp.mean(grad_normed * normed, -1, keepdims=True)
    return inv_scale * (grad_normed - centre_term - normed * slope_term)


def vectors(vec_ref):
    return jnp.transpose(vec_ref[...].astype(F32))[:8]


def long_short(width, n_long):
    return [
        pl.BlockSpec((ROWS, width), lambda i: (jnp.minimum(i, n_long - 1), 0)),
        pl.BlockSpec((ROWS, width), lambda i: (jnp.maximum(i - n_long, 0), 0)),
    ]


def gather_kernel(n_dp, n_f, own_ref, out_ref, z_send, z_recv, p_send, p_recv, c_send, c_recv, l_sem):
    z = lax.axis_index("dp")
    f = lax.axis_index("fsdp")
    half = n_f // 2
    partner = f + 1 - 2 * lax.rem(f, 2)
    barrier = pltpu.get_barrier_semaphore()
    for k in range(1, n_dp):
        pl.semaphore_signal(barrier, 1, device_id=(lax.rem(z + k, n_dp), f), device_id_type=MESH)
    for k in range(1, half):
        pl.semaphore_signal(barrier, 1, device_id=(z, lax.rem(f + 2 * k, n_f)), device_id_type=MESH)
    pl.semaphore_signal(barrier, 1, device_id=(z, partner), device_id_type=MESH)
    local = pltpu.make_async_copy(own_ref, out_ref.at[z, f], l_sem)
    local.start()
    pl.semaphore_wait(barrier, n_dp - 1 + half)

    z_copies = []
    for k in range(1, n_dp):
        copy = pltpu.make_async_remote_copy(
            own_ref, out_ref.at[z, f], z_send.at[k], z_recv.at[k],
            device_id=(lax.rem(z + k, n_dp), f), device_id_type=MESH,
        )
        copy.start()
        z_copies.append(copy)
    local.wait()
    for copy in z_copies:
        copy.wait_recv()
    p_copies = []
    for k in range(1, half):
        copy = pltpu.make_async_remote_copy(
            out_ref.at[:, f], out_ref.at[:, f], p_send.at[k], p_recv.at[k],
            device_id=(z, lax.rem(f + 2 * k, n_f)), device_id_type=MESH,
        )
        copy.start()
        p_copies.append(copy)
    c_copies = []
    for k in range(half):
        if k:
            p_copies[k - 1].wait_recv()
        column = lax.rem(f + n_f - 2 * k, n_f)
        copy = pltpu.make_async_remote_copy(
            out_ref.at[:, column], out_ref.at[:, column], c_send.at[k], c_recv.at[k],
            device_id=(z, partner), device_id_type=MESH,
        )
        copy.start()
        c_copies.append(copy)
    for copy in c_copies:
        copy.wait_recv()
    for copy in z_copies + p_copies + c_copies:
        copy.wait_send()


def gather_dense(own, n_dp, n_f):
    return pl.pallas_call(
        functools.partial(gather_kernel, n_dp, n_f),
        out_shape=jax.ShapeDtypeStruct((n_dp, n_f) + own.shape, own.dtype),
        in_specs=[pl.BlockSpec(memory_space=pl.ANY)],
        out_specs=pl.BlockSpec(memory_space=pl.ANY),
        scratch_shapes=[
            pltpu.SemaphoreType.DMA((n_dp,)),
            pltpu.SemaphoreType.DMA((n_dp,)),
            pltpu.SemaphoreType.DMA((n_f // 2,)),
            pltpu.SemaphoreType.DMA((n_f // 2,)),
            pltpu.SemaphoreType.DMA((n_f // 2,)),
            pltpu.SemaphoreType.DMA((n_f // 2,)),
            pltpu.SemaphoreType.DMA,
        ],
        compiler_params=pltpu.CompilerParams(collective_id=0, has_side_effects=True),
        cost_estimate=cost(0, 100e6),
        name="gather_dense",
    )(own)


def scatter_kernel(
    n_dp, n_f, in_ref, out_ref, got1, sum1, got2, sum2, got3,
    c_send, c_recv, p_send, p_recv, z_send, z_recv,
):
    z = lax.axis_index("dp")
    f = lax.axis_index("fsdp")
    half = n_f // 2
    parity = lax.rem(f, 2)
    mine = f // 2
    partner = f + 1 - 2 * parity
    barrier = pltpu.get_barrier_semaphore()
    for k in range(1, n_dp):
        pl.semaphore_signal(barrier, 1, device_id=(lax.rem(z + k, n_dp), f), device_id_type=MESH)
    for k in range(1, half):
        pl.semaphore_signal(barrier, 1, device_id=(z, lax.rem(f + 2 * k, n_f)), device_id_type=MESH)
    pl.semaphore_signal(barrier, 1, device_id=(z, partner), device_id_type=MESH)
    pl.semaphore_wait(barrier, n_dp - 1 + half)

    c_copies = []
    order = list(range(1, half)) + [0]
    for k in order:
        slot = lax.rem(mine + k, half)
        copy = pltpu.make_async_remote_copy(
            in_ref.at[:, 2 * slot + 1 - parity], got1.at[slot], c_send.at[k], c_recv.at[k],
            device_id=(z, partner), device_id_type=MESH,
        )
        copy.start()
        c_copies.append(copy)
    p_copies = []
    for k, c_copy in zip(order, c_copies):
        c_copy.wait_recv()
        slot = lax.rem(mine + k, half)
        sum1[slot] = (in_ref[:, 2 * slot + parity].astype(F32) + got1[slot].astype(F32)).astype(BF16)
        if k:
            copy = pltpu.make_async_remote_copy(
                sum1.at[slot], got2.at[k], p_send.at[k], p_recv.at[k],
                device_id=(z, lax.rem(f + 2 * k, n_f)), device_id_type=MESH,
            )
            copy.start()
            p_copies.append(copy)
    for copy in p_copies:
        copy.wait_recv()
    total = sum1[mine].astype(F32)
    for k in range(1, half):
        total = total + got2[k].astype(F32)
    sum2[...] = total.astype(BF16)
    z_copies = []
    for k in range(1, n_dp):
        there = lax.rem(z + k, n_dp)
        copy = pltpu.make_async_remote_copy(
            sum2.at[there], got3.at[k], z_send.at[k], z_recv.at[k],
            device_id=(there, f), device_id_type=MESH,
        )
        copy.start()
        z_copies.append(copy)
    for copy in z_copies:
        copy.wait_recv()
    total = sum2[z].astype(F32)
    for k in range(1, n_dp):
        total = total + got3[k].astype(F32)
    out_ref[...] = total
    for copy in c_copies + p_copies + z_copies:
        copy.wait_send()


def scatter_dense(grads, n_dp, n_f):
    block = grads.shape[2:]
    half = n_f // 2
    return pl.pallas_call(
        functools.partial(scatter_kernel, n_dp, n_f),
        out_shape=jax.ShapeDtypeStruct(block, F32),
        in_specs=[pl.BlockSpec(memory_space=pltpu.VMEM)],
        out_specs=pl.BlockSpec(memory_space=pltpu.VMEM),
        scratch_shapes=[
            pltpu.VMEM((half, n_dp) + block, BF16),
            pltpu.VMEM((half, n_dp) + block, BF16),
            pltpu.VMEM((half, n_dp) + block, BF16),
            pltpu.VMEM((n_dp,) + block, BF16),
            pltpu.VMEM((n_dp,) + block, BF16),
            pltpu.SemaphoreType.DMA((half,)),
            pltpu.SemaphoreType.DMA((half,)),
            pltpu.SemaphoreType.DMA((half,)),
            pltpu.SemaphoreType.DMA((half,)),
            pltpu.SemaphoreType.DMA((n_dp,)),
            pltpu.SemaphoreType.DMA((n_dp,)),
        ],
        compiler_params=params(collective_id=1, has_side_effects=True),
        cost_estimate=cost(0, 100e6),
        name="scatter_dense",
    )(grads)


def dispatch_block(slot_row_ref, rows, block):
    first = block * BLOCK
    slot_id = first + lax.broadcasted_iota(jnp.int32, (BLOCK, 1), 0)
    chosen = (slot_row_ref[0:1, :] == slot_id).astype(F32).astype(BF16)
    return dot(chosen, rows).astype(BF16)


def cot_kernel(n_long, n_rows, cap, ids_ref, long_ref, short_ref, col_ref, row_ref, slots_ref, rows_ref):
    i = pl.program_id(0)

    @pl.when(i == 0)
    def _():
        count = ids_ref.shape[0]
        lane = lax.broadcasted_iota(jnp.int32, (1, LANES), 1)
        onehot = (ids_ref[...] == lane).astype(F32)
        onehot_low = onehot.astype(BF16)
        col = lax.broadcasted_iota(jnp.int32, (1, count), 1)
        base = (lane * cap).astype(F32)
        ones = jnp.ones((8, LANES), F32)
        for start in range(0, count, ROWS):
            row = start + lax.broadcasted_iota(jnp.int32, (ROWS, 1), 0)
            before = dot((col < row).astype(F32).astype(BF16), onehot_low)
            picked = (before + base) * onehot[start : start + ROWS]
            col_ref[start : start + ROWS, :] = jnp.sum(picked, 1, keepdims=True).astype(jnp.int32)
            row_ref[:, start : start + ROWS] = dot(
                ones, picked, NT, precision=lax.Precision.HIGHEST
            ).astype(jnp.int32)

    @pl.when(i < n_long)
    def _():
        rows_ref[pl.ds(pl.multiple_of(i * ROWS, ROWS), ROWS), :] = long_ref[...].astype(BF16)

    @pl.when((i >= n_long) & (i < n_rows))
    def _():
        rows_ref[pl.ds(pl.multiple_of(i * ROWS, ROWS), ROWS), :] = short_ref[...].astype(BF16)

    @pl.when(i >= n_rows)
    def _():
        slots_ref[...] = dispatch_block(row_ref, rows_ref[...], i - n_rows)


def route_cot(ids, long_cot, short_cot, slots, cap):
    width = long_cot.shape[1]
    n_long, n_short = long_cot.shape[0] // ROWS, short_cot.shape[0] // ROWS
    n_rows = n_long + n_short
    count = ids.shape[0]
    return pl.pallas_call(
        functools.partial(cot_kernel, n_long, n_rows, cap),
        grid=(n_rows + slots // BLOCK,),
        in_specs=[
            constant((count, 1)),
            pl.BlockSpec((ROWS, width), lambda i: (jnp.minimum(i, n_long - 1), 0)),
            pl.BlockSpec((ROWS, width), lambda i: (jnp.clip(i - n_long, 0, n_short - 1), 0)),
        ],
        out_specs=[
            pl.BlockSpec((count, 1), lambda i: (0, 0)),
            pl.BlockSpec((8, count), lambda i: (0, 0)),
            pl.BlockSpec((BLOCK, width), lambda i: (jnp.maximum(i - n_rows, 0), 0)),
        ],
        out_shape=[
            jax.ShapeDtypeStruct((count, 1), jnp.int32),
            jax.ShapeDtypeStruct((8, count), jnp.int32),
            jax.ShapeDtypeStruct((slots, width), BF16),
        ],
        scratch_shapes=[pltpu.VMEM((count, width), BF16)],
        compiler_params=params(),
        cost_estimate=cost(2 * slots * count * width, 4 * count * width + 2 * slots * width),
        name="route_cot",
    )(ids, long_cot, short_cot)


def qkv_kernel(n_long, width, long_ref, short_ref, w_ref, vec_ref, qkv_ref, vec_scr):
    i = pl.program_id(0)

    @pl.when(i == 0)
    def _():
        vec_scr[...] = vectors(vec_ref)

    def body(x_ref):
        normed, _ = norm_parts(x_ref[...])
        rows = (normed * vec_scr[0:1, :] + vec_scr[1:2, :]).astype(BF16)
        for part in range(3):
            cut = slice(part * width, (part + 1) * width)
            out = dot(rows, w_ref[:, cut])
            if part == 0:
                out = out * HEAD_DIM ** (-0.5)
            qkv_ref[:, cut] = out.astype(BF16)

    pl.when(i < n_long)(lambda: body(long_ref))
    pl.when(i >= n_long)(lambda: body(short_ref))


def make_qkv(long_x, short_x, dense):
    width = long_x.shape[1]
    n_long, n_short = long_x.shape[0] // ROWS, short_x.shape[0] // ROWS
    count = long_x.shape[0] + short_x.shape[0]
    return pl.pallas_call(
        functools.partial(qkv_kernel, n_long, width),
        grid=(n_long + n_short,),
        in_specs=long_short(width, n_long)
        + [
            constant((width, 3 * width)),
            pl.BlockSpec((width, LANES), lambda i: (0, 4 * width // LANES)),
        ],
        out_specs=pl.BlockSpec((ROWS, 3 * width), lambda i: (i, 0)),
        out_shape=jax.ShapeDtypeStruct((count, 3 * width), BF16),
        scratch_shapes=[pltpu.VMEM((8, width), F32)],
        compiler_params=params(),
        cost_estimate=cost(6 * count * width * width, count * width * 10 + 6 * width * width),
        name="make_qkv",
    )(long_x, short_x, dense, dense)


def sequences(long_shape, short_shape):
    found = []
    start = 0
    for which, (number, length) in enumerate((long_shape, short_shape)):
        for index in range(number):
            found.append((start, length, which, index))
            start += length
    return found


def head_masks():
    lane = lax.broadcasted_iota(jnp.int32, (1, LANES), 1)
    return (lane < HEAD_DIM, lane >= HEAD_DIM)


def attend_kernel(seqs, long_len, short_len, q_ref, k_ref, v_ref, o_ref, lse_ref):
    pair = pl.program_id(0)
    masks = head_masks()
    lane = lax.broadcasted_iota(jnp.int32, (1, LANES), 1)

    @pl.when(pair == 0)
    def _():
        lse_ref[...] = jnp.zeros_like(lse_ref)

    causal = lax.broadcasted_iota(jnp.int32, (BLOCK, BLOCK), 1) <= lax.broadcasted_iota(
        jnp.int32, (BLOCK, BLOCK), 0
    )
    for start, length, which, index in seqs:
        valid = (short_len if which else long_len)[index]
        key_pos = lax.broadcasted_iota(jnp.int32, (1, length), 1)
        bias = jnp.where(key_pos < valid, 0.0, MASKED)
        for first in range(0, length, BLOCK):
            here = slice(start + first, start + first + BLOCK)
            past = slice(start, start + first)
            q = q_ref[here, :]
            outs = []
            stats = jnp.zeros((BLOCK, LANES), F32)
            for head in range(2):
                qh = jnp.where(masks[head], q, jnp.zeros_like(q))
                near = dot(qh, k_ref[here, :], NT) + bias[:, first : first + BLOCK]
                near = jnp.where(causal, near, MASKED)
                top = jnp.max(near, 1, keepdims=True)
                if first:
                    far = dot(qh, k_ref[past, :], NT) + bias[:, :first]
                    top = jnp.maximum(top, jnp.max(far, 1, keepdims=True))
                near = jnp.exp(near - top)
                total = jnp.sum(near, 1, keepdims=True)
                out = dot(near.astype(BF16), v_ref[here, :])
                if first:
                    far = jnp.exp(far - top)
                    total = total + jnp.sum(far, 1, keepdims=True)
                    out = out + dot(far.astype(BF16), v_ref[past, :])
                outs.append(out * (1.0 / total))
                stats = jnp.where(lane == 2 * pair + head, top + jnp.log(total), stats)
            o_ref[here, :] = jnp.where(masks[0], outs[0], outs[1]).astype(BF16)
            lse_ref[here, :] = lse_ref[here, :] + stats


def attend(qkv, long_len, short_len, seqs):
    count, width = qkv.shape[0], qkv.shape[1] // 3
    pairs = width // LANES
    return pl.pallas_call(
        functools.partial(attend_kernel, seqs),
        grid=(pairs,),
        in_specs=[pl.BlockSpec(memory_space=pltpu.SMEM)] * 2
        + [
            pl.BlockSpec((count, LANES), lambda i: (0, i)),
            pl.BlockSpec((count, LANES), lambda i: (0, i + pairs)),
            pl.BlockSpec((count, LANES), lambda i: (0, i + 2 * pairs)),
        ],
        out_specs=[
            pl.BlockSpec((count, LANES), lambda i: (0, i)),
            pl.BlockSpec((count, LANES), lambda i: (0, 0)),
        ],
        out_shape=[
            jax.ShapeDtypeStruct((count, width), BF16),
            jax.ShapeDtypeStruct((count, LANES), F32),
        ],
        compiler_params=params(),
        cost_estimate=cost(16e9, 8 * count * width, 10e6),
        name="attend",
    )(long_len, short_len, qkv, qkv, qkv)


def attend_back_kernel(
    seqs, long_len, short_len, q_ref, k_ref, v_ref, o_ref, do_ref, lse_ref,
    dq_ref, dk_ref, dv_ref, acc_ref, row_ref,
):
    pair = pl.program_id(0)
    masks = head_masks()
    lane = lax.broadcasted_iota(jnp.int32, (8, LANES), 1)
    which_row = lax.broadcasted_iota(jnp.int32, (8, LANES), 0)
    pick = (lane == 2 * pair + which_row).astype(F32) * (which_row < 2).astype(F32)
    split = (lane // HEAD_DIM == which_row).astype(F32)
    row_ref[0:8, :] = dot(pick, lse_ref[...], NT, precision=lax.Precision.HIGHEST)
    row_ref[8:16, :] = dot(
        split, do_ref[...].astype(F32) * o_ref[...].astype(F32), NT,
        precision=lax.Precision.HIGHEST,
    )
    acc_ref[...] = jnp.zeros_like(acc_ref)
    causal = lax.broadcasted_iota(jnp.int32, (BLOCK, BLOCK), 0) <= lax.broadcasted_iota(
        jnp.int32, (BLOCK, BLOCK), 1
    )
    for start, length, which, index in seqs:
        valid = (short_len if which else long_len)[index]
        for first in range(0, length, BLOCK):
            here = slice(start + first, start + first + BLOCK)
            k, v = k_ref[here, :], v_ref[here, :]
            key_pos = first + lax.broadcasted_iota(jnp.int32, (BLOCK, 1), 0)
            inside = key_pos < valid
            dk = jnp.zeros((BLOCK, LANES), F32)
            dv = jnp.zeros((BLOCK, LANES), F32)
            for head in range(2):
                kh = jnp.where(masks[head], k, jnp.zeros_like(k))
                for rows, allowed in (
                    (here, inside & causal),
                    (slice(here.stop, start + length), inside),
                ):
                    if rows.start == rows.stop:
                        continue
                    q, do = q_ref[rows, :], do_ref[rows, :]
                    qh = jnp.where(masks[head], q, jnp.zeros_like(q))
                    doh = jnp.where(masks[head], do, jnp.zeros_like(do))
                    scores = dot(k, qh, NT)
                    p = jnp.where(allowed, jnp.exp(scores - row_ref[head : head + 1, rows]), 0.0)
                    dp = dot(v, doh, NT)
                    ds = (p * (dp - row_ref[8 + head : 9 + head, rows])).astype(BF16)
                    dv = dv + dot(p.astype(BF16), doh)
                    dk = dk + dot(ds, qh)
                    acc_ref[rows, :] = acc_ref[rows, :] + dot(ds, kh, TN)
            dk_ref[here, :] = dk.astype(BF16)
            dv_ref[here, :] = dv.astype(BF16)
    dq_ref[...] = (acc_ref[...] * HEAD_DIM ** (-0.5)).astype(BF16)


def attend_back(qkv, o, d_o, lse, long_len, short_len, seqs):
    count, width = o.shape
    pairs = width // LANES
    one = pl.BlockSpec((count, LANES), lambda i: (0, i))
    return pl.pallas_call(
        functools.partial(attend_back_kernel, seqs),
        grid=(pairs,),
        in_specs=[pl.BlockSpec(memory_space=pltpu.SMEM)] * 2
        + [
            one,
            pl.BlockSpec((count, LANES), lambda i: (0, i + pairs)),
            pl.BlockSpec((count, LANES), lambda i: (0, i + 2 * pairs)),
            one,
            one,
            constant((count, LANES)),
        ],
        out_specs=[one, one, one],
        out_shape=[jax.ShapeDtypeStruct((count, width), BF16)] * 3,
        scratch_shapes=[pltpu.VMEM((count, LANES), F32), pltpu.VMEM((16, count), F32)],
        compiler_params=params(),
        cost_estimate=cost(40e9, 16 * count * width, 10e6),
        name="attend_back",
    )(long_len, short_len, qkv, qkv, qkv, o, d_o, lse)


def project_kernel(
    n_long, n_rows, long_ref, short_ref, o_ref, w_ref, vec_ref, row_ref,
    h_ref, slots_ref, rows_ref, vec_scr,
):
    i = pl.program_id(0)

    @pl.when(i == 0)
    def _():
        vec_scr[...] = vectors(vec_ref)

    def body(x_ref):
        hidden = x_ref[...] + dot(o_ref[...], w_ref[...], NT)
        h_ref[...] = hidden
        normed, _ = norm_parts(hidden)
        rows_ref[pl.ds(pl.multiple_of(i * ROWS, ROWS), ROWS), :] = (
            normed * vec_scr[2:3, :] + vec_scr[3:4, :]
        ).astype(BF16)

    pl.when(i < n_long)(lambda: body(long_ref))
    pl.when((i >= n_long) & (i < n_rows))(lambda: body(short_ref))

    @pl.when(i >= n_rows)
    def _():
        slots_ref[...] = dispatch_block(row_ref, rows_ref[...], i - n_rows)


def project(long_x, short_x, o, dense, slot_row, slots):
    width = long_x.shape[1]
    n_long, n_short = long_x.shape[0] // ROWS, short_x.shape[0] // ROWS
    n_rows = n_long + n_short
    count = o.shape[0]
    return pl.pallas_call(
        functools.partial(project_kernel, n_long, n_rows),
        grid=(n_rows + slots // BLOCK,),
        in_specs=[
            pl.BlockSpec((ROWS, width), lambda i: (jnp.minimum(i, n_long - 1), 0)),
            pl.BlockSpec((ROWS, width), lambda i: (jnp.clip(i - n_long, 0, n_short - 1), 0)),
            pl.BlockSpec((ROWS, width), lambda i: (jnp.minimum(i, n_rows - 1), 0)),
            pl.BlockSpec((width, width), lambda i: (0, 3)),
            pl.BlockSpec((width, LANES), lambda i: (0, 4 * width // LANES)),
            constant((8, count)),
        ],
        out_specs=[
            pl.BlockSpec((ROWS, width), lambda i: (jnp.minimum(i, n_rows - 1), 0)),
            pl.BlockSpec((BLOCK, width), lambda i: (jnp.maximum(i - n_rows, 0), 0)),
        ],
        out_shape=[
            jax.ShapeDtypeStruct((count, width), F32),
            jax.ShapeDtypeStruct((slots, width), BF16),
        ],
        scratch_shapes=[pltpu.VMEM((count, width), BF16), pltpu.VMEM((8, width), F32)],
        compiler_params=params(),
        cost_estimate=cost(2 * (slots + width) * count * width, 12 * count * width),
        name="project",
    )(long_x, short_x, o, dense, dense, slot_row)


def gelu_parts(pre):
    scale = 0.7978845608028654
    square = pre * pre
    flat = jnp.tanh(scale * pre * (1.0 + 0.044715 * square))
    half = 0.5 * (1.0 + flat)
    slope = half + (0.5 * scale) * pre * (1.0 - flat * flat) * (1.0 + 0.134145 * square)
    return half * pre, slope


def experts_kernel(n_r, b_ref, g_ref, up_ref, act_ref, slope_ref, gd_ref, all_ref):
    r = pl.program_id(1)
    pre = dot(b_ref[...], up_ref[...])
    act, slope = gelu_parts(pre)
    act = act.astype(BF16)
    act_ref[...] = act
    slope_ref[...] = slope.astype(BF16)
    all_ref[pl.ds(pl.multiple_of(r * ROWS, ROWS), ROWS), :] = act

    @pl.when(r == n_r - 1)
    def _():
        gd_ref[...] = dot(all_ref[...], g_ref[...], TN).astype(BF16)


def experts_up(b_slots, g_slots, up):
    rows, width = b_slots.shape
    hidden = up.shape[1]
    n_r, n_f = rows // ROWS, hidden // width
    tile = pl.BlockSpec((ROWS, width), lambda f, r: (r, f))
    return pl.pallas_call(
        functools.partial(experts_kernel, n_r),
        grid=(n_f, n_r),
        in_specs=[
            pl.BlockSpec((ROWS, width), lambda f, r: (r, 0)),
            constant((rows, width)),
            pl.BlockSpec((width, width), lambda f, r: (0, f)),
        ],
        out_specs=[tile, tile, pl.BlockSpec((width, width), lambda f, r: (f, 0))],
        out_shape=[
            jax.ShapeDtypeStruct((rows, hidden), BF16),
            jax.ShapeDtypeStruct((rows, hidden), BF16),
            jax.ShapeDtypeStruct((hidden, width), BF16),
        ],
        scratch_shapes=[pltpu.VMEM((rows, width), BF16)],
        compiler_params=params(),
        cost_estimate=cost(4 * rows * width * hidden, 6 * rows * hidden, rows * hidden),
        name="experts_up",
    )(b_slots, g_slots, up)


def experts_back_kernel(
    n_f, n_r, b_ref, g_ref, act_ref, slope_ref, up_ref, down_ref,
    y_ref, db_ref, gu_ref, y_acc, db_acc, all_ref,
):
    f, r = pl.program_id(0), pl.program_id(1)
    rows = pl.ds(pl.multiple_of(r * ROWS, ROWS), ROWS)
    d_act = dot(g_ref[rows, :], down_ref[...], NT)
    d_pre = (d_act * slope_ref[...].astype(F32)).astype(BF16)
    all_ref[rows, :] = d_pre
    y = dot(act_ref[...], down_ref[...])
    db = dot(d_pre, up_ref[...], NT)

    @pl.when(f == 0)
    def _():
        y_acc[rows, :] = y
        db_acc[rows, :] = db

    @pl.when((f > 0) & (f < n_f - 1))
    def _():
        y_acc[rows, :] = y_acc[rows, :] + y
        db_acc[rows, :] = db_acc[rows, :] + db

    @pl.when(f == n_f - 1)
    def _():
        y_ref[rows, :] = (y_acc[rows, :] + y).astype(BF16)
        db_ref[rows, :] = (db_acc[rows, :] + db).astype(BF16)

    @pl.when(r == n_r - 1)
    def _():
        gu_ref[...] = dot(b_ref[...], all_ref[...], TN).astype(BF16)


def experts_back(b_slots, g_slots, act, slope, up, down):
    rows, width = b_slots.shape
    hidden = up.shape[1]
    n_r, n_f = rows // ROWS, hidden // width
    tile = pl.BlockSpec((ROWS, width), lambda f, r: (r, f))
    whole = pl.BlockSpec((rows, width), lambda f, r: (0, 0))
    return pl.pallas_call(
        functools.partial(experts_back_kernel, n_f, n_r),
        grid=(n_f, n_r),
        in_specs=[
            constant((rows, width)),
            constant((rows, width)),
            tile,
            tile,
            pl.BlockSpec((width, width), lambda f, r: (0, f)),
            pl.BlockSpec((width, width), lambda f, r: (f, 0)),
        ],
        out_specs=[whole, whole, pl.BlockSpec((width, width), lambda f, r: (0, f))],
        out_shape=[
            jax.ShapeDtypeStruct((rows, width), BF16),
            jax.ShapeDtypeStruct((rows, width), BF16),
            jax.ShapeDtypeStruct((width, hidden), BF16),
        ],
        scratch_shapes=[
            pltpu.VMEM((rows, width), F32),
            pltpu.VMEM((rows, width), F32),
            pltpu.VMEM((rows, width), BF16),
        ],
        compiler_params=params(),
        cost_estimate=cost(8 * rows * width * hidden, 8 * rows * hidden),
        name="experts_back",
    )(b_slots, g_slots, act, slope, up, down)


def combine_rows(col_ref, slots_ref):
    slot_id = lax.broadcasted_iota(jnp.int32, (1, slots_ref.shape[0]), 1)
    chosen = (col_ref[...] == slot_id).astype(F32).astype(BF16)
    return dot(chosen, slots_ref[...])


def finish_kernel(n_long, h_ref, col_ref, y_ref, long_ref, short_ref):
    i = pl.program_id(0)
    out = h_ref[...] + combine_rows(col_ref, y_ref)

    @pl.when(i < n_long)
    def _():
        long_ref[...] = out

    @pl.when(i >= n_long)
    def _():
        short_ref[...] = out


def finish(h, slot_col, y_back, n_long, n_short):
    count, width = h.shape
    slots = y_back.shape[0]
    return pl.pallas_call(
        functools.partial(finish_kernel, n_long),
        grid=(n_long + n_short,),
        in_specs=[
            pl.BlockSpec((ROWS, width), lambda i: (i, 0)),
            pl.BlockSpec((ROWS, 1), lambda i: (i, 0)),
            constant((slots, width)),
        ],
        out_specs=long_short(width, n_long),
        out_shape=[
            jax.ShapeDtypeStruct((n_long * ROWS, width), F32),
            jax.ShapeDtypeStruct((n_short * ROWS, width), F32),
        ],
        compiler_params=params(),
        cost_estimate=cost(2 * slots * count * width, 8 * count * width + 2 * slots * width),
        name="finish",
    )(h, slot_col, y_back)


def hidden_back_kernel(
    n_long, n_rows, h_ref, col_ref, db_ref, long_ref, short_ref, o_ref, w_ref, vec_ref,
    dh_ref, do_ref, gp_ref, gv_ref, acc_ref, vec_scr,
):
    i = pl.program_id(0)

    @pl.when(i == 0)
    def _():
        vec_scr[...] = vectors(vec_ref)
        acc_ref[...] = jnp.zeros_like(acc_ref)
        gv_ref[...] = jnp.zeros_like(gv_ref)

    def body(cot_ref):
        d_b = combine_rows(col_ref, db_ref)
        normed, inv_scale = norm_parts(h_ref[...])
        gv_ref[0:1, :] = gv_ref[0:1, :] + jnp.sum(d_b * normed, 0, keepdims=True)
        gv_ref[1:2, :] = gv_ref[1:2, :] + jnp.sum(d_b, 0, keepdims=True)
        d_h = cot_ref[...] + norm_back(d_b * vec_scr[2:3, :], normed, inv_scale)
        dh_ref[...] = d_h
        d_attn = d_h.astype(BF16)
        do_ref[...] = dot(d_attn, w_ref[...]).astype(BF16)
        acc_ref[...] = acc_ref[...] + dot(d_attn, o_ref[...], TN)

    pl.when(i < n_long)(lambda: body(long_ref))
    pl.when(i >= n_long)(lambda: body(short_ref))

    @pl.when(i == n_rows - 1)
    def _():
        gp_ref[...] = acc_ref[...].astype(BF16)


def hidden_back(h, slot_col, db_back, long_cot, short_cot, o, dense):
    count, width = h.shape
    slots = db_back.shape[0]
    n_long, n_short = long_cot.shape[0] // ROWS, short_cot.shape[0] // ROWS
    n_rows = n_long + n_short
    row = pl.BlockSpec((ROWS, width), lambda i: (i, 0))
    return pl.pallas_call(
        functools.partial(hidden_back_kernel, n_long, n_rows),
        grid=(n_rows,),
        in_specs=[row, pl.BlockSpec((ROWS, 1), lambda i: (i, 0)), constant((slots, width))]
        + long_short(width, n_long)
        + [
            row,
            pl.BlockSpec((width, width), lambda i: (0, 3)),
            pl.BlockSpec((width, LANES), lambda i: (0, 4 * width // LANES)),
        ],
        out_specs=[
            row,
            row,
            pl.BlockSpec((width, width), lambda i: (0, 0)),
            pl.BlockSpec((8, width), lambda i: (0, 0)),
        ],
        out_shape=[
            jax.ShapeDtypeStruct((count, width), F32),
            jax.ShapeDtypeStruct((count, width), BF16),
            jax.ShapeDtypeStruct((width, width), BF16),
            jax.ShapeDtypeStruct((8, width), F32),
        ],
        scratch_shapes=[pltpu.VMEM((width, width), F32), pltpu.VMEM((8, width), F32)],
        compiler_params=params(),
        cost_estimate=cost(2 * (slots + 2 * width) * count * width, 16 * count * width),
        name="hidden_back",
    )(h, slot_col, db_back, long_cot, short_cot, o, dense, dense)


def input_back_kernel(
    n_long, n_rows, width, long_ref, short_ref, dh_ref, dq_ref, dk_ref, dv_ref, w_ref, vec_ref,
    gp_ref, gv_ref, lg_ref, sg_ref, out_ref, acc_ref, vec_scr, gv_scr,
):
    i = pl.program_id(0)

    @pl.when(i == 0)
    def _():
        vec_scr[...] = vectors(vec_ref)
        acc_ref[...] = jnp.zeros_like(acc_ref)
        gv_scr[...] = jnp.zeros_like(gv_scr)
        gv_scr[2:4, :] = gv_ref[0:2, :]

    def body(x_ref, grad_ref):
        normed, inv_scale = norm_parts(x_ref[...])
        rows = (normed * vec_scr[0:1, :] + vec_scr[1:2, :]).astype(BF16)
        entered = jnp.zeros_like(normed)
        for part, d_ref in enumerate((dq_ref, dk_ref, dv_ref)):
            cut = slice(part * width, (part + 1) * width)
            entered = entered + dot(d_ref[...], w_ref[:, cut], NT)
            acc_ref[:, cut] = acc_ref[:, cut] + dot(rows, d_ref[...], TN)
        gv_scr[0:1, :] = gv_scr[0:1, :] + jnp.sum(entered * normed, 0, keepdims=True)
        gv_scr[1:2, :] = gv_scr[1:2, :] + jnp.sum(entered, 0, keepdims=True)
        grad_ref[...] = dh_ref[...] + norm_back(entered * vec_scr[0:1, :], normed, inv_scale)

    pl.when(i < n_long)(lambda: body(long_ref, lg_ref))
    pl.when(i >= n_long)(lambda: body(short_ref, sg_ref))

    @pl.when(i == n_rows - 1)
    def _():
        out_ref[:, : 3 * width] = acc_ref[...].astype(BF16)
        out_ref[:, 3 * width : 4 * width] = gp_ref[...]
        out_ref[:, 4 * width :] = jnp.transpose(gv_scr[...]).astype(BF16)


def input_back(long_x, short_x, d_h, dq, dk, dv, dense, grad_proj, grad_vec):
    count, width = d_h.shape
    n_long, n_short = long_x.shape[0] // ROWS, short_x.shape[0] // ROWS
    n_rows = n_long + n_short
    row = pl.BlockSpec((ROWS, width), lambda i: (i, 0))
    return pl.pallas_call(
        functools.partial(input_back_kernel, n_long, n_rows, width),
        grid=(n_rows,),
        in_specs=long_short(width, n_long)
        + [
            row,
            row,
            row,
            row,
            constant((width, 3 * width)),
            pl.BlockSpec((width, LANES), lambda i: (0, 4 * width // LANES)),
            constant((width, width)),
            constant((8, width)),
        ],
        out_specs=long_short(width, n_long)
        + [pl.BlockSpec((width, 4 * width + LANES), lambda i: (0, 0))],
        out_shape=[
            jax.ShapeDtypeStruct(long_x.shape, F32),
            jax.ShapeDtypeStruct(short_x.shape, F32),
            jax.ShapeDtypeStruct((width, 4 * width + LANES), BF16),
        ],
        scratch_shapes=[
            pltpu.VMEM((width, 3 * width), F32),
            pltpu.VMEM((8, width), F32),
            pltpu.VMEM((LANES, width), F32),
        ],
        compiler_params=params(),
        cost_estimate=cost(12 * count * width * width, 20 * count * width),
        name="input_back",
    )(long_x, short_x, d_h, dq, dk, dv, dense, dense, grad_proj, grad_vec)


def on_device(
    n_dp, n_f, long_x, short_x, long_len, short_len, expert_ids, ln1_gain, ln1_bias,
    w_qkv, w_proj, ln2_gain, ln2_bias, w_up, w_down, long_cot, short_cot,
):
    width = long_x.shape[2]
    share = w_qkv.shape[0]
    seqs = sequences(long_x.shape[:2], short_x.shape[:2])
    flat = lambda a: a.reshape(-1, width)
    xl, xs, gl, gs = flat(long_x), flat(short_x), flat(long_cot), flat(short_cot)
    n_long, n_short = xl.shape[0] // ROWS, xs.shape[0] // ROWS
    experts = n_f * w_up.shape[0]
    cap = 4 * expert_ids.shape[0] // (3 * experts)
    slots = experts * cap

    up = lax.all_gather(w_up, "dp", axis=2, tiled=True)[0]
    down = lax.all_gather(w_down, "dp", axis=1, tiled=True)[0]

    vec = jnp.stack([ln1_gain, ln1_bias, ln2_gain, ln2_bias], 1)
    own = jnp.concatenate(
        [w_qkv, w_proj.T, jnp.pad(vec, ((0, 0), (0, LANES - vec.shape[1])))], 1
    )
    dense = gather_dense(own, n_dp, n_f).reshape(n_dp * n_f * share, own.shape[1])

    def exchange(rows):
        sent = lax.all_to_all(
            rows.reshape(n_f, slots // n_f, width), "fsdp", split_axis=0, concat_axis=0, tiled=True
        )
        return sent.reshape(slots, width)

    slot_col, slot_row, g_slots = route_cot(expert_ids, gl, gs, slots, cap)
    qkv = make_qkv(xl, xs, dense)
    g_there = exchange(g_slots)
    o, lse = attend(qkv, long_len, short_len, seqs)
    h, b_slots = project(xl, xs, o, dense, slot_row, slots)
    b_there = exchange(b_slots)
    act, slope, grad_down = experts_up(b_there, g_there, up)
    grad_down = lax.psum_scatter(grad_down, "dp", scatter_dimension=0, tiled=True).astype(F32)
    y, d_b, grad_up = experts_back(b_there, g_there, act, slope, up, down)
    grad_up = lax.psum_scatter(grad_up, "dp", scatter_dimension=1, tiled=True).astype(F32)
    db_back = exchange(d_b)
    y_back = exchange(y)
    d_h, d_o, grad_proj, grad_vec = hidden_back(h, slot_col, db_back, gl, gs, o, dense)
    long_out, short_out = finish(h, slot_col, y_back, n_long, n_short)
    dq, dk, dv = attend_back(qkv, o, d_o, lse, long_len, short_len, seqs)
    long_grad, short_grad, grads = input_back(xl, xs, d_h, dq, dk, dv, dense, grad_proj, grad_vec)
    owned = scatter_dense(grads.reshape(n_dp, n_f, share, own.shape[1]), n_dp, n_f)
    return (
        long_out.reshape(long_x.shape),
        short_out.reshape(short_x.shape),
        long_grad.reshape(long_x.shape),
        short_grad.reshape(short_x.shape),
        owned[:, 4 * width],
        owned[:, 4 * width + 1],
        owned[:, : 3 * width],
        owned[:, 3 * width : 4 * width].T,
        owned[:, 4 * width + 2],
        owned[:, 4 * width + 3],
        grad_up[None],
        grad_down[None],
    )


def solution(mesh):
    both = ("dp", "fsdp")
    return jax.shard_map(
        functools.partial(on_device, mesh.shape["dp"], mesh.shape["fsdp"]),
        mesh=mesh,
        in_specs=(
            P(both, None, None),
            P(both, None, None),
            P(both),
            P(both),
            P(both, None),
            P(both),
            P(both),
            P(both, None),
            P(None, both),
            P(both),
            P(both),
            P("fsdp", None, "dp"),
            P("fsdp", "dp", None),
            P(both, None, None),
            P(both, None, None),
        ),
        out_specs=(
            P(both, None, None),
            P(both, None, None),
            P(both, None, None),
            P(both, None, None),
            P(both),
            P(both),
            P(both, None),
            P(None, both),
            P(both),
            P(both),
            P("fsdp", None, "dp"),
            P("fsdp", "dp", None),
        ),
        check_vma=False,
    )
```

```python
import functools

import jax
import jax.numpy as jnp
from jax import lax
from jax.experimental import pallas as pl
from jax.experimental.pallas import tpu as pltpu
from jax.sharding import PartitionSpec as P

MESH = pl.DeviceIdType.MESH
HEAD_DIM = 64
EPSILON = 1e-05
MASKED = -1e30
BF16 = jnp.bfloat16
F32 = jnp.float32
LANES = 128
ROWS = 512
BLOCK = 256
VMEM_LIMIT = 60 * 2**20

NN = (((1,), (0,)), ((), ()))
NT = (((1,), (1,)), ((), ()))
TN = (((0,), (0,)), ((), ()))


def dot(a, b, dims=NN, precision=None):
    return lax.dot_general(a, b, dims, preferred_element_type=F32, precision=precision)


def params(**extra):
    return pltpu.CompilerParams(vmem_limit_bytes=VMEM_LIMIT, **extra)


def cost(flops, moved, exps=0):
    return pl.CostEstimate(flops=int(flops), bytes_accessed=int(moved), transcendentals=int(exps))


def constant(shape):
    return pl.BlockSpec(shape, lambda *_: (0,) * len(shape), pipeline_mode=pl.Buffered(1))


def norm_parts(inputs):
    average = jnp.mean(inputs, -1, keepdims=True)
    centred = inputs - average
    inv_scale = lax.rsqrt(jnp.mean(centred * centred, -1, keepdims=True) + EPSILON)
    return centred * inv_scale, inv_scale


def norm_back(grad_normed, normed, inv_scale):
    centre_term = jnp.mean(grad_normed, -1, keepdims=True)
    slope_term = jnp.mean(grad_normed * normed, -1, keepdims=True)
    return inv_scale * (grad_normed - centre_term - normed * slope_term)


def vectors(vec_ref):
    return jnp.transpose(vec_ref[...].astype(F32))[:8]


def long_short(width, n_long):
    return [
        pl.BlockSpec((ROWS, width), lambda i: (jnp.minimum(i, n_long - 1), 0)),
        pl.BlockSpec((ROWS, width), lambda i: (jnp.maximum(i - n_long, 0), 0)),
    ]


def gather_kernel(
    n_dp, n_f, cap, own_ref, ids_ref, long_ref, short_ref, out_ref, col_ref, row_ref, slots_ref,
    rows_ref, z_send, z_recv, p_send, p_recv, c_send, c_recv, l_sem,
):
    z = lax.axis_index("dp")
    f = lax.axis_index("fsdp")
    half = n_f // 2
    partner = f + 1 - 2 * lax.rem(f, 2)
    barrier = pltpu.get_barrier_semaphore()
    for k in range(1, n_dp):
        pl.semaphore_signal(barrier, 1, device_id=(lax.rem(z + k, n_dp), f), device_id_type=MESH)
    for k in range(1, half):
        pl.semaphore_signal(barrier, 1, device_id=(z, lax.rem(f + 2 * k, n_f)), device_id_type=MESH)
    pl.semaphore_signal(barrier, 1, device_id=(z, partner), device_id_type=MESH)
    local = pltpu.make_async_copy(own_ref, out_ref.at[z, f], l_sem)
    local.start()
    pl.semaphore_wait(barrier, n_dp - 1 + half)

    z_copies = []
    for k in range(1, n_dp):
        copy = pltpu.make_async_remote_copy(
            own_ref, out_ref.at[z, f], z_send.at[k], z_recv.at[k],
            device_id=(lax.rem(z + k, n_dp), f), device_id_type=MESH,
        )
        copy.start()
        z_copies.append(copy)
    number_slots(cap, ids_ref, col_ref, row_ref)
    n_long = long_ref.shape[0]
    rows_ref[:n_long, :] = long_ref[...].astype(BF16)
    rows_ref[n_long:, :] = short_ref[...].astype(BF16)
    local.wait()
    for copy in z_copies:
        copy.wait_recv()
    p_copies = []
    for k in range(1, half):
        copy = pltpu.make_async_remote_copy(
            out_ref.at[:, f], out_ref.at[:, f], p_send.at[k], p_recv.at[k],
            device_id=(z, lax.rem(f + 2 * k, n_f)), device_id_type=MESH,
        )
        copy.start()
        p_copies.append(copy)

    def fill(block, carry):
        start = pl.multiple_of(block * BLOCK, BLOCK)
        slots_ref[pl.ds(start, BLOCK), :] = dispatch_block(row_ref, rows_ref[...], start, BLOCK)
        return carry

    lax.fori_loop(0, slots_ref.shape[0] // BLOCK, fill, 0)
    c_copies = []
    for k in range(half):
        if k:
            p_copies[k - 1].wait_recv()
        column = lax.rem(f + n_f - 2 * k, n_f)
        copy = pltpu.make_async_remote_copy(
            out_ref.at[:, column], out_ref.at[:, column], c_send.at[k], c_recv.at[k],
            device_id=(z, partner), device_id_type=MESH,
        )
        copy.start()
        c_copies.append(copy)
    for copy in c_copies:
        copy.wait_recv()
    for copy in z_copies + p_copies + c_copies:
        copy.wait_send()


def gather_dense(own, ids, long_cot, short_cot, n_dp, n_f, cap, slots):
    count, width = ids.shape[0], long_cot.shape[1]
    vmem = pl.BlockSpec(memory_space=pltpu.VMEM)
    return pl.pallas_call(
        functools.partial(gather_kernel, n_dp, n_f, cap),
        out_shape=[
            jax.ShapeDtypeStruct((n_dp, n_f) + own.shape, own.dtype),
            jax.ShapeDtypeStruct((count, 1), jnp.int32),
            jax.ShapeDtypeStruct((8, count), jnp.int32),
            jax.ShapeDtypeStruct((slots, width), BF16),
        ],
        in_specs=[pl.BlockSpec(memory_space=pl.ANY), vmem, vmem, vmem],
        out_specs=[pl.BlockSpec(memory_space=pl.ANY), vmem, vmem, vmem],
        scratch_shapes=[
            pltpu.VMEM((count, width), BF16),
            pltpu.SemaphoreType.DMA((n_dp,)),
            pltpu.SemaphoreType.DMA((n_dp,)),
            pltpu.SemaphoreType.DMA((n_f // 2,)),
            pltpu.SemaphoreType.DMA((n_f // 2,)),
            pltpu.SemaphoreType.DMA((n_f // 2,)),
            pltpu.SemaphoreType.DMA((n_f // 2,)),
            pltpu.SemaphoreType.DMA,
        ],
        compiler_params=params(collective_id=0, has_side_effects=True),
        cost_estimate=cost(0, 100e6),
        name="gather_dense",
    )(own, ids, long_cot, short_cot)


def scatter_kernel(
    n_dp, n_f, in_ref, out_ref, got1, sum1, got2, sum2, got3,
    c_send, c_recv, p_send, p_recv, z_send, z_recv,
):
    z = lax.axis_index("dp")
    f = lax.axis_index("fsdp")
    half = n_f // 2
    parity = lax.rem(f, 2)
    mine = f // 2
    partner = f + 1 - 2 * parity
    barrier = pltpu.get_barrier_semaphore()
    for k in range(1, n_dp):
        pl.semaphore_signal(barrier, 1, device_id=(lax.rem(z + k, n_dp), f), device_id_type=MESH)
    for k in range(1, half):
        pl.semaphore_signal(barrier, 1, device_id=(z, lax.rem(f + 2 * k, n_f)), device_id_type=MESH)
    pl.semaphore_signal(barrier, 1, device_id=(z, partner), device_id_type=MESH)
    pl.semaphore_wait(barrier, n_dp - 1 + half)

    c_copies = []
    order = list(range(1, half)) + [0]
    for k in order:
        slot = lax.rem(mine + k, half)
        copy = pltpu.make_async_remote_copy(
            in_ref.at[:, 2 * slot + 1 - parity], got1.at[slot], c_send.at[k], c_recv.at[k],
            device_id=(z, partner), device_id_type=MESH,
        )
        copy.start()
        c_copies.append(copy)
    p_copies = []
    for k, c_copy in zip(order, c_copies):
        c_copy.wait_recv()
        slot = lax.rem(mine + k, half)
        sum1[slot] = (in_ref[:, 2 * slot + parity].astype(F32) + got1[slot].astype(F32)).astype(BF16)
        if k:
            copy = pltpu.make_async_remote_copy(
                sum1.at[slot], got2.at[k], p_send.at[k], p_recv.at[k],
                device_id=(z, lax.rem(f + 2 * k, n_f)), device_id_type=MESH,
            )
            copy.start()
            p_copies.append(copy)
    for copy in p_copies:
        copy.wait_recv()
    total = sum1[mine].astype(F32)
    for k in range(1, half):
        total = total + got2[k].astype(F32)
    sum2[...] = total.astype(BF16)
    z_copies = []
    for k in range(1, n_dp):
        there = lax.rem(z + k, n_dp)
        copy = pltpu.make_async_remote_copy(
            sum2.at[there], got3.at[k], z_send.at[k], z_recv.at[k],
            device_id=(there, f), device_id_type=MESH,
        )
        copy.start()
        z_copies.append(copy)
    for copy in z_copies:
        copy.wait_recv()
    total = sum2[z].astype(F32)
    for k in range(1, n_dp):
        total = total + got3[k].astype(F32)
    out_ref[...] = total
    for copy in c_copies + p_copies + z_copies:
        copy.wait_send()


def scatter_dense(grads, n_dp, n_f):
    block = grads.shape[2:]
    half = n_f // 2
    return pl.pallas_call(
        functools.partial(scatter_kernel, n_dp, n_f),
        out_shape=jax.ShapeDtypeStruct(block, F32),
        in_specs=[pl.BlockSpec(memory_space=pltpu.VMEM)],
        out_specs=pl.BlockSpec(memory_space=pltpu.VMEM),
        scratch_shapes=[
            pltpu.VMEM((half, n_dp) + block, BF16),
            pltpu.VMEM((half, n_dp) + block, BF16),
            pltpu.VMEM((half, n_dp) + block, BF16),
            pltpu.VMEM((n_dp,) + block, BF16),
            pltpu.VMEM((n_dp,) + block, BF16),
            pltpu.SemaphoreType.DMA((half,)),
            pltpu.SemaphoreType.DMA((half,)),
            pltpu.SemaphoreType.DMA((half,)),
            pltpu.SemaphoreType.DMA((half,)),
            pltpu.SemaphoreType.DMA((n_dp,)),
            pltpu.SemaphoreType.DMA((n_dp,)),
        ],
        compiler_params=params(collective_id=1, has_side_effects=True),
        cost_estimate=cost(0, 100e6),
        name="scatter_dense",
    )(grads)


def dispatch_block(slot_row_ref, rows, first, size):
    slot_id = first + lax.broadcasted_iota(jnp.int32, (size, 1), 0)
    chosen = (slot_row_ref[0:1, :] == slot_id).astype(F32).astype(BF16)
    return dot(chosen, rows).astype(BF16)


def number_slots(cap, ids_ref, col_ref, row_ref):
    count = ids_ref.shape[0]
    lane = lax.broadcasted_iota(jnp.int32, (1, LANES), 1)
    onehot = (ids_ref[...] == lane).astype(F32)
    onehot_low = onehot.astype(BF16)
    col = lax.broadcasted_iota(jnp.int32, (1, count), 1)
    base = (lane * cap).astype(F32)
    ones = jnp.ones((8, LANES), F32)
    for start in range(0, count, ROWS):
        row = start + lax.broadcasted_iota(jnp.int32, (ROWS, 1), 0)
        before = dot((col < row).astype(F32).astype(BF16), onehot_low)
        picked = (before + base) * onehot[start : start + ROWS]
        col_ref[start : start + ROWS, :] = jnp.sum(picked, 1, keepdims=True).astype(jnp.int32)
        row_ref[:, start : start + ROWS] = dot(
            ones, picked, NT, precision=lax.Precision.HIGHEST
        ).astype(jnp.int32)


def peers(n_f):
    f = lax.axis_index("fsdp")
    half = n_f // 2
    chip, core = f // 2, lax.rem(f, 2)

    def to(k):
        return lax.rem(chip + k // 2, half) * 2 + lax.rem(core + lax.rem(k, 2), 2)

    def source(k):
        return lax.rem(chip + half - k // 2, half) * 2 + lax.rem(core + lax.rem(k, 2), 2)

    return f, to, source


def greet(n_f, to):
    z = lax.axis_index("dp")
    barrier = pltpu.get_barrier_semaphore()
    for k in range(1, n_f):
        pl.semaphore_signal(barrier, 1, device_id=(z, to(k)), device_id_type=MESH)


def qkv_kernel(n_long, width, long_ref, short_ref, w_ref, vec_ref, qkv_ref, vec_scr):
    i = pl.program_id(0)

    @pl.when(i == 0)
    def _():
        vec_scr[...] = vectors(vec_ref)

    def body(x_ref):
        normed, _ = norm_parts(x_ref[...])
        rows = (normed * vec_scr[0:1, :] + vec_scr[1:2, :]).astype(BF16)
        for part in range(3):
            cut = slice(part * width, (part + 1) * width)
            out = dot(rows, w_ref[:, cut])
            if part == 0:
                out = out * HEAD_DIM ** (-0.5)
            qkv_ref[:, cut] = out.astype(BF16)

    pl.when(i < n_long)(lambda: body(long_ref))
    pl.when(i >= n_long)(lambda: body(short_ref))


def make_qkv(long_x, short_x, dense):
    width = long_x.shape[1]
    n_long, n_short = long_x.shape[0] // ROWS, short_x.shape[0] // ROWS
    count = long_x.shape[0] + short_x.shape[0]
    return pl.pallas_call(
        functools.partial(qkv_kernel, n_long, width),
        grid=(n_long + n_short,),
        in_specs=long_short(width, n_long)
        + [
            constant((width, 3 * width)),
            pl.BlockSpec((width, LANES), lambda i: (0, 4 * width // LANES)),
        ],
        out_specs=pl.BlockSpec((ROWS, 3 * width), lambda i: (i, 0)),
        out_shape=jax.ShapeDtypeStruct((count, 3 * width), BF16),
        scratch_shapes=[pltpu.VMEM((8, width), F32)],
        compiler_params=params(),
        cost_estimate=cost(6 * count * width * width, count * width * 10 + 6 * width * width),
        name="make_qkv",
    )(long_x, short_x, dense, dense)


def sequences(long_shape, short_shape):
    found = []
    start = 0
    for which, (number, length) in enumerate((long_shape, short_shape)):
        for index in range(number):
            found.append((start, length, which, index))
            start += length
    return found


def head_masks():
    lane = lax.broadcasted_iota(jnp.int32, (1, LANES), 1)
    return (lane < HEAD_DIM, lane >= HEAD_DIM)


def attend_kernel(seqs, long_len, short_len, q_ref, k_ref, v_ref, o_ref, lse_ref):
    pair = pl.program_id(0)
    masks = head_masks()
    lane = lax.broadcasted_iota(jnp.int32, (1, LANES), 1)

    @pl.when(pair == 0)
    def _():
        lse_ref[...] = jnp.zeros_like(lse_ref)

    causal = lax.broadcasted_iota(jnp.int32, (BLOCK, BLOCK), 1) <= lax.broadcasted_iota(
        jnp.int32, (BLOCK, BLOCK), 0
    )
    for start, length, which, index in seqs:
        valid = (short_len if which else long_len)[index]
        key_pos = lax.broadcasted_iota(jnp.int32, (1, length), 1)
        bias = jnp.where(key_pos < valid, 0.0, MASKED)
        for first in range(0, length, BLOCK):
            here = slice(start + first, start + first + BLOCK)
            past = slice(start, start + first)
            q = q_ref[here, :]
            outs = []
            stats = jnp.zeros((BLOCK, LANES), F32)
            for head in range(2):
                qh = jnp.where(masks[head], q, jnp.zeros_like(q))
                near = dot(qh, k_ref[here, :], NT) + bias[:, first : first + BLOCK]
                near = jnp.where(causal, near, MASKED)
                top = jnp.max(near, 1, keepdims=True)
                if first:
                    far = dot(qh, k_ref[past, :], NT) + bias[:, :first]
                    top = jnp.maximum(top, jnp.max(far, 1, keepdims=True))
                near = jnp.exp(near - top)
                total = jnp.sum(near, 1, keepdims=True)
                out = dot(near.astype(BF16), v_ref[here, :])
                if first:
                    far = jnp.exp(far - top)
                    total = total + jnp.sum(far, 1, keepdims=True)
                    out = out + dot(far.astype(BF16), v_ref[past, :])
                outs.append(out * (1.0 / total))
                stats = jnp.where(lane == 2 * pair + head, top + jnp.log(total), stats)
            o_ref[here, :] = jnp.where(masks[0], outs[0], outs[1]).astype(BF16)
            lse_ref[here, :] = lse_ref[here, :] + stats


def attend(qkv, long_len, short_len, seqs):
    count, width = qkv.shape[0], qkv.shape[1] // 3
    pairs = width // LANES
    return pl.pallas_call(
        functools.partial(attend_kernel, seqs),
        grid=(pairs,),
        in_specs=[pl.BlockSpec(memory_space=pltpu.SMEM)] * 2
        + [
            pl.BlockSpec((count, LANES), lambda i: (0, i)),
            pl.BlockSpec((count, LANES), lambda i: (0, i + pairs)),
            pl.BlockSpec((count, LANES), lambda i: (0, i + 2 * pairs)),
        ],
        out_specs=[
            pl.BlockSpec((count, LANES), lambda i: (0, i)),
            pl.BlockSpec((count, LANES), lambda i: (0, 0)),
        ],
        out_shape=[
            jax.ShapeDtypeStruct((count, width), BF16),
            jax.ShapeDtypeStruct((count, LANES), F32),
        ],
        compiler_params=params(),
        cost_estimate=cost(16e9, 8 * count * width, 10e6),
        name="attend",
    )(long_len, short_len, qkv, qkv, qkv)


def attend_back_kernel(
    seqs, long_len, short_len, q_ref, k_ref, v_ref, o_ref, do_ref, lse_ref,
    dq_ref, dk_ref, dv_ref, acc_ref, row_ref,
):
    pair = pl.program_id(0)
    masks = head_masks()
    lane = lax.broadcasted_iota(jnp.int32, (8, LANES), 1)
    which_row = lax.broadcasted_iota(jnp.int32, (8, LANES), 0)
    pick = (lane == 2 * pair + which_row).astype(F32) * (which_row < 2).astype(F32)
    split = (lane // HEAD_DIM == which_row).astype(F32)
    row_ref[0:8, :] = dot(pick, lse_ref[...], NT, precision=lax.Precision.HIGHEST)
    row_ref[8:16, :] = dot(
        split, do_ref[...].astype(F32) * o_ref[...].astype(F32), NT,
        precision=lax.Precision.HIGHEST,
    )
    acc_ref[...] = jnp.zeros_like(acc_ref)
    causal = lax.broadcasted_iota(jnp.int32, (BLOCK, BLOCK), 0) <= lax.broadcasted_iota(
        jnp.int32, (BLOCK, BLOCK), 1
    )
    for start, length, which, index in seqs:
        valid = (short_len if which else long_len)[index]
        for first in range(0, length, BLOCK):
            here = slice(start + first, start + first + BLOCK)
            k, v = k_ref[here, :], v_ref[here, :]
            key_pos = first + lax.broadcasted_iota(jnp.int32, (BLOCK, 1), 0)
            inside = key_pos < valid
            dk = jnp.zeros((BLOCK, LANES), F32)
            dv = jnp.zeros((BLOCK, LANES), F32)
            for head in range(2):
                kh = jnp.where(masks[head], k, jnp.zeros_like(k))
                for rows, allowed in (
                    (here, inside & causal),
                    (slice(here.stop, start + length), inside),
                ):
                    if rows.start == rows.stop:
                        continue
                    q, do = q_ref[rows, :], do_ref[rows, :]
                    qh = jnp.where(masks[head], q, jnp.zeros_like(q))
                    doh = jnp.where(masks[head], do, jnp.zeros_like(do))
                    scores = dot(k, qh, NT)
                    p = jnp.where(allowed, jnp.exp(scores - row_ref[head : head + 1, rows]), 0.0)
                    dp = dot(v, doh, NT)
                    ds = (p * (dp - row_ref[8 + head : 9 + head, rows])).astype(BF16)
                    dv = dv + dot(p.astype(BF16), doh)
                    dk = dk + dot(ds, qh)
                    acc_ref[rows, :] = acc_ref[rows, :] + dot(ds, kh, TN)
            dk_ref[here, :] = dk.astype(BF16)
            dv_ref[here, :] = dv.astype(BF16)
    dq_ref[...] = (acc_ref[...] * HEAD_DIM ** (-0.5)).astype(BF16)


def attend_back(qkv, o, d_o, lse, long_len, short_len, seqs):
    count, width = o.shape
    pairs = width // LANES
    one = pl.BlockSpec((count, LANES), lambda i: (0, i))
    return pl.pallas_call(
        functools.partial(attend_back_kernel, seqs),
        grid=(pairs,),
        in_specs=[pl.BlockSpec(memory_space=pltpu.SMEM)] * 2
        + [
            one,
            pl.BlockSpec((count, LANES), lambda i: (0, i + pairs)),
            pl.BlockSpec((count, LANES), lambda i: (0, i + 2 * pairs)),
            one,
            one,
            constant((count, LANES)),
        ],
        out_specs=[one, one, one],
        out_shape=[jax.ShapeDtypeStruct((count, width), BF16)] * 3,
        scratch_shapes=[pltpu.VMEM((count, LANES), F32), pltpu.VMEM((16, count), F32)],
        compiler_params=params(),
        cost_estimate=cost(40e9, 16 * count * width, 10e6),
        name="attend_back",
    )(long_len, short_len, qkv, qkv, qkv, o, d_o, lse)


def gelu_parts(pre):
    scale = 0.7978845608028654
    square = pre * pre
    flat = jnp.tanh(scale * pre * (1.0 + 0.044715 * square))
    half = 0.5 * (1.0 + flat)
    slope = half + (0.5 * scale) * pre * (1.0 - flat * flat) * (1.0 + 0.134145 * square)
    return half * pre, slope


def forward_kernel(
    n_f, n_long, n_rows, long_ref, short_ref, o_ref, w_ref, vec_ref, row_ref, g_ref, up_ref,
    h_ref, there_ref, act_ref, slope_ref, gd_ref,
    rows_ref, vec_scr, out_buf, in_buf, all_ref, send, recv,
):
    i = pl.program_id(0)
    z = lax.axis_index("dp")
    f, to, source = peers(n_f)
    cap, width = out_buf.shape[1:]
    n_up = n_rows + n_f
    n_down = n_up + n_f
    barrier = pltpu.get_barrier_semaphore()

    def transfer(k):
        return pltpu.make_async_remote_copy(
            out_buf.at[k], in_buf.at[f], send.at[k], recv.at[k],
            device_id=(z, to(k)), device_id_type=MESH,
        )

    @pl.when(i == 0)
    def _():
        greet(n_f, to)
        vec_scr[...] = vectors(vec_ref)

    def body(x_ref):
        hidden = x_ref[...] + dot(o_ref[...], w_ref[...], NT)
        h_ref[...] = hidden
        normed, _ = norm_parts(hidden)
        rows_ref[pl.ds(pl.multiple_of(i * ROWS, ROWS), ROWS), :] = (
            normed * vec_scr[2:3, :] + vec_scr[3:4, :]
        ).astype(BF16)

    pl.when(i < n_long)(lambda: body(long_ref))
    pl.when((i >= n_long) & (i < n_rows))(lambda: body(short_ref))

    @pl.when(i == n_rows)
    def _():
        pl.semaphore_wait(barrier, n_f - 1)

    @pl.when((i >= n_rows) & (i < n_up - 1))
    def _():
        k = i - n_rows + 1
        out_buf[k] = dispatch_block(row_ref, rows_ref[...], to(k) * cap, cap)
        transfer(k).start()

    @pl.when(i == n_up - 1)
    def _():
        in_buf[f] = dispatch_block(row_ref, rows_ref[...], f * cap, cap)

    @pl.when((i > n_up) & (i < n_down))
    def _():
        transfer(i - n_up).wait_recv()

    @pl.when((i >= n_up) & (i < n_down))
    def _():
        origin = source(i - n_up)
        rows = in_buf[origin]
        here = pl.ds(pl.multiple_of(origin * cap, cap), cap)
        for first in range(0, up_ref.shape[1], width):
            cut = slice(first, first + width)
            act, slope = gelu_parts(dot(rows, up_ref[:, cut]))
            act = act.astype(BF16)
            act_ref[:, cut] = act
            slope_ref[:, cut] = slope.astype(BF16)
            all_ref[here, cut] = act
        there_ref[here, :] = rows

    @pl.when(i >= n_down)
    def _():
        cut = pl.ds(pl.multiple_of((i - n_down) * width, width), width)
        gd_ref[...] = dot(all_ref[:, cut], g_ref[...], TN).astype(BF16)

    @pl.when(i == pl.num_programs(0) - 1)
    def _():
        for k in range(1, n_f):
            transfer(k).wait_send()


def forward_experts(long_x, short_x, o, dense, slot_row, g_there, up, n_f, cap):
    width = long_x.shape[1]
    hidden = up.shape[1]
    n_long, n_short = long_x.shape[0] // ROWS, short_x.shape[0] // ROWS
    n_rows = n_long + n_short
    n_up = n_rows + n_f
    n_down = n_up + n_f
    n_hidden = hidden // width
    slots = n_f * cap
    count = o.shape[0]
    tile = pl.BlockSpec((cap, hidden), lambda i: (jnp.clip(i - n_up, 0, n_f - 1), 0))
    return pl.pallas_call(
        functools.partial(forward_kernel, n_f, n_long, n_rows),
        grid=(n_down + n_hidden,),
        in_specs=[
            pl.BlockSpec((ROWS, width), lambda i: (jnp.minimum(i, n_long - 1), 0)),
            pl.BlockSpec((ROWS, width), lambda i: (jnp.clip(i - n_long, 0, n_short - 1), 0)),
            pl.BlockSpec((ROWS, width), lambda i: (jnp.minimum(i, n_rows - 1), 0)),
            pl.BlockSpec((width, width), lambda i: (0, 3), pipeline_mode=pl.Buffered(1)),
            pl.BlockSpec((width, LANES), lambda i: (0, 4 * width // LANES)),
            constant((8, count)),
            constant((slots, width)),
            constant((width, hidden)),
        ],
        out_specs=[
            pl.BlockSpec((ROWS, width), lambda i: (jnp.minimum(i, n_rows - 1), 0)),
            pl.BlockSpec((slots, width), lambda i: (0, 0)),
            tile,
            tile,
            pl.BlockSpec((width, width), lambda i: (jnp.clip(i - n_down, 0, n_hidden - 1), 0)),
        ],
        out_shape=[
            jax.ShapeDtypeStruct((count, width), F32),
            jax.ShapeDtypeStruct((slots, width), BF16),
            jax.ShapeDtypeStruct((slots, hidden), BF16),
            jax.ShapeDtypeStruct((slots, hidden), BF16),
            jax.ShapeDtypeStruct((hidden, width), BF16),
        ],
        scratch_shapes=[
            pltpu.VMEM((count, width), BF16),
            pltpu.VMEM((8, width), F32),
            pltpu.VMEM((n_f, cap, width), BF16),
            pltpu.VMEM((n_f, cap, width), BF16),
            pltpu.VMEM((slots, hidden), BF16),
            pltpu.SemaphoreType.DMA((n_f,)),
            pltpu.SemaphoreType.DMA((n_f,)),
        ],
        compiler_params=params(collective_id=2, has_side_effects=True),
        cost_estimate=cost(
            2 * slots * width * (count + 2 * hidden), 60e6, slots * hidden
        ),
        name="forward_experts",
    )(long_x, short_x, o, dense, dense, slot_row, g_there, up)


def back_kernel(
    n_f, b_ref, g_ref, act_ref, slope_ref, up_ref, down_ref, y_ref, db_ref, gu_ref,
    out_buf, all_ref, send, recv, l_sem,
):
    i = pl.program_id(0)
    z = lax.axis_index("dp")
    f, to, source = peers(n_f)
    cap, width = out_buf.shape[1:]
    barrier = pltpu.get_barrier_semaphore()

    def transfer(k):
        return pltpu.make_async_remote_copy(
            out_buf.at[k], db_ref.at[f], send.at[k], recv.at[k],
            device_id=(z, source(k)), device_id_type=MESH,
        )

    keep = pltpu.make_async_copy(out_buf.at[0], db_ref.at[f], l_sem)

    @pl.when(i == 0)
    def _():
        z_ = lax.axis_index("dp")
        for k in range(1, n_f):
            pl.semaphore_signal(barrier, 1, device_id=(z_, source(k)), device_id_type=MESH)

    @pl.when(i < n_f)
    def _():
        k = n_f - 1 - i
        here = pl.ds(pl.multiple_of(source(k) * cap, cap), cap)
        g = g_ref[here, :]
        d_b = jnp.zeros((cap, width), F32)
        for first in range(0, up_ref.shape[1], width):
            cut = slice(first, first + width)
            d_act = dot(g, down_ref[cut, :], NT)
            d_pre = (d_act * slope_ref[:, cut].astype(F32)).astype(BF16)
            all_ref[here, cut] = d_pre
            d_b = d_b + dot(d_pre, up_ref[:, cut], NT)
        out_buf[k] = d_b.astype(BF16)

    @pl.when(i == 0)
    def _():
        pl.semaphore_wait(barrier, n_f - 1)

    @pl.when(i < n_f - 1)
    def _():
        transfer(n_f - 1 - i).start()

    @pl.when(i == n_f - 1)
    def _():
        keep.start()

    @pl.when(i < n_f)
    def _():
        here = pl.ds(pl.multiple_of(source(n_f - 1 - i) * cap, cap), cap)
        y_ref[here, :] = dot(act_ref[...], down_ref[...]).astype(BF16)

    @pl.when(i >= n_f)
    def _():
        cut = pl.ds(pl.multiple_of((i - n_f) * width, width), width)
        gu_ref[...] = dot(b_ref[...], all_ref[:, cut], TN).astype(BF16)

    @pl.when(i == pl.num_programs(0) - 1)
    def _():
        keep.wait()
        for k in range(1, n_f):
            transfer(k).wait_recv()
        for k in range(1, n_f):
            transfer(k).wait_send()


def back_experts(b_there, g_there, act, slope, up, down, n_f, cap):
    slots, width = b_there.shape
    hidden = up.shape[1]
    n_hidden = hidden // width
    tile = pl.BlockSpec((cap, hidden), lambda i: (jnp.maximum(n_f - 1 - i, 0), 0))
    return pl.pallas_call(
        functools.partial(back_kernel, n_f),
        grid=(n_f + n_hidden,),
        in_specs=[
            constant((slots, width)),
            constant((slots, width)),
            tile,
            tile,
            constant((width, hidden)),
            constant((hidden, width)),
        ],
        out_specs=[
            pl.BlockSpec((slots, width), lambda i: (0, 0)),
            pl.BlockSpec(memory_space=pl.ANY),
            pl.BlockSpec((width, width), lambda i: (0, jnp.maximum(i - n_f, 0))),
        ],
        out_shape=[
            jax.ShapeDtypeStruct((slots, width), BF16),
            jax.ShapeDtypeStruct((n_f, cap, width), BF16),
            jax.ShapeDtypeStruct((width, hidden), BF16),
        ],
        scratch_shapes=[
            pltpu.VMEM((n_f, cap, width), BF16),
            pltpu.VMEM((slots, hidden), BF16),
            pltpu.SemaphoreType.DMA((n_f,)),
            pltpu.SemaphoreType.DMA((n_f,)),
            pltpu.SemaphoreType.DMA,
        ],
        compiler_params=params(collective_id=3, has_side_effects=True),
        cost_estimate=cost(8 * slots * width * hidden, 60e6),
        name="back_experts",
    )(b_there, g_there, act, slope, up, down)


def combine_rows(col_ref, slots_ref):
    slot_id = lax.broadcasted_iota(jnp.int32, (1, slots_ref.shape[0]), 1)
    chosen = (col_ref[...] == slot_id).astype(F32).astype(BF16)
    return dot(chosen, slots_ref[...])


def finish_kernel(n_long, h_ref, col_ref, y_ref, long_ref, short_ref):
    i = pl.program_id(0)
    out = h_ref[...] + combine_rows(col_ref, y_ref)

    @pl.when(i < n_long)
    def _():
        long_ref[...] = out

    @pl.when(i >= n_long)
    def _():
        short_ref[...] = out


def finish(h, slot_col, y_back, n_long, n_short):
    count, width = h.shape
    slots = y_back.shape[0]
    return pl.pallas_call(
        functools.partial(finish_kernel, n_long),
        grid=(n_long + n_short,),
        in_specs=[
            pl.BlockSpec((ROWS, width), lambda i: (i, 0)),
            pl.BlockSpec((ROWS, 1), lambda i: (i, 0)),
            constant((slots, width)),
        ],
        out_specs=long_short(width, n_long),
        out_shape=[
            jax.ShapeDtypeStruct((n_long * ROWS, width), F32),
            jax.ShapeDtypeStruct((n_short * ROWS, width), F32),
        ],
        compiler_params=params(),
        cost_estimate=cost(2 * slots * count * width, 8 * count * width + 2 * slots * width),
        name="finish",
    )(h, slot_col, y_back)


def hidden_back_kernel(
    n_long, n_rows, h_ref, col_ref, db_ref, long_ref, short_ref, o_ref, w_ref, vec_ref,
    dh_ref, do_ref, gp_ref, gv_ref, acc_ref, vec_scr,
):
    i = pl.program_id(0)

    @pl.when(i == 0)
    def _():
        vec_scr[...] = vectors(vec_ref)
        acc_ref[...] = jnp.zeros_like(acc_ref)
        gv_ref[...] = jnp.zeros_like(gv_ref)

    def body(cot_ref):
        d_b = combine_rows(col_ref, db_ref)
        normed, inv_scale = norm_parts(h_ref[...])
        gv_ref[0:1, :] = gv_ref[0:1, :] + jnp.sum(d_b * normed, 0, keepdims=True)
        gv_ref[1:2, :] = gv_ref[1:2, :] + jnp.sum(d_b, 0, keepdims=True)
        d_h = cot_ref[...] + norm_back(d_b * vec_scr[2:3, :], normed, inv_scale)
        dh_ref[...] = d_h
        d_attn = d_h.astype(BF16)
        do_ref[...] = dot(d_attn, w_ref[...]).astype(BF16)
        acc_ref[...] = acc_ref[...] + dot(d_attn, o_ref[...], TN)

    pl.when(i < n_long)(lambda: body(long_ref))
    pl.when(i >= n_long)(lambda: body(short_ref))

    @pl.when(i == n_rows - 1)
    def _():
        gp_ref[...] = acc_ref[...].astype(BF16)


def hidden_back(h, slot_col, db_back, long_cot, short_cot, o, dense):
    count, width = h.shape
    slots = db_back.shape[0]
    n_long, n_short = long_cot.shape[0] // ROWS, short_cot.shape[0] // ROWS
    n_rows = n_long + n_short
    row = pl.BlockSpec((ROWS, width), lambda i: (i, 0))
    return pl.pallas_call(
        functools.partial(hidden_back_kernel, n_long, n_rows),
        grid=(n_rows,),
        in_specs=[row, pl.BlockSpec((ROWS, 1), lambda i: (i, 0)), constant((slots, width))]
        + long_short(width, n_long)
        + [
            row,
            pl.BlockSpec((width, width), lambda i: (0, 3)),
            pl.BlockSpec((width, LANES), lambda i: (0, 4 * width // LANES)),
        ],
        out_specs=[
            row,
            row,
            pl.BlockSpec((width, width), lambda i: (0, 0)),
            pl.BlockSpec((8, width), lambda i: (0, 0)),
        ],
        out_shape=[
            jax.ShapeDtypeStruct((count, width), F32),
            jax.ShapeDtypeStruct((count, width), BF16),
            jax.ShapeDtypeStruct((width, width), BF16),
            jax.ShapeDtypeStruct((8, width), F32),
        ],
        scratch_shapes=[pltpu.VMEM((width, width), F32), pltpu.VMEM((8, width), F32)],
        compiler_params=params(),
        cost_estimate=cost(2 * (slots + 2 * width) * count * width, 16 * count * width),
        name="hidden_back",
    )(h, slot_col, db_back, long_cot, short_cot, o, dense, dense)


def input_back_kernel(
    n_long, n_rows, width, long_ref, short_ref, dh_ref, dq_ref, dk_ref, dv_ref, w_ref, vec_ref,
    gp_ref, gv_ref, lg_ref, sg_ref, out_ref, acc_ref, vec_scr, gv_scr,
):
    i = pl.program_id(0)

    @pl.when(i == 0)
    def _():
        vec_scr[...] = vectors(vec_ref)
        acc_ref[...] = jnp.zeros_like(acc_ref)
        gv_scr[...] = jnp.zeros_like(gv_scr)
        gv_scr[2:4, :] = gv_ref[0:2, :]

    def body(x_ref, grad_ref):
        normed, inv_scale = norm_parts(x_ref[...])
        rows = (normed * vec_scr[0:1, :] + vec_scr[1:2, :]).astype(BF16)
        entered = jnp.zeros_like(normed)
        for part, d_ref in enumerate((dq_ref, dk_ref, dv_ref)):
            cut = slice(part * width, (part + 1) * width)
            entered = entered + dot(d_ref[...], w_ref[:, cut], NT)
            acc_ref[:, cut] = acc_ref[:, cut] + dot(rows, d_ref[...], TN)
        gv_scr[0:1, :] = gv_scr[0:1, :] + jnp.sum(entered * normed, 0, keepdims=True)
        gv_scr[1:2, :] = gv_scr[1:2, :] + jnp.sum(entered, 0, keepdims=True)
        grad_ref[...] = dh_ref[...] + norm_back(entered * vec_scr[0:1, :], normed, inv_scale)

    pl.when(i < n_long)(lambda: body(long_ref, lg_ref))
    pl.when(i >= n_long)(lambda: body(short_ref, sg_ref))

    @pl.when(i == n_rows - 1)
    def _():
        out_ref[:, : 3 * width] = acc_ref[...].astype(BF16)
        out_ref[:, 3 * width : 4 * width] = gp_ref[...]
        out_ref[:, 4 * width :] = jnp.transpose(gv_scr[...]).astype(BF16)


def input_back(long_x, short_x, d_h, dq, dk, dv, dense, grad_proj, grad_vec):
    count, width = d_h.shape
    n_long, n_short = long_x.shape[0] // ROWS, short_x.shape[0] // ROWS
    n_rows = n_long + n_short
    row = pl.BlockSpec((ROWS, width), lambda i: (i, 0))
    return pl.pallas_call(
        functools.partial(input_back_kernel, n_long, n_rows, width),
        grid=(n_rows,),
        in_specs=long_short(width, n_long)
        + [
            row,
            row,
            row,
            row,
            constant((width, 3 * width)),
            pl.BlockSpec((width, LANES), lambda i: (0, 4 * width // LANES)),
            constant((width, width)),
            constant((8, width)),
        ],
        out_specs=long_short(width, n_long)
        + [pl.BlockSpec((width, 4 * width + LANES), lambda i: (0, 0))],
        out_shape=[
            jax.ShapeDtypeStruct(long_x.shape, F32),
            jax.ShapeDtypeStruct(short_x.shape, F32),
            jax.ShapeDtypeStruct((width, 4 * width + LANES), BF16),
        ],
        scratch_shapes=[
            pltpu.VMEM((width, 3 * width), F32),
            pltpu.VMEM((8, width), F32),
            pltpu.VMEM((LANES, width), F32),
        ],
        compiler_params=params(),
        cost_estimate=cost(12 * count * width * width, 20 * count * width),
        name="input_back",
    )(long_x, short_x, d_h, dq, dk, dv, dense, dense, grad_proj, grad_vec)


def on_device(
    n_dp, n_f, long_x, short_x, long_len, short_len, expert_ids, ln1_gain, ln1_bias,
    w_qkv, w_proj, ln2_gain, ln2_bias, w_up, w_down, long_cot, short_cot,
):
    width = long_x.shape[2]
    share = w_qkv.shape[0]
    seqs = sequences(long_x.shape[:2], short_x.shape[:2])
    flat = lambda a: a.reshape(-1, width)
    xl, xs, gl, gs = flat(long_x), flat(short_x), flat(long_cot), flat(short_cot)
    n_long, n_short = xl.shape[0] // ROWS, xs.shape[0] // ROWS
    experts = n_f * w_up.shape[0]
    cap = 4 * expert_ids.shape[0] // (3 * experts)
    slots = experts * cap

    up = lax.all_gather(w_up, "dp", axis=2, tiled=True)[0]
    down = lax.all_gather(w_down, "dp", axis=1, tiled=True)[0]

    vec = jnp.stack([ln1_gain, ln1_bias, ln2_gain, ln2_bias], 1)
    own = jnp.concatenate(
        [w_qkv, w_proj.T, jnp.pad(vec, ((0, 0), (0, LANES - vec.shape[1])))], 1
    )
    dense, slot_col, slot_row, g_slots = gather_dense(
        own, expert_ids, gl, gs, n_dp, n_f, cap, slots
    )
    dense = dense.reshape(n_dp * n_f * share, own.shape[1])

    def exchange(rows):
        sent = lax.all_to_all(
            rows.reshape(n_f, cap, width), "fsdp", split_axis=0, concat_axis=0, tiled=True
        )
        return sent.reshape(slots, width)

    g_there = exchange(g_slots)
    qkv = make_qkv(xl, xs, dense)
    o, lse = attend(qkv, long_len, short_len, seqs)
    h, b_there, act, slope, grad_down = forward_experts(
        xl, xs, o, dense, slot_row, g_there, up, n_f, cap
    )
    grad_down = lax.psum_scatter(grad_down, "dp", scatter_dimension=0, tiled=True).astype(F32)
    y, db_back, grad_up = back_experts(b_there, g_there, act, slope, up, down, n_f, cap)
    db_back = db_back.reshape(slots, width)
    grad_up = lax.psum_scatter(grad_up, "dp", scatter_dimension=1, tiled=True).astype(F32)
    y_back = exchange(y)
    d_h, d_o, grad_proj, grad_vec = hidden_back(h, slot_col, db_back, gl, gs, o, dense)
    long_out, short_out = finish(h, slot_col, y_back, n_long, n_short)
    dq, dk, dv = attend_back(qkv, o, d_o, lse, long_len, short_len, seqs)
    long_grad, short_grad, grads = input_back(xl, xs, d_h, dq, dk, dv, dense, grad_proj, grad_vec)
    owned = scatter_dense(grads.reshape(n_dp, n_f, share, own.shape[1]), n_dp, n_f)
    return (
        long_out.reshape(long_x.shape),
        short_out.reshape(short_x.shape),
        long_grad.reshape(long_x.shape),
        short_grad.reshape(short_x.shape),
        owned[:, 4 * width],
        owned[:, 4 * width + 1],
        owned[:, : 3 * width],
        owned[:, 3 * width : 4 * width].T,
        owned[:, 4 * width + 2],
        owned[:, 4 * width + 3],
        grad_up[None],
        grad_down[None],
    )


def solution(mesh):
    both = ("dp", "fsdp")
    return jax.shard_map(
        functools.partial(on_device, mesh.shape["dp"], mesh.shape["fsdp"]),
        mesh=mesh,
        in_specs=(
            P(both, None, None),
            P(both, None, None),
            P(both),
            P(both),
            P(both, None),
            P(both),
            P(both),
            P(both, None),
            P(None, both),
            P(both),
            P(both),
            P("fsdp", None, "dp"),
            P("fsdp", "dp", None),
            P(both, None, None),
            P(both, None, None),
        ),
        out_specs=(
            P(both, None, None),
            P(both, None, None),
            P(both, None, None),
            P(both, None, None),
            P(both),
            P(both),
            P(both, None),
            P(None, both),
            P(both),
            P(both),
            P("fsdp", None, "dp"),
            P("fsdp", "dp", None),
        ),
        check_vma=False,
    )
```

```python
import functools

import jax
import jax.numpy as jnp
from jax import lax
from jax.experimental import pallas as pl
from jax.experimental.pallas import tpu as pltpu
from jax.sharding import PartitionSpec as P

MESH = pl.DeviceIdType.MESH
HEAD_DIM = 64
EPSILON = 1e-05
MASKED = -1e30
BF16 = jnp.bfloat16
F32 = jnp.float32
LANES = 128
ROWS = 512
BLOCK = 256
ATTEND = 512
ATTEND_BACK = 512
VMEM_LIMIT = 60 * 2**20
N_CHUNKS = 3

NN = (((1,), (0,)), ((), ()))
NT = (((1,), (1,)), ((), ()))
TN = (((0,), (0,)), ((), ()))


def dot(a, b, dims=NN, precision=None):
    return lax.dot_general(a, b, dims, preferred_element_type=F32, precision=precision)


def params(**extra):
    return pltpu.CompilerParams(vmem_limit_bytes=VMEM_LIMIT, **extra)


def cost(flops, moved, exps=0):
    return pl.CostEstimate(flops=int(flops), bytes_accessed=int(moved), transcendentals=int(exps))


def constant(shape):
    return pl.BlockSpec(shape, lambda *_: (0,) * len(shape), pipeline_mode=pl.Buffered(1))


def norm_parts(inputs):
    average = jnp.mean(inputs, -1, keepdims=True)
    centred = inputs - average
    inv_scale = lax.rsqrt(jnp.mean(centred * centred, -1, keepdims=True) + EPSILON)
    return centred * inv_scale, inv_scale


def norm_back(grad_normed, normed, inv_scale):
    centre_term = jnp.mean(grad_normed, -1, keepdims=True)
    slope_term = jnp.mean(grad_normed * normed, -1, keepdims=True)
    return inv_scale * (grad_normed - centre_term - normed * slope_term)


def vectors(vec_ref):
    return jnp.transpose(vec_ref[...].astype(F32))[:8]


def long_short(width, n_long):
    return [
        pl.BlockSpec((ROWS, width), lambda i: (jnp.minimum(i, n_long - 1), 0)),
        pl.BlockSpec((ROWS, width), lambda i: (jnp.maximum(i - n_long, 0), 0)),
    ]


def column_chunks(columns):
    tiles = columns // LANES
    edges = [LANES * (tiles * c // N_CHUNKS) for c in range(N_CHUNKS + 1)]
    return [slice(lo, hi) for lo, hi in zip(edges, edges[1:])]


def gather_kernel(
    n_dp, n_f, cap, own_ref, ids_ref, long_ref, short_ref, out_ref, col_ref, row_ref, slots_ref,
    rows_ref, z_send, z_recv, p_send, p_recv, c_send, c_recv, l_sem,
):
    z = lax.axis_index("dp")
    f = lax.axis_index("fsdp")
    half = n_f // 2
    partner = f + 1 - 2 * lax.rem(f, 2)
    barrier = pltpu.get_barrier_semaphore()
    for k in range(1, n_dp):
        pl.semaphore_signal(barrier, 1, device_id=(lax.rem(z + k, n_dp), f), device_id_type=MESH)
    for k in range(1, half):
        pl.semaphore_signal(barrier, 1, device_id=(z, lax.rem(f + 2 * k, n_f)), device_id_type=MESH)
    pl.semaphore_signal(barrier, 1, device_id=(z, partner), device_id_type=MESH)
    local = pltpu.make_async_copy(own_ref, out_ref.at[z, f], l_sem)
    local.start()
    pl.semaphore_wait(barrier, n_dp - 1 + half)

    chunks = column_chunks(own_ref.shape[1])
    z_copies, p_copies, c_copies = [], [], []

    def send_z(c):
        for k in range(1, n_dp):
            copy = pltpu.make_async_remote_copy(
                own_ref.at[:, chunks[c]], out_ref.at[z, f, :, chunks[c]],
                z_send.at[c, k], z_recv.at[c, k],
                device_id=(lax.rem(z + k, n_dp), f), device_id_type=MESH,
            )
            copy.start()
            z_copies.append(copy)

    def send_p(c):
        for k in range(1, n_dp):
            z_copies[c * (n_dp - 1) + k - 1].wait_recv()
        for k in range(1, half):
            copy = pltpu.make_async_remote_copy(
                out_ref.at[:, f, :, chunks[c]], out_ref.at[:, f, :, chunks[c]],
                p_send.at[c, k], p_recv.at[c, k],
                device_id=(z, lax.rem(f + 2 * k, n_f)), device_id_type=MESH,
            )
            copy.start()
            p_copies.append(copy)

    def send_c(c):
        for k in range(half):
            if k:
                p_copies[c * (half - 1) + k - 1].wait_recv()
            column = lax.rem(f + n_f - 2 * k, n_f)
            copy = pltpu.make_async_remote_copy(
                out_ref.at[:, column, :, chunks[c]], out_ref.at[:, column, :, chunks[c]],
                c_send.at[c, k], c_recv.at[c, k],
                device_id=(z, partner), device_id_type=MESH,
            )
            copy.start()
            c_copies.append(copy)

    def fill(block, carry):
        start = pl.multiple_of(block * BLOCK, BLOCK)
        slots_ref[pl.ds(start, BLOCK), :] = dispatch_block(row_ref, rows_ref[...], start, BLOCK)
        return carry

    n_blocks = slots_ref.shape[0] // BLOCK
    for c in range(len(chunks)):
        send_z(c)
    number_slots(cap, ids_ref, col_ref, row_ref)
    n_long = long_ref.shape[0]
    rows_ref[:n_long, :] = long_ref[...].astype(BF16)
    rows_ref[n_long:, :] = short_ref[...].astype(BF16)
    local.wait()
    for c in range(len(chunks)):
        send_p(c)
        lax.fori_loop(c * n_blocks // len(chunks), (c + 1) * n_blocks // len(chunks), fill, 0)
    for c in range(len(chunks)):
        send_c(c)
    for copy in c_copies:
        copy.wait_recv()
    for copy in z_copies + p_copies + c_copies:
        copy.wait_send()


def gather_dense(own, ids, long_cot, short_cot, n_dp, n_f, cap, slots):
    count, width = ids.shape[0], long_cot.shape[1]
    vmem = pl.BlockSpec(memory_space=pltpu.VMEM)
    return pl.pallas_call(
        functools.partial(gather_kernel, n_dp, n_f, cap),
        out_shape=[
            jax.ShapeDtypeStruct((n_dp, n_f) + own.shape, own.dtype),
            jax.ShapeDtypeStruct((count, 1), jnp.int32),
            jax.ShapeDtypeStruct((8, count), jnp.int32),
            jax.ShapeDtypeStruct((slots, width), BF16),
        ],
        in_specs=[pl.BlockSpec(memory_space=pl.ANY), vmem, vmem, vmem],
        out_specs=[pl.BlockSpec(memory_space=pl.ANY), vmem, vmem, vmem],
        scratch_shapes=[
            pltpu.VMEM((count, width), BF16),
            pltpu.SemaphoreType.DMA((N_CHUNKS, n_dp)),
            pltpu.SemaphoreType.DMA((N_CHUNKS, n_dp)),
            pltpu.SemaphoreType.DMA((N_CHUNKS, n_f // 2)),
            pltpu.SemaphoreType.DMA((N_CHUNKS, n_f // 2)),
            pltpu.SemaphoreType.DMA((N_CHUNKS, n_f // 2)),
            pltpu.SemaphoreType.DMA((N_CHUNKS, n_f // 2)),
            pltpu.SemaphoreType.DMA,
        ],
        compiler_params=params(collective_id=0, has_side_effects=True),
        cost_estimate=cost(0, 100e6),
        name="gather_dense",
    )(own, ids, long_cot, short_cot)


def dispatch_block(slot_row_ref, rows, first, size):
    slot_id = first + lax.broadcasted_iota(jnp.int32, (size, 1), 0)
    chosen = (slot_row_ref[0:1, :] == slot_id).astype(F32).astype(BF16)
    return dot(chosen, rows).astype(BF16)


def number_slots(cap, ids_ref, col_ref, row_ref):
    count = ids_ref.shape[0]
    lane = lax.broadcasted_iota(jnp.int32, (1, LANES), 1)
    onehot = (ids_ref[...] == lane).astype(F32)
    onehot_low = onehot.astype(BF16)
    col = lax.broadcasted_iota(jnp.int32, (1, count), 1)
    base = (lane * cap).astype(F32)
    ones = jnp.ones((8, LANES), F32)
    for start in range(0, count, ROWS):
        row = start + lax.broadcasted_iota(jnp.int32, (ROWS, 1), 0)
        before = dot((col < row).astype(F32).astype(BF16), onehot_low)
        picked = (before + base) * onehot[start : start + ROWS]
        col_ref[start : start + ROWS, :] = jnp.sum(picked, 1, keepdims=True).astype(jnp.int32)
        row_ref[:, start : start + ROWS] = dot(
            ones, picked, NT, precision=lax.Precision.HIGHEST
        ).astype(jnp.int32)


def peers(n_f):
    f = lax.axis_index("fsdp")
    half = n_f // 2
    chip, core = f // 2, lax.rem(f, 2)

    def to(k):
        return lax.rem(chip + k // 2, half) * 2 + lax.rem(core + lax.rem(k, 2), 2)

    def source(k):
        return lax.rem(chip + half - k // 2, half) * 2 + lax.rem(core + lax.rem(k, 2), 2)

    return f, to, source


def greet(n_f, to):
    z = lax.axis_index("dp")
    barrier = pltpu.get_barrier_semaphore()
    for k in range(1, n_f):
        pl.semaphore_signal(barrier, 1, device_id=(z, to(k)), device_id_type=MESH)


def qkv_kernel(n_long, width, long_ref, short_ref, w_ref, vec_ref, qkv_ref, vec_scr):
    i = pl.program_id(0)

    @pl.when(i == 0)
    def _():
        vec_scr[...] = vectors(vec_ref)

    def body(x_ref):
        normed, _ = norm_parts(x_ref[...])
        rows = (normed * vec_scr[0:1, :] + vec_scr[1:2, :]).astype(BF16)
        for part in range(3):
            cut = slice(part * width, (part + 1) * width)
            out = dot(rows, w_ref[:, cut])
            if part == 0:
                out = out * HEAD_DIM ** (-0.5)
            qkv_ref[:, cut] = out.astype(BF16)

    pl.when(i < n_long)(lambda: body(long_ref))
    pl.when(i >= n_long)(lambda: body(short_ref))


def make_qkv(long_x, short_x, dense):
    width = long_x.shape[1]
    n_long, n_short = long_x.shape[0] // ROWS, short_x.shape[0] // ROWS
    count = long_x.shape[0] + short_x.shape[0]
    return pl.pallas_call(
        functools.partial(qkv_kernel, n_long, width),
        grid=(n_long + n_short,),
        in_specs=long_short(width, n_long)
        + [
            constant((width, 3 * width)),
            pl.BlockSpec((width, LANES), lambda i: (0, 4 * width // LANES)),
        ],
        out_specs=pl.BlockSpec((ROWS, 3 * width), lambda i: (i, 0)),
        out_shape=jax.ShapeDtypeStruct((count, 3 * width), BF16),
        scratch_shapes=[pltpu.VMEM((8, width), F32)],
        compiler_params=params(),
        cost_estimate=cost(6 * count * width * width, count * width * 10 + 6 * width * width),
        name="make_qkv",
    )(long_x, short_x, dense, dense)


def sequences(long_shape, short_shape):
    found = []
    start = 0
    for which, (number, length) in enumerate((long_shape, short_shape)):
        for index in range(number):
            found.append((start, length, which, index))
            start += length
    return found


def head_masks():
    lane = lax.broadcasted_iota(jnp.int32, (1, LANES), 1)
    return (lane < HEAD_DIM, lane >= HEAD_DIM)


def marked(q, k, valid, first, masks, lane):
    key_pos = first + lax.broadcasted_iota(jnp.int32, (k.shape[0], 1), 0)
    bias = jnp.where(key_pos < valid, 0.0, MASKED).astype(BF16)
    found = []
    for head in range(2):
        spare = HEAD_DIM * (1 - head)
        qh = jnp.where(masks[head], q, jnp.where(lane == spare, 1.0, 0.0).astype(BF16))
        kh = jnp.where(masks[head], k, jnp.where(lane == spare, bias, jnp.zeros_like(bias)))
        found.append((qh, kh))
    return found


def attend_kernel(seqs, long_len, short_len, q_ref, k_ref, v_ref, o_ref, lse_ref):
    pair = pl.program_id(0)
    masks = head_masks()
    lane = lax.broadcasted_iota(jnp.int32, (1, LANES), 1)

    @pl.when(pair == 0)
    def _():
        lse_ref[...] = jnp.zeros_like(lse_ref)

    causal = lax.broadcasted_iota(jnp.int32, (ATTEND, ATTEND), 0) <= lax.broadcasted_iota(
        jnp.int32, (ATTEND, ATTEND), 1
    )
    upper = lax.broadcasted_iota(jnp.int32, (LANES, 1), 0) < HEAD_DIM
    for start, length, which, index in seqs:
        valid = (short_len if which else long_len)[index]
        rows = slice(start, start + length)
        heads = marked(q_ref[rows, :], k_ref[rows, :], valid, 0, masks, lane)
        v = jnp.transpose(v_ref[rows, :].astype(F32))
        values = [
            jnp.where(upper, v, 1.0).astype(BF16),
            jnp.where(upper, 1.0, v).astype(BF16),
        ]
        for first in range(0, length, ATTEND):
            last = first + ATTEND
            outs = []
            for head, (qh, kh) in enumerate(heads):
                qb = qh[first:last]
                near = dot(kh[first:last], qb, NT)
                near = jnp.where(causal, near, MASKED)
                top = jnp.max(near, 0, keepdims=True)
                if first:
                    far = dot(kh[:first], qb, NT)
                    top = jnp.maximum(top, jnp.max(far, 0, keepdims=True))
                out = dot(values[head][:, first:last], jnp.exp(near - top).astype(BF16))
                if first:
                    out = out + dot(values[head][:, :first], jnp.exp(far - top).astype(BF16))
                total = out[LANES - 1 : LANES] if head == 0 else out[0:1]
                outs.append(out * (1.0 / total))
                lse_ref[pl.ds(2 * pair + head, 1), start + first : start + last] = top + jnp.log(
                    total
                )
            o_ref[start + first : start + last, :] = jnp.transpose(
                jnp.where(upper, outs[0], outs[1])
            ).astype(BF16)


def attend(qkv, long_len, short_len, seqs):
    count, width = qkv.shape[0], qkv.shape[1] // 3
    pairs = width // LANES
    return pl.pallas_call(
        functools.partial(attend_kernel, seqs),
        grid=(pairs,),
        in_specs=[pl.BlockSpec(memory_space=pltpu.SMEM)] * 2
        + [
            pl.BlockSpec((count, LANES), lambda i: (0, i)),
            pl.BlockSpec((count, LANES), lambda i: (0, i + pairs)),
            pl.BlockSpec((count, LANES), lambda i: (0, i + 2 * pairs)),
        ],
        out_specs=[
            pl.BlockSpec((count, LANES), lambda i: (0, i)),
            pl.BlockSpec((LANES, count), lambda i: (0, 0)),
        ],
        out_shape=[
            jax.ShapeDtypeStruct((count, width), BF16),
            jax.ShapeDtypeStruct((LANES, count), F32),
        ],
        compiler_params=params(),
        cost_estimate=cost(16e9, 8 * count * width, 10e6),
        name="attend",
    )(long_len, short_len, qkv, qkv, qkv)


def attend_back_kernel(
    seqs, long_len, short_len, q_ref, k_ref, v_ref, o_ref, do_ref, lse_ref,
    d_ref, dkt_ref, dvt_ref, lse_scr,
):
    pair = pl.program_id(0)
    masks = head_masks()
    lane = lax.broadcasted_iota(jnp.int32, (1, LANES), 1)

    @pl.when(pair == 0)
    def _():
        lse_scr[...] = jnp.transpose(lse_ref[...])

    causal = lax.broadcasted_iota(jnp.int32, (ATTEND_BACK, ATTEND_BACK), 1) <= (
        lax.broadcasted_iota(jnp.int32, (ATTEND_BACK, ATTEND_BACK), 0)
    )
    for start, length, which, index in seqs:
        valid = (short_len if which else long_len)[index]
        rows = slice(start, start + length)
        q, k, v, do = q_ref[rows, :], k_ref[rows, :], v_ref[rows, :], do_ref[rows, :]
        heads = marked(q, k, valid, 0, masks, lane)
        q_t = jnp.transpose(q.astype(F32)).astype(BF16)
        do_t = jnp.transpose(do.astype(F32)).astype(BF16)
        both = do.astype(F32) * o_ref[rows, :].astype(F32)
        lse_all = lse_scr[rows, :]
        dkt_ref[...] = jnp.zeros_like(dkt_ref)
        dvt_ref[...] = jnp.zeros_like(dvt_ref)
        for first in range(0, length, ATTEND_BACK):
            last = first + ATTEND_BACK
            dqs = []
            for head, (qh, kh) in enumerate(heads):
                part = slice(HEAD_DIM * head, HEAD_DIM * (head + 1))
                doh = jnp.where(masks[head], do[first:last], jnp.zeros_like(do[first:last]))
                lse = jnp.sum(
                    jnp.where(lane == 2 * pair + head, lse_all[first:last], 0.0), 1, keepdims=True
                )
                delta = jnp.sum(jnp.where(masks[head], both[first:last], 0.0), 1, keepdims=True)
                dq = jnp.zeros((ATTEND_BACK, LANES), F32)
                for keys in (slice(0, first), slice(first, last)):
                    if keys.stop == keys.start:
                        continue
                    p = jnp.exp(dot(qh[first:last], kh[keys], NT) - lse)
                    if keys.start == first:
                        p = jnp.where(causal, p, 0.0)
                    dp = dot(doh, v[keys], NT)
                    ds = (p * (dp - delta)).astype(BF16)
                    dvt_ref[part, keys] = dvt_ref[part, keys] + dot(
                        do_t[part, first:last], p.astype(BF16)
                    )
                    dkt_ref[part, keys] = dkt_ref[part, keys] + dot(q_t[part, first:last], ds)
                    dq = dq + dot(ds, k[keys])
                dqs.append(dq)
            d_ref[0, start + first : start + last, :] = (
                jnp.where(masks[0], dqs[0], dqs[1]) * HEAD_DIM ** (-0.5)
            ).astype(BF16)
        d_ref[1, rows, :] = jnp.transpose(dkt_ref[:, :length]).astype(BF16)
        d_ref[2, rows, :] = jnp.transpose(dvt_ref[:, :length]).astype(BF16)


def attend_back(qkv, o, d_o, lse, long_len, short_len, seqs):
    count, width = o.shape
    pairs = width // LANES
    longest = max(length for _, length, _, _ in seqs)
    one = pl.BlockSpec((count, LANES), lambda i: (0, i))
    return pl.pallas_call(
        functools.partial(attend_back_kernel, seqs),
        grid=(pairs,),
        in_specs=[pl.BlockSpec(memory_space=pltpu.SMEM)] * 2
        + [
            one,
            pl.BlockSpec((count, LANES), lambda i: (0, i + pairs)),
            pl.BlockSpec((count, LANES), lambda i: (0, i + 2 * pairs)),
            one,
            one,
            constant((LANES, count)),
        ],
        out_specs=pl.BlockSpec((3, count, LANES), lambda i: (0, 0, i)),
        out_shape=jax.ShapeDtypeStruct((3, count, width), BF16),
        scratch_shapes=[
            pltpu.VMEM((LANES, longest), F32),
            pltpu.VMEM((LANES, longest), F32),
            pltpu.VMEM((count, LANES), F32),
        ],
        compiler_params=params(),
        cost_estimate=cost(40e9, 16 * count * width, 10e6),
        name="attend_back",
    )(long_len, short_len, qkv, qkv, qkv, o, d_o, lse)


def gelu_parts(pre):
    scale = 0.7978845608028654
    square = pre * pre
    flat = jnp.tanh(scale * pre * (1.0 + 0.044715 * square))
    half = 0.5 * (1.0 + flat)
    slope = half + (0.5 * scale) * pre * (1.0 - flat * flat) * (1.0 + 0.134145 * square)
    return half * pre, slope


def forward_kernel(
    n_f, n_long, n_rows, long_ref, short_ref, o_ref, w_ref, vec_ref, row_ref, g_ref, up_ref,
    h_ref, there_ref, act_ref, slope_ref, gd_ref,
    rows_ref, vec_scr, out_buf, in_buf, all_ref, send, recv,
):
    i = pl.program_id(0)
    z = lax.axis_index("dp")
    f, to, source = peers(n_f)
    cap, width = out_buf.shape[1:]
    n_up = n_rows + n_f
    n_down = n_up + n_f
    barrier = pltpu.get_barrier_semaphore()

    def transfer(k):
        return pltpu.make_async_remote_copy(
            out_buf.at[k], in_buf.at[f], send.at[k], recv.at[k],
            device_id=(z, to(k)), device_id_type=MESH,
        )

    @pl.when(i == 0)
    def _():
        greet(n_f, to)
        vec_scr[...] = vectors(vec_ref)

    def body(x_ref):
        hidden = x_ref[...] + dot(o_ref[...], w_ref[...], NT)
        h_ref[...] = hidden
        normed, _ = norm_parts(hidden)
        rows_ref[pl.ds(pl.multiple_of(i * ROWS, ROWS), ROWS), :] = (
            normed * vec_scr[2:3, :] + vec_scr[3:4, :]
        ).astype(BF16)

    pl.when(i < n_long)(lambda: body(long_ref))
    pl.when((i >= n_long) & (i < n_rows))(lambda: body(short_ref))

    @pl.when(i == n_rows)
    def _():
        pl.semaphore_wait(barrier, n_f - 1)

    @pl.when((i >= n_rows) & (i < n_up - 1))
    def _():
        k = i - n_rows + 1
        out_buf[k] = dispatch_block(row_ref, rows_ref[...], to(k) * cap, cap)
        transfer(k).start()

    @pl.when(i == n_up - 1)
    def _():
        in_buf[f] = dispatch_block(row_ref, rows_ref[...], f * cap, cap)

    @pl.when((i > n_up) & (i < n_down))
    def _():
        transfer(i - n_up).wait_recv()

    @pl.when((i >= n_up) & (i < n_down))
    def _():
        origin = source(i - n_up)
        rows = in_buf[origin]
        here = pl.ds(pl.multiple_of(origin * cap, cap), cap)
        for first in range(0, up_ref.shape[1], width):
            cut = slice(first, first + width)
            act, slope = gelu_parts(dot(rows, up_ref[:, cut]))
            act = act.astype(BF16)
            act_ref[:, cut] = act
            slope_ref[:, cut] = slope.astype(BF16)
            all_ref[here, cut] = act
        there_ref[here, :] = rows

    @pl.when(i >= n_down)
    def _():
        cut = pl.ds(pl.multiple_of((i - n_down) * width, width), width)
        gd_ref[...] = dot(all_ref[:, cut], g_ref[...], TN).astype(BF16)

    @pl.when(i == pl.num_programs(0) - 1)
    def _():
        for k in range(1, n_f):
            transfer(k).wait_send()


def forward_experts(long_x, short_x, o, dense, slot_row, g_there, up, n_f, cap):
    width = long_x.shape[1]
    hidden = up.shape[1]
    n_long, n_short = long_x.shape[0] // ROWS, short_x.shape[0] // ROWS
    n_rows = n_long + n_short
    n_up = n_rows + n_f
    n_down = n_up + n_f
    n_hidden = hidden // width
    slots = n_f * cap
    count = o.shape[0]
    tile = pl.BlockSpec((cap, hidden), lambda i: (jnp.clip(i - n_up, 0, n_f - 1), 0))
    return pl.pallas_call(
        functools.partial(forward_kernel, n_f, n_long, n_rows),
        grid=(n_down + n_hidden,),
        in_specs=[
            pl.BlockSpec((ROWS, width), lambda i: (jnp.minimum(i, n_long - 1), 0)),
            pl.BlockSpec((ROWS, width), lambda i: (jnp.clip(i - n_long, 0, n_short - 1), 0)),
            pl.BlockSpec((ROWS, width), lambda i: (jnp.minimum(i, n_rows - 1), 0)),
            pl.BlockSpec((width, width), lambda i: (0, 3), pipeline_mode=pl.Buffered(1)),
            pl.BlockSpec((width, LANES), lambda i: (0, 4 * width // LANES)),
            constant((8, count)),
            constant((slots, width)),
            constant((width, hidden)),
        ],
        out_specs=[
            pl.BlockSpec((ROWS, width), lambda i: (jnp.minimum(i, n_rows - 1), 0)),
            pl.BlockSpec((slots, width), lambda i: (0, 0)),
            tile,
            tile,
            pl.BlockSpec((width, width), lambda i: (jnp.clip(i - n_down, 0, n_hidden - 1), 0)),
        ],
        out_shape=[
            jax.ShapeDtypeStruct((count, width), F32),
            jax.ShapeDtypeStruct((slots, width), BF16),
            jax.ShapeDtypeStruct((slots, hidden), BF16),
            jax.ShapeDtypeStruct((slots, hidden), BF16),
            jax.ShapeDtypeStruct((hidden, width), BF16),
        ],
        scratch_shapes=[
            pltpu.VMEM((count, width), BF16),
            pltpu.VMEM((8, width), F32),
            pltpu.VMEM((n_f, cap, width), BF16),
            pltpu.VMEM((n_f, cap, width), BF16),
            pltpu.VMEM((slots, hidden), BF16),
            pltpu.SemaphoreType.DMA((n_f,)),
            pltpu.SemaphoreType.DMA((n_f,)),
        ],
        compiler_params=params(collective_id=2, has_side_effects=True),
        cost_estimate=cost(
            2 * slots * width * (count + 2 * hidden), 60e6, slots * hidden
        ),
        name="forward_experts",
    )(long_x, short_x, o, dense, dense, slot_row, g_there, up)


def own_kernel(
    n_f, z_ref, b_ref, g_ref, act_ref, slope_ref, up_ref, down_ref, y_ref, db_ref, gu_ref, all_ref
):
    i = pl.program_id(0)
    _, _, source = peers(n_f)
    cap = y_ref.shape[0]

    @pl.when(i < n_f)
    def _():
        here = pl.ds(pl.multiple_of(source(i) * cap, cap), cap)
        d_act = dot(g_ref[here, :], down_ref[...], NT)
        d_pre = (d_act * slope_ref[...].astype(F32)).astype(BF16)
        all_ref[here, :] = d_pre
        db_ref[...] = dot(d_pre, up_ref[...], NT)
        y_ref[...] = dot(act_ref[...], down_ref[...])

    @pl.when(i >= n_f)
    def _():
        gu_ref[...] = dot(b_ref[...], all_ref[...], TN).astype(BF16)


def own_experts(z, b_there, g_there, act, slope, up, own_down, n_f, cap):
    slots, width = b_there.shape
    piece = own_down.shape[0]
    tile = pl.BlockSpec((cap, piece), lambda i, z: (jnp.minimum(i, n_f - 1), z[0]))
    out = pl.BlockSpec((cap, width), lambda i, z: (jnp.minimum(i, n_f - 1), 0))
    return pl.pallas_call(
        functools.partial(own_kernel, n_f),
        grid_spec=pltpu.PrefetchScalarGridSpec(
            num_scalar_prefetch=1,
            grid=(n_f + 1,),
            in_specs=[
                constant((slots, width)),
                constant((slots, width)),
                tile,
                tile,
                pl.BlockSpec((width, piece), lambda i, z: (0, z[0])),
                constant((piece, width)),
            ],
            out_specs=[out, out, pl.BlockSpec((width, piece), lambda i, z: (0, 0))],
            scratch_shapes=[pltpu.VMEM((slots, piece), BF16)],
        ),
        out_shape=[
            jax.ShapeDtypeStruct((slots, width), F32),
            jax.ShapeDtypeStruct((slots, width), F32),
            jax.ShapeDtypeStruct((width, piece), BF16),
        ],
        compiler_params=params(),
        cost_estimate=cost(8 * slots * width * piece, 30e6),
        name="own_experts",
    )(z, b_there, g_there, act, slope, up, own_down)


def back_kernel(
    n_dp, n_f, b_ref, g_ref, act_ref, slope_ref, up_ref, down_ref, y0_ref, db0_ref, gu0_ref,
    y_ref, db_ref, gu_ref, out_buf, all_ref, send, recv, l_sem,
):
    i = pl.program_id(0)
    z = lax.axis_index("dp")
    f, to, source = peers(n_f)
    cap, width = out_buf.shape[1:]
    piece = gu_ref.shape[1]
    barrier = pltpu.get_barrier_semaphore()

    def transfer(k):
        return pltpu.make_async_remote_copy(
            out_buf.at[k], db_ref.at[f], send.at[k], recv.at[k],
            device_id=(z, source(k)), device_id_type=MESH,
        )

    def other(m):
        return pl.ds(pl.multiple_of(lax.rem(z + m, n_dp) * piece, piece), piece)

    keep = pltpu.make_async_copy(out_buf.at[0], db_ref.at[f], l_sem)

    @pl.when(i == 0)
    def _():
        greet(n_f, to)

    @pl.when(i < n_f)
    def _():
        k = n_f - 1 - i
        here = pl.ds(pl.multiple_of(source(k) * cap, cap), cap)
        g = g_ref[here, :]
        d_b = db0_ref[...]
        for m in range(1, n_dp):
            d_act = dot(g, down_ref[other(m), :], NT)
            d_pre = (d_act * slope_ref[:, other(m)].astype(F32)).astype(BF16)
            all_ref[here, other(m)] = d_pre
            d_b = d_b + dot(d_pre, up_ref[:, other(m)], NT)
        out_buf[k] = d_b.astype(BF16)

    @pl.when(i == 0)
    def _():
        pl.semaphore_wait(barrier, n_f - 1)

    @pl.when(i < n_f - 1)
    def _():
        transfer(n_f - 1 - i).start()

    @pl.when(i == n_f - 1)
    def _():
        keep.start()

    @pl.when(i < n_f)
    def _():
        here = pl.ds(pl.multiple_of(source(n_f - 1 - i) * cap, cap), cap)
        y = y0_ref[...]
        for m in range(1, n_dp):
            y = y + dot(act_ref[:, other(m)], down_ref[other(m), :])
        y_ref[here, :] = y.astype(BF16)

    @pl.when((i >= n_f) & (i - n_f == z))
    def _():
        gu_ref[...] = gu0_ref[...]

    @pl.when((i >= n_f) & (i - n_f != z))
    def _():
        cut = pl.ds(pl.multiple_of((i - n_f) * piece, piece), piece)
        gu_ref[...] = dot(b_ref[...], all_ref[:, cut], TN).astype(BF16)

    @pl.when(i == pl.num_programs(0) - 1)
    def _():
        keep.wait()
        for k in range(1, n_f):
            transfer(k).wait_recv()
        for k in range(1, n_f):
            transfer(k).wait_send()


def back_experts(b_there, g_there, act, slope, up, down, y0, db0, gu0, n_dp, n_f, cap):
    slots, width = b_there.shape
    hidden = up.shape[1]
    piece = hidden // n_dp
    tile = pl.BlockSpec((cap, hidden), lambda i: (jnp.maximum(n_f - 1 - i, 0), 0))
    begun = pl.BlockSpec((cap, width), lambda i: (jnp.maximum(n_f - 1 - i, 0), 0))
    return pl.pallas_call(
        functools.partial(back_kernel, n_dp, n_f),
        grid=(n_f + n_dp,),
        in_specs=[
            constant((slots, width)),
            constant((slots, width)),
            tile,
            tile,
            constant((width, hidden)),
            constant((hidden, width)),
            begun,
            begun,
            constant((width, piece)),
        ],
        out_specs=[
            pl.BlockSpec((slots, width), lambda i: (0, 0)),
            pl.BlockSpec(memory_space=pl.ANY),
            pl.BlockSpec((width, piece), lambda i: (0, jnp.maximum(i - n_f, 0))),
        ],
        out_shape=[
            jax.ShapeDtypeStruct((slots, width), BF16),
            jax.ShapeDtypeStruct((n_f, cap, width), BF16),
            jax.ShapeDtypeStruct((width, hidden), BF16),
        ],
        scratch_shapes=[
            pltpu.VMEM((n_f, cap, width), BF16),
            pltpu.VMEM((slots, hidden), BF16),
            pltpu.SemaphoreType.DMA((n_f,)),
            pltpu.SemaphoreType.DMA((n_f,)),
            pltpu.SemaphoreType.DMA,
        ],
        compiler_params=params(collective_id=3, has_side_effects=True),
        cost_estimate=cost(6 * slots * width * hidden, 60e6),
        name="back_experts",
    )(b_there, g_there, act, slope, up, down, y0, db0, gu0)


def combine_rows(col_ref, slots_ref):
    slot_id = lax.broadcasted_iota(jnp.int32, (1, slots_ref.shape[0]), 1)
    chosen = (col_ref[...] == slot_id).astype(F32).astype(BF16)
    return dot(chosen, slots_ref[...])


def hidden_back_kernel(
    n_long, n_rows, h_ref, col_ref, db_ref, long_ref, short_ref, o_ref, w_ref, vec_ref,
    dh_ref, do_ref, gp_ref, gv_ref, acc_ref, vec_scr,
):
    i = pl.program_id(0)

    @pl.when(i == 0)
    def _():
        vec_scr[...] = vectors(vec_ref)
        acc_ref[...] = jnp.zeros_like(acc_ref)
        gv_ref[...] = jnp.zeros_like(gv_ref)

    def body(cot_ref):
        d_b = combine_rows(col_ref, db_ref)
        normed, inv_scale = norm_parts(h_ref[...])
        gv_ref[2:3, :] = gv_ref[2:3, :] + jnp.sum(d_b * normed, 0, keepdims=True)
        gv_ref[3:4, :] = gv_ref[3:4, :] + jnp.sum(d_b, 0, keepdims=True)
        d_h = cot_ref[...] + norm_back(d_b * vec_scr[2:3, :], normed, inv_scale)
        dh_ref[...] = d_h
        d_attn = d_h.astype(BF16)
        do_ref[...] = dot(d_attn, w_ref[...]).astype(BF16)
        acc_ref[...] = acc_ref[...] + dot(d_attn, o_ref[...], TN)

    pl.when(i < n_long)(lambda: body(long_ref))
    pl.when(i >= n_long)(lambda: body(short_ref))

    @pl.when(i == n_rows - 1)
    def _():
        gp_ref[...] = acc_ref[...].astype(BF16)


def hidden_back(h, slot_col, db_back, long_cot, short_cot, o, dense):
    count, width = h.shape
    slots = db_back.shape[0]
    n_long, n_short = long_cot.shape[0] // ROWS, short_cot.shape[0] // ROWS
    n_rows = n_long + n_short
    row = pl.BlockSpec((ROWS, width), lambda i: (i, 0))
    return pl.pallas_call(
        functools.partial(hidden_back_kernel, n_long, n_rows),
        grid=(n_rows,),
        in_specs=[row, pl.BlockSpec((ROWS, 1), lambda i: (i, 0)), constant((slots, width))]
        + long_short(width, n_long)
        + [
            row,
            pl.BlockSpec((width, width), lambda i: (0, 3)),
            pl.BlockSpec((width, LANES), lambda i: (0, 4 * width // LANES)),
        ],
        out_specs=[
            row,
            row,
            pl.BlockSpec((width, width), lambda i: (0, 0)),
            pl.BlockSpec((LANES, width), lambda i: (0, 0)),
        ],
        out_shape=[
            jax.ShapeDtypeStruct((count, width), F32),
            jax.ShapeDtypeStruct((count, width), BF16),
            jax.ShapeDtypeStruct((width, width), BF16),
            jax.ShapeDtypeStruct((LANES, width), F32),
        ],
        scratch_shapes=[pltpu.VMEM((width, width), F32), pltpu.VMEM((8, width), F32)],
        compiler_params=params(),
        cost_estimate=cost(2 * (slots + 2 * width) * count * width, 16 * count * width),
        name="hidden_back",
    )(h, slot_col, db_back, long_cot, short_cot, o, dense, dense)


def grads_kernel(
    n_long, n_rows, width, long_ref, short_ref, d_ref, w_ref, vec_ref, gp_ref, gv_ref,
    out_ref, acc_ref, vec_scr, sum_scr,
):
    i = pl.program_id(0)

    @pl.when(i == 0)
    def _():
        vec_scr[...] = vectors(vec_ref)
        acc_ref[...] = jnp.zeros_like(acc_ref)
        sum_scr[...] = jnp.zeros_like(sum_scr)

    def body(x_ref):
        normed, _ = norm_parts(x_ref[...])
        rows = (normed * vec_scr[0:1, :] + vec_scr[1:2, :]).astype(BF16)
        for part in range(3):
            cut = slice(part * width, (part + 1) * width)
            acc_ref[:, cut] = acc_ref[:, cut] + dot(rows, d_ref[part], TN)
            sum_scr[:, cut] = sum_scr[:, cut] + jnp.sum(
                d_ref[part].astype(F32), 0, keepdims=True
            )

    pl.when(i < n_long)(lambda: body(long_ref))
    pl.when(i >= n_long)(lambda: body(short_ref))

    @pl.when(i == n_rows - 1)
    def _():
        out_ref[:, :width] = gp_ref[...]
        out_ref[:, width : 4 * width] = acc_ref[...].astype(BF16)
        weighted = jnp.zeros((width, 1), F32)
        bias_grad = jnp.zeros((width, 1), F32)
        for part in range(3):
            cut = slice(part * width, (part + 1) * width)
            weight = w_ref[:, cut].astype(F32)
            weighted = weighted + jnp.sum(weight * acc_ref[:, cut], 1, keepdims=True)
            bias_grad = bias_grad + jnp.sum(weight * sum_scr[:, cut], 1, keepdims=True)
        out_ref[:, 4 * width :] = norm1_grads(weighted, bias_grad, vec_ref, gv_ref)


def dense_grads(long_x, short_x, d_qkv, dense, grad_proj, grad_vec):
    count, width = d_qkv.shape[1:]
    n_long, n_short = long_x.shape[0] // ROWS, short_x.shape[0] // ROWS
    n_rows = n_long + n_short
    return pl.pallas_call(
        functools.partial(grads_kernel, n_long, n_rows, width),
        grid=(n_rows,),
        in_specs=long_short(width, n_long)
        + [
            pl.BlockSpec((3, ROWS, width), lambda i: (0, i, 0)),
            constant((width, 3 * width)),
            pl.BlockSpec((width, LANES), lambda i: (0, 4 * width // LANES)),
            constant((width, width)),
            constant((LANES, width)),
        ],
        out_specs=pl.BlockSpec((width, 4 * width + LANES), lambda i: (0, 0)),
        out_shape=jax.ShapeDtypeStruct((width, 4 * width + LANES), BF16),
        scratch_shapes=[
            pltpu.VMEM((width, 3 * width), F32),
            pltpu.VMEM((8, width), F32),
            pltpu.VMEM((1, 3 * width), F32),
        ],
        compiler_params=params(),
        cost_estimate=cost(6 * count * width * width, 16 * count * width),
        name="dense_grads",
    )(long_x, short_x, d_qkv, dense, dense, grad_proj, grad_vec)


class Reducer:
    def __init__(self, part_ref, out_ref, chunks, scratch):
        self.part, self.out, self.chunks = part_ref, out_ref, chunks
        self.got1, self.sum1, self.got2, self.sum2, self.got3 = scratch[:5]
        self.sems = scratch[5:]
        self.n_dp, self.n_f = part_ref.shape[:2]
        self.z = lax.axis_index("dp")
        self.f = lax.axis_index("fsdp")
        self.half = self.n_f // 2
        self.parity = lax.rem(self.f, 2)
        self.mine = self.f // 2
        self.partner = self.f + 1 - 2 * self.parity
        self.order = list(range(1, self.half)) + [0]
        self.barrier = pltpu.get_barrier_semaphore()

    def greet(self):
        z, f = self.z, self.f
        for k in range(1, self.n_dp):
            pl.semaphore_signal(
                self.barrier, 1, device_id=(lax.rem(z + k, self.n_dp), f), device_id_type=MESH
            )
        for k in range(1, self.half):
            pl.semaphore_signal(
                self.barrier, 1, device_id=(z, lax.rem(f + 2 * k, self.n_f)), device_id_type=MESH
            )
        pl.semaphore_signal(self.barrier, 1, device_id=(z, self.partner), device_id_type=MESH)

    def meet(self):
        pl.semaphore_wait(self.barrier, self.n_dp - 1 + self.half)

    def slot(self, k):
        return lax.rem(self.mine + k, self.half)

    def core_copy(self, c, k):
        cut, slot = self.chunks[c], self.slot(k)
        return pltpu.make_async_remote_copy(
            self.part.at[:, 2 * slot + 1 - self.parity, :, cut], self.got1.at[slot, :, :, cut],
            self.sems[0].at[c, k], self.sems[1].at[c, k],
            device_id=(self.z, self.partner), device_id_type=MESH,
        )

    def chip_copy(self, c, k):
        cut = self.chunks[c]
        return pltpu.make_async_remote_copy(
            self.sum1.at[self.slot(k), :, :, cut], self.got2.at[k, :, :, cut],
            self.sems[2].at[c, k], self.sems[3].at[c, k],
            device_id=(self.z, lax.rem(self.f + 2 * k, self.n_f)), device_id_type=MESH,
        )

    def plane_copy(self, c, k):
        cut, there = self.chunks[c], lax.rem(self.z + k, self.n_dp)
        return pltpu.make_async_remote_copy(
            self.sum2.at[there, :, cut], self.got3.at[k, :, cut],
            self.sems[4].at[c, k], self.sems[5].at[c, k],
            device_id=(there, self.f), device_id_type=MESH,
        )

    def start_core(self, c):
        for k in self.order:
            self.core_copy(c, k).start()

    def start_chip(self, c):
        cut = self.chunks[c]
        for k in self.order:
            slot = self.slot(k)
            self.core_copy(c, k).wait_recv()
            self.sum1[slot, :, :, cut] = (
                self.part[:, 2 * slot + self.parity, :, cut].astype(F32)
                + self.got1[slot, :, :, cut].astype(F32)
            ).astype(BF16)
            if k:
                self.chip_copy(c, k).start()

    def start_plane(self, c):
        cut = self.chunks[c]
        total = self.sum1[self.mine, :, :, cut].astype(F32)
        for k in range(1, self.half):
            self.chip_copy(c, k).wait_recv()
            total = total + self.got2[k, :, :, cut].astype(F32)
        self.sum2[:, :, cut] = total.astype(BF16)
        for k in range(1, self.n_dp):
            self.plane_copy(c, k).start()

    def close(self, c):
        cut = self.chunks[c]
        total = self.sum2[self.z, :, cut].astype(F32)
        for k in range(1, self.n_dp):
            self.plane_copy(c, k).wait_recv()
            total = total + self.got3[k, :, cut].astype(F32)
        self.out[:, cut] = total

    def drain(self):
        for c in range(len(self.chunks)):
            for k in range(self.half):
                self.core_copy(c, k).wait_send()
            for k in range(1, self.half):
                self.chip_copy(c, k).wait_send()
            for k in range(1, self.n_dp):
                self.plane_copy(c, k).wait_send()


def reducer_scratch(n_chunks, n_dp, n_f, share, columns):
    half = n_f // 2
    return [
        pltpu.VMEM((half, n_dp, share, columns), BF16),
        pltpu.VMEM((half, n_dp, share, columns), BF16),
        pltpu.VMEM((half, n_dp, share, columns), BF16),
        pltpu.VMEM((n_dp, share, columns), BF16),
        pltpu.VMEM((n_dp, share, columns), BF16),
        pltpu.SemaphoreType.DMA((n_chunks, half)),
        pltpu.SemaphoreType.DMA((n_chunks, half)),
        pltpu.SemaphoreType.DMA((n_chunks, half)),
        pltpu.SemaphoreType.DMA((n_chunks, half)),
        pltpu.SemaphoreType.DMA((n_chunks, n_dp)),
        pltpu.SemaphoreType.DMA((n_chunks, n_dp)),
    ]


def input_grad(x_ref, dh_ref, d_ref, w_ref, vec_scr, grad_ref):
    width = dh_ref.shape[1]
    normed, inv_scale = norm_parts(x_ref)
    entered = jnp.zeros_like(normed)
    for part in range(3):
        entered = entered + dot(d_ref[part], w_ref[:, part * width : (part + 1) * width], NT)
    grad_ref[...] = dh_ref[...] + norm_back(entered * vec_scr[0:1, :], normed, inv_scale)


def norm1_grads(weighted, bias_grad, vec_ref, gv_ref):
    gain, bias = vec_ref[:, 0:1].astype(F32), vec_ref[:, 1:2].astype(F32)
    lane = lax.broadcasted_iota(jnp.int32, (1, LANES), 1)
    found = jnp.transpose(gv_ref[...])
    found = jnp.where(lane == 0, (weighted - bias * bias_grad) / gain, found)
    return jnp.where(lane == 1, bias_grad, found).astype(BF16)


def last_kernel(
    n_long, n_rows, part_ref, long_ref, short_ref, dh_ref, d_ref, w_ref, vec_ref,
    h_ref, col_ref, y_ref, out_ref, lg_ref, sg_ref, lo_ref, so_ref, vec_scr, *scratch,
):
    i = pl.program_id(0)
    reducer = Reducer(part_ref, out_ref, column_chunks(part_ref.shape[3]), scratch)

    @pl.when(i == 0)
    def _():
        reducer.greet()
        vec_scr[...] = vectors(vec_ref)
        reducer.meet()
        for c in range(N_CHUNKS):
            reducer.start_core(c)

    def back(x_ref, grad_ref):
        input_grad(x_ref[...], dh_ref, d_ref, w_ref, vec_scr, grad_ref)

    pl.when(i < n_long)(lambda: back(long_ref, lg_ref))
    pl.when((i >= n_long) & (i < n_rows))(lambda: back(short_ref, sg_ref))

    @pl.when(i == 0)
    def _():
        for c in range(N_CHUNKS):
            reducer.start_chip(c)

    def finish(out):
        out[...] = h_ref[...] + combine_rows(col_ref, y_ref)

    pl.when((i >= n_rows) & (i < n_rows + n_long))(lambda: finish(lo_ref))
    pl.when((i >= n_rows + n_long) & (i < 2 * n_rows))(lambda: finish(so_ref))

    @pl.when(i == 2 * n_rows - 1)
    def _():
        for c in range(N_CHUNKS):
            reducer.start_plane(c)
        for c in range(N_CHUNKS):
            reducer.close(c)
        reducer.drain()


def last_stage(partial, long_x, short_x, d_h, d_qkv, dense, h, slot_col, y_back):
    n_dp, n_f, share, columns = partial.shape
    count, width = d_h.shape
    n_long, n_short = long_x.shape[0] // ROWS, short_x.shape[0] // ROWS
    n_rows = n_long + n_short
    slots = y_back.shape[0]
    row = pl.BlockSpec((ROWS, width), lambda i: (jnp.minimum(i, n_rows - 1), 0))
    late = lambda i: (jnp.clip(i - n_rows, 0, n_rows - 1), 0)
    return pl.pallas_call(
        functools.partial(last_kernel, n_long, n_rows),
        grid=(2 * n_rows,),
        in_specs=[
            constant(partial.shape),
            pl.BlockSpec((ROWS, width), lambda i: (jnp.minimum(i, n_long - 1), 0)),
            pl.BlockSpec((ROWS, width), lambda i: (jnp.clip(i - n_long, 0, n_short - 1), 0)),
            row,
            pl.BlockSpec((3, ROWS, width), lambda i: (0, jnp.minimum(i, n_rows - 1), 0)),
            constant((width, 3 * width)),
            pl.BlockSpec((width, LANES), lambda i: (0, 4 * width // LANES)),
            pl.BlockSpec((ROWS, width), late),
            pl.BlockSpec((ROWS, 1), late),
            constant((slots, width)),
        ],
        out_specs=[
            pl.BlockSpec((share, columns), lambda i: (0, 0)),
            pl.BlockSpec((ROWS, width), lambda i: (jnp.minimum(i, n_long - 1), 0)),
            pl.BlockSpec((ROWS, width), lambda i: (jnp.clip(i - n_long, 0, n_short - 1), 0)),
            pl.BlockSpec((ROWS, width), lambda i: (jnp.clip(i - n_rows, 0, n_long - 1), 0)),
            pl.BlockSpec(
                (ROWS, width), lambda i: (jnp.clip(i - n_rows - n_long, 0, n_short - 1), 0)
            ),
        ],
        out_shape=[
            jax.ShapeDtypeStruct((share, columns), F32),
            jax.ShapeDtypeStruct(long_x.shape, F32),
            jax.ShapeDtypeStruct(short_x.shape, F32),
            jax.ShapeDtypeStruct(long_x.shape, F32),
            jax.ShapeDtypeStruct(short_x.shape, F32),
        ],
        scratch_shapes=[pltpu.VMEM((8, width), F32)]
        + reducer_scratch(N_CHUNKS, n_dp, n_f, share, columns),
        compiler_params=params(collective_id=1, has_side_effects=True),
        cost_estimate=cost(2 * count * width * (3 * width + slots), 60e6),
        name="last_stage",
    )(partial, long_x, short_x, d_h, d_qkv, dense, dense, h, slot_col, y_back)


def close_kernel(
    n_long, n_rows, proj_ref, gv_ref, long_ref, short_ref, dp_ref, dh_ref, d_ref, w_ref, vec_ref,
    h_ref, col_ref, y_ref, out_ref, lg_ref, sg_ref, lo_ref, so_ref,
    vec_scr, rows_ref, part_ref, stat_ref, *scratch,
):
    i = pl.program_id(0)
    n_dp, n_f, share, columns = part_ref.shape
    width = dh_ref.shape[1]
    chunks = [slice(c * width, (c + 1) * width) for c in range(3)] + [slice(3 * width, columns)]
    reducer = Reducer(part_ref, out_ref, chunks, scratch)
    begin_back, begin_out = 3, 3 + n_rows

    def scatter(value, cut):
        for index in range(n_dp * n_f):
            part_ref[index // n_f, index % n_f, :, cut] = value[
                index * share : (index + 1) * share
            ].astype(BF16)

    @pl.when(i == 0)
    def _():
        reducer.greet()
        vec_scr[...] = vectors(vec_ref)
        part_ref[:, :, :, :width] = proj_ref[...]
        reducer.meet()
        reducer.start_core(0)
        n = long_ref.shape[0]
        for ref, first in ((long_ref, 0), (short_ref, n)):
            for start in range(0, ref.shape[0], ROWS):
                normed, _ = norm_parts(ref[start : start + ROWS, :])
                rows_ref[first + start : first + start + ROWS, :] = (
                    normed * vec_scr[0:1, :] + vec_scr[1:2, :]
                ).astype(BF16)
        stat_ref[...] = jnp.zeros_like(stat_ref)
        reducer.start_chip(0)

    for part in range(3):

        @pl.when(i == part)
        def _(part=part):
            value = dot(rows_ref[...], dp_ref[0], TN)
            scatter(value, slice((part + 1) * width, (part + 2) * width))
            weight = w_ref[:, part * width : (part + 1) * width].astype(F32)
            sums = jnp.sum(dp_ref[0].astype(F32), 0, keepdims=True)
            stat_ref[:, 0:1] = stat_ref[:, 0:1] + jnp.sum(weight * value, 1, keepdims=True)
            stat_ref[:, 1:2] = stat_ref[:, 1:2] + jnp.sum(weight * sums, 1, keepdims=True)
            if part == 2:
                found = norm1_grads(stat_ref[:, 0:1], stat_ref[:, 1:2], vec_ref, gv_ref)
                scatter(found.astype(F32), slice(4 * width, columns))
            reducer.start_core(part + 1)
            if part:
                reducer.start_chip(part)

    @pl.when(i == begin_back)
    def _():
        reducer.start_chip(3)

    def back(x_ref, index, grad_ref):
        rows = pl.ds(pl.multiple_of(index * ROWS, ROWS), ROWS)
        input_grad(x_ref[rows, :], dh_ref, d_ref, w_ref, vec_scr, grad_ref)

    j = i - begin_back
    pl.when((j >= 0) & (j < n_long))(lambda: back(long_ref, j, lg_ref))
    pl.when((j >= n_long) & (j < n_rows))(lambda: back(short_ref, j - n_long, sg_ref))

    def finish(out):
        out[...] = h_ref[...] + combine_rows(col_ref, y_ref)

    m = i - begin_out
    pl.when((m >= 0) & (m < n_long))(lambda: finish(lo_ref))
    pl.when((m >= n_long) & (m < n_rows))(lambda: finish(so_ref))

    @pl.when(i == begin_out - 1)
    def _():
        reducer.start_plane(0)

    @pl.when(i == begin_out)
    def _():
        reducer.start_plane(1)

    @pl.when(i == begin_out + n_rows - 1)
    def _():
        reducer.start_plane(2)
        reducer.start_plane(3)
        for c in range(4):
            reducer.close(c)
        reducer.drain()


def close_stage(grad_proj, grad_vec, long_x, short_x, d_h, d_qkv, dense, h, slot_col, y_back):
    n_dp, n_f, share = grad_proj.shape[:3]
    count, width = d_h.shape
    columns = 4 * width + LANES
    n_long, n_short = long_x.shape[0] // ROWS, short_x.shape[0] // ROWS
    n_rows = n_long + n_short
    slots = y_back.shape[0]
    step = lambda i, base, last: jnp.clip(i - base, 0, last)
    return pl.pallas_call(
        functools.partial(close_kernel, n_long, n_rows),
        grid=(3 + 2 * n_rows,),
        in_specs=[
            constant(grad_proj.shape),
            constant(grad_vec.shape),
            constant(long_x.shape),
            constant(short_x.shape),
            pl.BlockSpec((1, count, width), lambda i: (jnp.minimum(i, 2), 0, 0)),
            pl.BlockSpec((ROWS, width), lambda i: (step(i, 3, n_rows - 1), 0)),
            pl.BlockSpec((3, ROWS, width), lambda i: (0, step(i, 3, n_rows - 1), 0)),
            constant((width, 3 * width)),
            pl.BlockSpec((width, LANES), lambda i: (0, 4 * width // LANES)),
            pl.BlockSpec((ROWS, width), lambda i: (step(i, 3 + n_rows, n_rows - 1), 0)),
            pl.BlockSpec((ROWS, 1), lambda i: (step(i, 3 + n_rows, n_rows - 1), 0)),
            constant((slots, width)),
        ],
        out_specs=[
            pl.BlockSpec((share, columns), lambda i: (0, 0)),
            pl.BlockSpec((ROWS, width), lambda i: (step(i, 3, n_long - 1), 0)),
            pl.BlockSpec((ROWS, width), lambda i: (step(i, 3 + n_long, n_short - 1), 0)),
            pl.BlockSpec((ROWS, width), lambda i: (step(i, 3 + n_rows, n_long - 1), 0)),
            pl.BlockSpec((ROWS, width), lambda i: (step(i, 3 + n_rows + n_long, n_short - 1), 0)),
        ],
        out_shape=[
            jax.ShapeDtypeStruct((share, columns), F32),
            jax.ShapeDtypeStruct(long_x.shape, F32),
            jax.ShapeDtypeStruct(short_x.shape, F32),
            jax.ShapeDtypeStruct(long_x.shape, F32),
            jax.ShapeDtypeStruct(short_x.shape, F32),
        ],
        scratch_shapes=[
            pltpu.VMEM((8, width), F32),
            pltpu.VMEM((count, width), BF16),
            pltpu.VMEM((n_dp, n_f, share, columns), BF16),
            pltpu.VMEM((width, LANES), F32),
        ]
        + reducer_scratch(4, n_dp, n_f, share, columns),
        compiler_params=params(collective_id=4, has_side_effects=True),
        cost_estimate=cost(2 * count * width * (6 * width + slots), 60e6),
        name="close_stage",
    )(grad_proj, grad_vec, long_x, short_x, d_qkv, d_h, d_qkv, dense, dense, h, slot_col, y_back)


def on_device(
    n_dp, n_f, long_x, short_x, long_len, short_len, expert_ids, ln1_gain, ln1_bias,
    w_qkv, w_proj, ln2_gain, ln2_bias, w_up, w_down, long_cot, short_cot,
):
    width = long_x.shape[2]
    share = w_qkv.shape[0]
    seqs = sequences(long_x.shape[:2], short_x.shape[:2])
    flat = lambda a: a.reshape(-1, width)
    xl, xs, gl, gs = flat(long_x), flat(short_x), flat(long_cot), flat(short_cot)
    n_long, n_short = xl.shape[0] // ROWS, xs.shape[0] // ROWS
    experts = n_f * w_up.shape[0]
    cap = 4 * expert_ids.shape[0] // (3 * experts)
    slots = experts * cap

    up = lax.all_gather(w_up, "dp", axis=2, tiled=True)[0]
    down = lax.all_gather(w_down, "dp", axis=1, tiled=True)[0]

    vec = jnp.stack([ln1_gain, ln1_bias, ln2_gain, ln2_bias], 1)
    own = jnp.concatenate(
        [w_qkv, w_proj.T, jnp.pad(vec, ((0, 0), (0, LANES - vec.shape[1])))], 1
    )
    dense, slot_col, slot_row, g_slots = gather_dense(
        own, expert_ids, gl, gs, n_dp, n_f, cap, slots
    )
    dense = dense.reshape(n_dp * n_f * share, own.shape[1])

    def exchange(rows):
        sent = lax.all_to_all(
            rows.reshape(n_f, cap, width), "fsdp", split_axis=0, concat_axis=0, tiled=True
        )
        return sent.reshape(slots, width)

    g_there = exchange(g_slots)
    qkv = make_qkv(xl, xs, dense)
    o, lse = attend(qkv, long_len, short_len, seqs)
    h, b_there, act, slope, grad_down = forward_experts(
        xl, xs, o, dense, slot_row, g_there, up, n_f, cap
    )
    grad_down = lax.psum_scatter(grad_down, "dp", scatter_dimension=0, tiled=True).astype(F32)
    y0, db0, gu0 = own_experts(
        lax.axis_index("dp").reshape(1), b_there, g_there, act, slope, up, w_down[0], n_f, cap
    )
    y, db_back, grad_up = back_experts(
        b_there, g_there, act, slope, up, down, y0, db0, gu0, n_dp, n_f, cap
    )
    db_back = db_back.reshape(slots, width)
    grad_up = lax.psum_scatter(grad_up, "dp", scatter_dimension=1, tiled=True).astype(F32)
    y_back = exchange(y)
    d_h, d_o, grad_proj, grad_vec = hidden_back(h, slot_col, db_back, gl, gs, o, dense)
    d_qkv = attend_back(qkv, o, d_o, lse, long_len, short_len, seqs)
    if share % 8 == 0:
        owned, long_grad, short_grad, long_out, short_out = close_stage(
            grad_proj.reshape(n_dp, n_f, share, width), grad_vec,
            xl, xs, d_h, d_qkv, dense, h, slot_col, y_back,
        )
    else:
        partial = dense_grads(xl, xs, d_qkv, dense, grad_proj, grad_vec)
        owned, long_grad, short_grad, long_out, short_out = last_stage(
            partial.reshape(n_dp, n_f, share, own.shape[1]),
            xl, xs, d_h, d_qkv, dense, h, slot_col, y_back,
        )
    return (
        long_out.reshape(long_x.shape),
        short_out.reshape(short_x.shape),
        long_grad.reshape(long_x.shape),
        short_grad.reshape(short_x.shape),
        owned[:, 4 * width],
        owned[:, 4 * width + 1],
        owned[:, width : 4 * width],
        owned[:, :width].T,
        owned[:, 4 * width + 2],
        owned[:, 4 * width + 3],
        grad_up[None],
        grad_down[None],
    )


def solution(mesh):
    both = ("dp", "fsdp")
    return jax.shard_map(
        functools.partial(on_device, mesh.shape["dp"], mesh.shape["fsdp"]),
        mesh=mesh,
        in_specs=(
            P(both, None, None),
            P(both, None, None),
            P(both),
            P(both),
            P(both, None),
            P(both),
            P(both),
            P(both, None),
            P(None, both),
            P(both),
            P(both),
            P("fsdp", None, "dp"),
            P("fsdp", "dp", None),
            P(both, None, None),
            P(both, None, None),
        ),
        out_specs=(
            P(both, None, None),
            P(both, None, None),
            P(both, None, None),
            P(both, None, None),
            P(both),
            P(both),
            P(both, None),
            P(None, both),
            P(both),
            P(both),
            P("fsdp", None, "dp"),
            P("fsdp", "dp", None),
        ),
        check_vma=False,
    )
```

```python
import functools

import jax
import jax.numpy as jnp
from jax import lax
from jax.experimental import pallas as pl
from jax.experimental.pallas import tpu as pltpu
from jax.sharding import PartitionSpec as P

MESH = pl.DeviceIdType.MESH
HEAD_DIM = 64
EPSILON = 1e-05
MASKED = -1e30
BF16 = jnp.bfloat16
F32 = jnp.float32
LANES = 128
ROWS = 512
BLOCK = 256
ATTEND = 512
ATTEND_BACK = 512
VMEM_LIMIT = 60 * 2**20
N_CHUNKS = 3

NN = (((1,), (0,)), ((), ()))
NT = (((1,), (1,)), ((), ()))
TN = (((0,), (0,)), ((), ()))


def dot(a, b, dims=NN, precision=None):
    return lax.dot_general(a, b, dims, preferred_element_type=F32, precision=precision)


def params(**extra):
    return pltpu.CompilerParams(vmem_limit_bytes=VMEM_LIMIT, **extra)


def cost(flops, moved, exps=0):
    return pl.CostEstimate(flops=int(flops), bytes_accessed=int(moved), transcendentals=int(exps))


def constant(shape):
    return pl.BlockSpec(shape, lambda *_: (0,) * len(shape), pipeline_mode=pl.Buffered(1))


def norm_parts(inputs):
    average = jnp.mean(inputs, -1, keepdims=True)
    centred = inputs - average
    inv_scale = lax.rsqrt(jnp.mean(centred * centred, -1, keepdims=True) + EPSILON)
    return centred * inv_scale, inv_scale


def norm_back(grad_normed, normed, inv_scale):
    centre_term = jnp.mean(grad_normed, -1, keepdims=True)
    slope_term = jnp.mean(grad_normed * normed, -1, keepdims=True)
    return inv_scale * (grad_normed - centre_term - normed * slope_term)


def vectors(vec_ref):
    return jnp.transpose(vec_ref[...].astype(F32))[:8]


def long_short(width, n_long):
    return [
        pl.BlockSpec((ROWS, width), lambda i: (jnp.minimum(i, n_long - 1), 0)),
        pl.BlockSpec((ROWS, width), lambda i: (jnp.maximum(i - n_long, 0), 0)),
    ]


def column_chunks(columns):
    tiles = columns // LANES
    edges = [LANES * (tiles * c // N_CHUNKS) for c in range(N_CHUNKS + 1)]
    return [slice(lo, hi) for lo, hi in zip(edges, edges[1:])]


def gather_kernel(
    n_dp, n_f, cap, own_ref, ids_ref, long_ref, short_ref, out_ref, col_ref, row_ref, slots_ref,
    rows_ref, z_send, z_recv, p_send, p_recv, c_send, c_recv, l_sem,
):
    z = lax.axis_index("dp")
    f = lax.axis_index("fsdp")
    half = n_f // 2
    partner = f + 1 - 2 * lax.rem(f, 2)
    barrier = pltpu.get_barrier_semaphore()
    for k in range(1, n_dp):
        pl.semaphore_signal(barrier, 1, device_id=(lax.rem(z + k, n_dp), f), device_id_type=MESH)
    for k in range(1, half):
        pl.semaphore_signal(barrier, 1, device_id=(z, lax.rem(f + 2 * k, n_f)), device_id_type=MESH)
    pl.semaphore_signal(barrier, 1, device_id=(z, partner), device_id_type=MESH)
    local = pltpu.make_async_copy(own_ref, out_ref.at[z, f], l_sem)
    local.start()
    pl.semaphore_wait(barrier, n_dp - 1 + half)

    chunks = column_chunks(own_ref.shape[1])
    z_copies, p_copies, c_copies = [], [], []

    def send_z(c):
        for k in range(1, n_dp):
            copy = pltpu.make_async_remote_copy(
                own_ref.at[:, chunks[c]], out_ref.at[z, f, :, chunks[c]],
                z_send.at[c, k], z_recv.at[c, k],
                device_id=(lax.rem(z + k, n_dp), f), device_id_type=MESH,
            )
            copy.start()
            z_copies.append(copy)

    def send_p(c):
        for k in range(1, n_dp):
            z_copies[c * (n_dp - 1) + k - 1].wait_recv()
        for k in range(1, half):
            copy = pltpu.make_async_remote_copy(
                out_ref.at[:, f, :, chunks[c]], out_ref.at[:, f, :, chunks[c]],
                p_send.at[c, k], p_recv.at[c, k],
                device_id=(z, lax.rem(f + 2 * k, n_f)), device_id_type=MESH,
            )
            copy.start()
            p_copies.append(copy)

    def send_c(c):
        for k in range(half):
            if k:
                p_copies[c * (half - 1) + k - 1].wait_recv()
            column = lax.rem(f + n_f - 2 * k, n_f)
            copy = pltpu.make_async_remote_copy(
                out_ref.at[:, column, :, chunks[c]], out_ref.at[:, column, :, chunks[c]],
                c_send.at[c, k], c_recv.at[c, k],
                device_id=(z, partner), device_id_type=MESH,
            )
            copy.start()
            c_copies.append(copy)

    def fill(block, carry):
        start = pl.multiple_of(block * BLOCK, BLOCK)
        slots_ref[pl.ds(start, BLOCK), :] = dispatch_block(row_ref, rows_ref[...], start, BLOCK)
        return carry

    n_blocks = slots_ref.shape[0] // BLOCK
    for c in range(len(chunks)):
        send_z(c)
    number_slots(cap, ids_ref, col_ref, row_ref)
    n_long = long_ref.shape[0]
    rows_ref[:n_long, :] = long_ref[...].astype(BF16)
    rows_ref[n_long:, :] = short_ref[...].astype(BF16)
    local.wait()
    for c in range(len(chunks)):
        send_p(c)
        lax.fori_loop(c * n_blocks // len(chunks), (c + 1) * n_blocks // len(chunks), fill, 0)
    for c in range(len(chunks)):
        send_c(c)
    for copy in c_copies:
        copy.wait_recv()
    for copy in z_copies + p_copies + c_copies:
        copy.wait_send()


def gather_dense(own, ids, long_cot, short_cot, n_dp, n_f, cap, slots):
    count, width = ids.shape[0], long_cot.shape[1]
    vmem = pl.BlockSpec(memory_space=pltpu.VMEM)
    return pl.pallas_call(
        functools.partial(gather_kernel, n_dp, n_f, cap),
        out_shape=[
            jax.ShapeDtypeStruct((n_dp, n_f) + own.shape, own.dtype),
            jax.ShapeDtypeStruct((count, 1), jnp.int32),
            jax.ShapeDtypeStruct((8, count), jnp.int32),
            jax.ShapeDtypeStruct((slots, width), BF16),
        ],
        in_specs=[pl.BlockSpec(memory_space=pl.ANY), vmem, vmem, vmem],
        out_specs=[pl.BlockSpec(memory_space=pl.ANY), vmem, vmem, vmem],
        scratch_shapes=[
            pltpu.VMEM((count, width), BF16),
            pltpu.SemaphoreType.DMA((N_CHUNKS, n_dp)),
            pltpu.SemaphoreType.DMA((N_CHUNKS, n_dp)),
            pltpu.SemaphoreType.DMA((N_CHUNKS, n_f // 2)),
            pltpu.SemaphoreType.DMA((N_CHUNKS, n_f // 2)),
            pltpu.SemaphoreType.DMA((N_CHUNKS, n_f // 2)),
            pltpu.SemaphoreType.DMA((N_CHUNKS, n_f // 2)),
            pltpu.SemaphoreType.DMA,
        ],
        compiler_params=params(collective_id=0, has_side_effects=True),
        cost_estimate=cost(0, 100e6),
        name="gather_dense",
    )(own, ids, long_cot, short_cot)


def dispatch_block(slot_row_ref, rows, first, size):
    slot_id = first + lax.broadcasted_iota(jnp.int32, (size, 1), 0)
    chosen = (slot_row_ref[0:1, :] == slot_id).astype(F32).astype(BF16)
    return dot(chosen, rows).astype(BF16)


def number_slots(cap, ids_ref, col_ref, row_ref):
    count = ids_ref.shape[0]
    lane = lax.broadcasted_iota(jnp.int32, (1, LANES), 1)
    onehot = (ids_ref[...] == lane).astype(F32)
    onehot_low = onehot.astype(BF16)
    col = lax.broadcasted_iota(jnp.int32, (1, count), 1)
    base = (lane * cap).astype(F32)
    ones = jnp.ones((8, LANES), F32)
    for start in range(0, count, ROWS):
        row = start + lax.broadcasted_iota(jnp.int32, (ROWS, 1), 0)
        before = dot((col < row).astype(F32).astype(BF16), onehot_low)
        picked = (before + base) * onehot[start : start + ROWS]
        col_ref[start : start + ROWS, :] = jnp.sum(picked, 1, keepdims=True).astype(jnp.int32)
        row_ref[:, start : start + ROWS] = dot(
            ones, picked, NT, precision=lax.Precision.HIGHEST
        ).astype(jnp.int32)


def peers(n_f):
    f = lax.axis_index("fsdp")

    def partner(k):
        place, digit = 0, 1
        while digit < n_f:
            place = place + digit * lax.rem(f // digit + k // digit, 2)
            digit *= 2
        return place

    return f, partner


def greet(n_f, to):
    z = lax.axis_index("dp")
    barrier = pltpu.get_barrier_semaphore()
    for k in range(1, n_f):
        pl.semaphore_signal(barrier, 1, device_id=(z, to(k)), device_id_type=MESH)


class Homeward:
    def __init__(self, n_f, ks, y_ref, yb_ref, send, recv):
        self.f, self.to = peers(n_f)
        self.n_f, self.ks = n_f, ks
        self.z = lax.axis_index("dp")
        self.y, self.yb, self.send, self.recv = y_ref, yb_ref, send, recv

    def transfer(self, k):
        return pltpu.make_async_remote_copy(
            self.y.at[self.to(k)], self.yb.at[self.f], self.send.at[k], self.recv.at[k],
            device_id=(self.z, self.to(k)), device_id_type=MESH,
        )

    def begin(self):
        greet(self.n_f, self.to)
        pl.semaphore_wait(pltpu.get_barrier_semaphore(), self.n_f - 1)
        for k in self.ks:
            self.transfer(k).start()

    def end(self):
        for k in self.ks:
            self.transfer(k).wait_recv()
            self.transfer(k).wait_send()


def qkv_kernel(n_long, width, long_ref, short_ref, w_ref, vec_ref, qkv_ref, vec_scr):
    i = pl.program_id(0)

    @pl.when(i == 0)
    def _():
        vec_scr[...] = vectors(vec_ref)

    def body(x_ref):
        normed, _ = norm_parts(x_ref[...])
        rows = (normed * vec_scr[0:1, :] + vec_scr[1:2, :]).astype(BF16)
        for part in range(3):
            cut = slice(part * width, (part + 1) * width)
            out = dot(rows, w_ref[:, cut])
            if part == 0:
                out = out * HEAD_DIM ** (-0.5)
            qkv_ref[:, cut] = out.astype(BF16)

    pl.when(i < n_long)(lambda: body(long_ref))
    pl.when(i >= n_long)(lambda: body(short_ref))


def make_qkv(long_x, short_x, dense):
    width = long_x.shape[1]
    n_long, n_short = long_x.shape[0] // ROWS, short_x.shape[0] // ROWS
    count = long_x.shape[0] + short_x.shape[0]
    return pl.pallas_call(
        functools.partial(qkv_kernel, n_long, width),
        grid=(n_long + n_short,),
        in_specs=long_short(width, n_long)
        + [
            constant((width, 3 * width)),
            pl.BlockSpec((width, LANES), lambda i: (0, 4 * width // LANES)),
        ],
        out_specs=pl.BlockSpec((ROWS, 3 * width), lambda i: (i, 0)),
        out_shape=jax.ShapeDtypeStruct((count, 3 * width), BF16),
        scratch_shapes=[pltpu.VMEM((8, width), F32)],
        compiler_params=params(),
        cost_estimate=cost(6 * count * width * width, count * width * 10 + 6 * width * width),
        name="make_qkv",
    )(long_x, short_x, dense, dense)


def sequences(long_shape, short_shape):
    found = []
    start = 0
    for which, (number, length) in enumerate((long_shape, short_shape)):
        for index in range(number):
            found.append((start, length, which, index))
            start += length
    return found


def head_masks():
    lane = lax.broadcasted_iota(jnp.int32, (1, LANES), 1)
    return (lane < HEAD_DIM, lane >= HEAD_DIM)


def marked(q, k, valid, first, masks, lane):
    key_pos = first + lax.broadcasted_iota(jnp.int32, (k.shape[0], 1), 0)
    bias = jnp.where(key_pos < valid, 0.0, MASKED).astype(BF16)
    found = []
    for head in range(2):
        spare = HEAD_DIM * (1 - head)
        qh = jnp.where(masks[head], q, jnp.where(lane == spare, 1.0, 0.0).astype(BF16))
        kh = jnp.where(masks[head], k, jnp.where(lane == spare, bias, jnp.zeros_like(bias)))
        found.append((qh, kh))
    return found


def attend_kernel(seqs, long_len, short_len, q_ref, k_ref, v_ref, o_ref, lse_ref):
    pair = pl.program_id(0)
    masks = head_masks()
    lane = lax.broadcasted_iota(jnp.int32, (1, LANES), 1)

    @pl.when(pair == 0)
    def _():
        lse_ref[...] = jnp.zeros_like(lse_ref)

    causal = lax.broadcasted_iota(jnp.int32, (ATTEND, ATTEND), 0) <= lax.broadcasted_iota(
        jnp.int32, (ATTEND, ATTEND), 1
    )
    upper = lax.broadcasted_iota(jnp.int32, (LANES, 1), 0) < HEAD_DIM
    for start, length, which, index in seqs:
        valid = (short_len if which else long_len)[index]
        rows = slice(start, start + length)
        heads = marked(q_ref[rows, :], k_ref[rows, :], valid, 0, masks, lane)
        v = jnp.transpose(v_ref[rows, :].astype(F32))
        values = [
            jnp.where(upper, v, 1.0).astype(BF16),
            jnp.where(upper, 1.0, v).astype(BF16),
        ]
        for first in range(0, length, ATTEND):
            last = first + ATTEND
            outs = []
            for head, (qh, kh) in enumerate(heads):
                qb = qh[first:last]
                near = dot(kh[first:last], qb, NT)
                near = jnp.where(causal, near, MASKED)
                top = jnp.max(near, 0, keepdims=True)
                if first:
                    far = dot(kh[:first], qb, NT)
                    top = jnp.maximum(top, jnp.max(far, 0, keepdims=True))
                out = dot(values[head][:, first:last], jnp.exp(near - top).astype(BF16))
                if first:
                    out = out + dot(values[head][:, :first], jnp.exp(far - top).astype(BF16))
                total = out[LANES - 1 : LANES] if head == 0 else out[0:1]
                outs.append(out * (1.0 / total))
                lse_ref[pl.ds(2 * pair + head, 1), start + first : start + last] = top + jnp.log(
                    total
                )
            o_ref[start + first : start + last, :] = jnp.transpose(
                jnp.where(upper, outs[0], outs[1])
            ).astype(BF16)


def attend(qkv, long_len, short_len, seqs):
    count, width = qkv.shape[0], qkv.shape[1] // 3
    pairs = width // LANES
    return pl.pallas_call(
        functools.partial(attend_kernel, seqs),
        grid=(pairs,),
        in_specs=[pl.BlockSpec(memory_space=pltpu.SMEM)] * 2
        + [
            pl.BlockSpec((count, LANES), lambda i: (0, i)),
            pl.BlockSpec((count, LANES), lambda i: (0, i + pairs)),
            pl.BlockSpec((count, LANES), lambda i: (0, i + 2 * pairs)),
        ],
        out_specs=[
            pl.BlockSpec((count, LANES), lambda i: (0, i)),
            pl.BlockSpec((LANES, count), lambda i: (0, 0)),
        ],
        out_shape=[
            jax.ShapeDtypeStruct((count, width), BF16),
            jax.ShapeDtypeStruct((LANES, count), F32),
        ],
        compiler_params=params(),
        cost_estimate=cost(16e9, 8 * count * width, 10e6),
        name="attend",
    )(long_len, short_len, qkv, qkv, qkv)


def attend_back_kernel(
    seqs, n_f, long_len, short_len, q_ref, k_ref, v_ref, o_ref, do_ref, lse_ref, y_ref, _,
    d_ref, yb_ref, dkt_ref, dvt_ref, lse_scr, send, recv, l_sem,
):
    pair = pl.program_id(0)
    masks = head_masks()
    lane = lax.broadcasted_iota(jnp.int32, (1, LANES), 1)

    home = Homeward(n_f, range(3 * n_f // 4, n_f), y_ref, yb_ref, send, recv)
    keep = pltpu.make_async_copy(y_ref.at[home.f], yb_ref.at[home.f], l_sem)

    @pl.when(pair == 0)
    def _():
        home.begin()
        keep.start()
        lse_scr[...] = jnp.transpose(lse_ref[...])

    causal = lax.broadcasted_iota(jnp.int32, (ATTEND_BACK, ATTEND_BACK), 1) <= (
        lax.broadcasted_iota(jnp.int32, (ATTEND_BACK, ATTEND_BACK), 0)
    )
    for start, length, which, index in seqs:
        valid = (short_len if which else long_len)[index]
        rows = slice(start, start + length)
        q, k, v, do = q_ref[rows, :], k_ref[rows, :], v_ref[rows, :], do_ref[rows, :]
        heads = marked(q, k, valid, 0, masks, lane)
        q_t = jnp.transpose(q.astype(F32)).astype(BF16)
        do_t = jnp.transpose(do.astype(F32)).astype(BF16)
        both = do.astype(F32) * o_ref[rows, :].astype(F32)
        lse_all = lse_scr[rows, :]
        dkt_ref[...] = jnp.zeros_like(dkt_ref)
        dvt_ref[...] = jnp.zeros_like(dvt_ref)
        for first in range(0, length, ATTEND_BACK):
            last = first + ATTEND_BACK
            dqs = []
            for head, (qh, kh) in enumerate(heads):
                part = slice(HEAD_DIM * head, HEAD_DIM * (head + 1))
                doh = jnp.where(masks[head], do[first:last], jnp.zeros_like(do[first:last]))
                lse = jnp.sum(
                    jnp.where(lane == 2 * pair + head, lse_all[first:last], 0.0), 1, keepdims=True
                )
                delta = jnp.sum(jnp.where(masks[head], both[first:last], 0.0), 1, keepdims=True)
                dq = jnp.zeros((ATTEND_BACK, LANES), F32)
                for keys in (slice(0, first), slice(first, last)):
                    if keys.stop == keys.start:
                        continue
                    p = jnp.exp(dot(qh[first:last], kh[keys], NT) - lse)
                    if keys.start == first:
                        p = jnp.where(causal, p, 0.0)
                    dp = dot(doh, v[keys], NT)
                    ds = (p * (dp - delta)).astype(BF16)
                    dvt_ref[part, keys] = dvt_ref[part, keys] + dot(
                        do_t[part, first:last], p.astype(BF16)
                    )
                    dkt_ref[part, keys] = dkt_ref[part, keys] + dot(q_t[part, first:last], ds)
                    dq = dq + dot(ds, k[keys])
                dqs.append(dq)
            d_ref[0, start + first : start + last, :] = (
                jnp.where(masks[0], dqs[0], dqs[1]) * HEAD_DIM ** (-0.5)
            ).astype(BF16)
        d_ref[1, rows, :] = jnp.transpose(dkt_ref[:, :length]).astype(BF16)
        d_ref[2, rows, :] = jnp.transpose(dvt_ref[:, :length]).astype(BF16)

    @pl.when(pair == pl.num_programs(0) - 1)
    def _():
        keep.wait()
        home.end()


def attend_back(qkv, o, d_o, lse, long_len, short_len, seqs, y, y_back):
    count, width = o.shape
    n_f = y.shape[0]
    pairs = width // LANES
    longest = max(length for _, length, _, _ in seqs)
    one = pl.BlockSpec((count, LANES), lambda i: (0, i))
    return pl.pallas_call(
        functools.partial(attend_back_kernel, seqs, n_f),
        grid=(pairs,),
        in_specs=[pl.BlockSpec(memory_space=pltpu.SMEM)] * 2
        + [
            one,
            pl.BlockSpec((count, LANES), lambda i: (0, i + pairs)),
            pl.BlockSpec((count, LANES), lambda i: (0, i + 2 * pairs)),
            one,
            one,
            constant((LANES, count)),
            pl.BlockSpec(memory_space=pl.ANY),
            pl.BlockSpec(memory_space=pl.ANY),
        ],
        out_specs=[
            pl.BlockSpec((3, count, LANES), lambda i: (0, 0, i)),
            pl.BlockSpec(memory_space=pl.ANY),
        ],
        input_output_aliases={9: 1},
        out_shape=[
            jax.ShapeDtypeStruct((3, count, width), BF16),
            jax.ShapeDtypeStruct(y.shape, BF16),
        ],
        scratch_shapes=[
            pltpu.VMEM((LANES, longest), F32),
            pltpu.VMEM((LANES, longest), F32),
            pltpu.VMEM((count, LANES), F32),
            pltpu.SemaphoreType.DMA((n_f,)),
            pltpu.SemaphoreType.DMA((n_f,)),
            pltpu.SemaphoreType.DMA,
        ],
        compiler_params=params(collective_id=5, has_side_effects=True),
        cost_estimate=cost(40e9, 16 * count * width, 10e6),
        name="attend_back",
    )(long_len, short_len, qkv, qkv, qkv, o, d_o, lse, y, y_back)


def gelu_parts(pre):
    scale = 0.7978845608028654
    square = pre * pre
    flat = jnp.tanh(scale * pre * (1.0 + 0.044715 * square))
    half = 0.5 * (1.0 + flat)
    slope = half + (0.5 * scale) * pre * (1.0 - flat * flat) * (1.0 + 0.134145 * square)
    return half * pre, slope


def forward_kernel(
    n_f, n_long, n_rows, long_ref, short_ref, o_ref, w_ref, vec_ref, row_ref, g_ref, up_ref,
    h_ref, there_ref, act_ref, slope_ref, gd_ref,
    rows_ref, vec_scr, out_buf, in_buf, all_ref, send, recv,
):
    i = pl.program_id(0)
    z = lax.axis_index("dp")
    f, partner = peers(n_f)
    cap, width = out_buf.shape[1:]
    n_up = n_rows + n_f
    n_down = n_up + n_f
    barrier = pltpu.get_barrier_semaphore()

    def transfer(k):
        return pltpu.make_async_remote_copy(
            out_buf.at[k], in_buf.at[f], send.at[k], recv.at[k],
            device_id=(z, partner(k)), device_id_type=MESH,
        )

    @pl.when(i == 0)
    def _():
        greet(n_f, partner)
        vec_scr[...] = vectors(vec_ref)

    def body(x_ref):
        hidden = x_ref[...] + dot(o_ref[...], w_ref[...], NT)
        h_ref[...] = hidden
        normed, _ = norm_parts(hidden)
        rows_ref[pl.ds(pl.multiple_of(i * ROWS, ROWS), ROWS), :] = (
            normed * vec_scr[2:3, :] + vec_scr[3:4, :]
        ).astype(BF16)

    pl.when(i < n_long)(lambda: body(long_ref))
    pl.when((i >= n_long) & (i < n_rows))(lambda: body(short_ref))

    @pl.when(i == n_rows)
    def _():
        pl.semaphore_wait(barrier, n_f - 1)

    @pl.when((i >= n_rows) & (i < n_up - 1))
    def _():
        k = i - n_rows + 1
        out_buf[k] = dispatch_block(row_ref, rows_ref[...], partner(k) * cap, cap)
        transfer(k).start()

    @pl.when(i == n_up - 1)
    def _():
        in_buf[f] = dispatch_block(row_ref, rows_ref[...], f * cap, cap)

    @pl.when((i > n_up) & (i < n_down))
    def _():
        transfer(i - n_up).wait_recv()

    @pl.when((i >= n_up) & (i < n_down))
    def _():
        origin = partner(i - n_up)
        rows = in_buf[origin]
        here = pl.ds(pl.multiple_of(origin * cap, cap), cap)
        for first in range(0, up_ref.shape[1], width):
            cut = slice(first, first + width)
            act, slope = gelu_parts(dot(rows, up_ref[:, cut]))
            act = act.astype(BF16)
            act_ref[:, cut] = act
            slope_ref[:, cut] = slope.astype(BF16)
            all_ref[here, cut] = act
        there_ref[here, :] = rows

    @pl.when(i >= n_down)
    def _():
        cut = pl.ds(pl.multiple_of((i - n_down) * width, width), width)
        gd_ref[...] = dot(all_ref[:, cut], g_ref[...], TN).astype(BF16)

    @pl.when(i == pl.num_programs(0) - 1)
    def _():
        for k in range(1, n_f):
            transfer(k).wait_send()


def forward_experts(long_x, short_x, o, dense, slot_row, g_there, up, n_f, cap):
    width = long_x.shape[1]
    hidden = up.shape[1]
    n_long, n_short = long_x.shape[0] // ROWS, short_x.shape[0] // ROWS
    n_rows = n_long + n_short
    n_up = n_rows + n_f
    n_down = n_up + n_f
    n_hidden = hidden // width
    slots = n_f * cap
    count = o.shape[0]
    tile = pl.BlockSpec((cap, hidden), lambda i: (jnp.clip(i - n_up, 0, n_f - 1), 0))
    return pl.pallas_call(
        functools.partial(forward_kernel, n_f, n_long, n_rows),
        grid=(n_down + n_hidden,),
        in_specs=[
            pl.BlockSpec((ROWS, width), lambda i: (jnp.minimum(i, n_long - 1), 0)),
            pl.BlockSpec((ROWS, width), lambda i: (jnp.clip(i - n_long, 0, n_short - 1), 0)),
            pl.BlockSpec((ROWS, width), lambda i: (jnp.minimum(i, n_rows - 1), 0)),
            pl.BlockSpec((width, width), lambda i: (0, 3), pipeline_mode=pl.Buffered(1)),
            pl.BlockSpec((width, LANES), lambda i: (0, 4 * width // LANES)),
            constant((8, count)),
            constant((slots, width)),
            constant((width, hidden)),
        ],
        out_specs=[
            pl.BlockSpec((ROWS, width), lambda i: (jnp.minimum(i, n_rows - 1), 0)),
            pl.BlockSpec((slots, width), lambda i: (0, 0)),
            tile,
            tile,
            pl.BlockSpec((width, width), lambda i: (jnp.clip(i - n_down, 0, n_hidden - 1), 0)),
        ],
        out_shape=[
            jax.ShapeDtypeStruct((count, width), F32),
            jax.ShapeDtypeStruct((slots, width), BF16),
            jax.ShapeDtypeStruct((slots, hidden), BF16),
            jax.ShapeDtypeStruct((slots, hidden), BF16),
            jax.ShapeDtypeStruct((hidden, width), BF16),
        ],
        scratch_shapes=[
            pltpu.VMEM((count, width), BF16),
            pltpu.VMEM((8, width), F32),
            pltpu.VMEM((n_f, cap, width), BF16),
            pltpu.VMEM((n_f, cap, width), BF16),
            pltpu.VMEM((slots, hidden), BF16),
            pltpu.SemaphoreType.DMA((n_f,)),
            pltpu.SemaphoreType.DMA((n_f,)),
        ],
        compiler_params=params(collective_id=2, has_side_effects=True),
        cost_estimate=cost(
            2 * slots * width * (count + 2 * hidden), 60e6, slots * hidden
        ),
        name="forward_experts",
    )(long_x, short_x, o, dense, dense, slot_row, g_there, up)


def own_kernel(
    n_f, z_ref, b_ref, g_ref, act_ref, slope_ref, up_ref, down_ref, y_ref, db_ref, gu_ref, all_ref
):
    i = pl.program_id(0)
    _, partner = peers(n_f)
    cap = y_ref.shape[0]

    @pl.when(i < n_f)
    def _():
        here = pl.ds(pl.multiple_of(partner(i) * cap, cap), cap)
        d_act = dot(g_ref[here, :], down_ref[...], NT)
        d_pre = (d_act * slope_ref[...].astype(F32)).astype(BF16)
        all_ref[here, :] = d_pre
        db_ref[...] = dot(d_pre, up_ref[...], NT)
        y_ref[...] = dot(act_ref[...], down_ref[...])

    @pl.when(i >= n_f)
    def _():
        gu_ref[...] = dot(b_ref[...], all_ref[...], TN).astype(BF16)


def own_experts(z, b_there, g_there, act, slope, up, own_down, n_f, cap):
    slots, width = b_there.shape
    piece = own_down.shape[0]
    tile = pl.BlockSpec((cap, piece), lambda i, z: (jnp.minimum(i, n_f - 1), z[0]))
    out = pl.BlockSpec((cap, width), lambda i, z: (jnp.minimum(i, n_f - 1), 0))
    return pl.pallas_call(
        functools.partial(own_kernel, n_f),
        grid_spec=pltpu.PrefetchScalarGridSpec(
            num_scalar_prefetch=1,
            grid=(n_f + 1,),
            in_specs=[
                constant((slots, width)),
                constant((slots, width)),
                tile,
                tile,
                pl.BlockSpec((width, piece), lambda i, z: (0, z[0])),
                constant((piece, width)),
            ],
            out_specs=[out, out, pl.BlockSpec((width, piece), lambda i, z: (0, 0))],
            scratch_shapes=[pltpu.VMEM((slots, piece), BF16)],
        ),
        out_shape=[
            jax.ShapeDtypeStruct((slots, width), F32),
            jax.ShapeDtypeStruct((slots, width), F32),
            jax.ShapeDtypeStruct((width, piece), BF16),
        ],
        compiler_params=params(),
        cost_estimate=cost(8 * slots * width * piece, 30e6),
        name="own_experts",
    )(z, b_there, g_there, act, slope, up, own_down)


def back_kernel(
    n_dp, n_f, b_ref, g_ref, act_ref, slope_ref, up_ref, down_ref, y0_ref, db0_ref, gu0_ref,
    y_ref, db_ref, gu_ref, out_buf, all_ref, send, recv, l_sem,
):
    i = pl.program_id(0)
    z = lax.axis_index("dp")
    f, partner = peers(n_f)
    cap, width = out_buf.shape[1:]
    piece = gu_ref.shape[1]
    barrier = pltpu.get_barrier_semaphore()

    def transfer(k):
        return pltpu.make_async_remote_copy(
            out_buf.at[k], db_ref.at[f], send.at[k], recv.at[k],
            device_id=(z, partner(k)), device_id_type=MESH,
        )

    def other(m):
        return pl.ds(pl.multiple_of(lax.rem(z + m, n_dp) * piece, piece), piece)

    keep = pltpu.make_async_copy(out_buf.at[0], db_ref.at[f], l_sem)

    @pl.when(i == 0)
    def _():
        greet(n_f, partner)

    @pl.when(i < n_f)
    def _():
        k = n_f - 1 - i
        here = pl.ds(pl.multiple_of(partner(k) * cap, cap), cap)
        g = g_ref[here, :]
        d_b = db0_ref[...]
        for m in range(1, n_dp):
            d_act = dot(g, down_ref[other(m), :], NT)
            d_pre = (d_act * slope_ref[:, other(m)].astype(F32)).astype(BF16)
            all_ref[here, other(m)] = d_pre
            d_b = d_b + dot(d_pre, up_ref[:, other(m)], NT)
        out_buf[k] = d_b.astype(BF16)

    @pl.when(i == 0)
    def _():
        pl.semaphore_wait(barrier, n_f - 1)

    @pl.when(i < n_f - 1)
    def _():
        transfer(n_f - 1 - i).start()

    @pl.when(i == n_f - 1)
    def _():
        keep.start()

    @pl.when(i < n_f)
    def _():
        here = pl.ds(pl.multiple_of(partner(n_f - 1 - i) * cap, cap), cap)
        y = y0_ref[...]
        for m in range(1, n_dp):
            y = y + dot(act_ref[:, other(m)], down_ref[other(m), :])
        y_ref[here, :] = y.astype(BF16)

    @pl.when((i >= n_f) & (i - n_f == z))
    def _():
        gu_ref[...] = gu0_ref[...]

    @pl.when((i >= n_f) & (i - n_f != z))
    def _():
        cut = pl.ds(pl.multiple_of((i - n_f) * piece, piece), piece)
        gu_ref[...] = dot(b_ref[...], all_ref[:, cut], TN).astype(BF16)

    @pl.when(i == pl.num_programs(0) - 1)
    def _():
        keep.wait()
        for k in range(1, n_f):
            transfer(k).wait_recv()
        for k in range(1, n_f):
            transfer(k).wait_send()


def back_experts(b_there, g_there, act, slope, up, down, y0, db0, gu0, n_dp, n_f, cap):
    slots, width = b_there.shape
    hidden = up.shape[1]
    piece = hidden // n_dp
    tile = pl.BlockSpec((cap, hidden), lambda i: (jnp.maximum(n_f - 1 - i, 0), 0))
    begun = pl.BlockSpec((cap, width), lambda i: (jnp.maximum(n_f - 1 - i, 0), 0))
    return pl.pallas_call(
        functools.partial(back_kernel, n_dp, n_f),
        grid=(n_f + n_dp,),
        in_specs=[
            constant((slots, width)),
            constant((slots, width)),
            tile,
            tile,
            constant((width, hidden)),
            constant((hidden, width)),
            begun,
            begun,
            constant((width, piece)),
        ],
        out_specs=[
            pl.BlockSpec((slots, width), lambda i: (0, 0)),
            pl.BlockSpec(memory_space=pl.ANY),
            pl.BlockSpec((width, piece), lambda i: (0, jnp.maximum(i - n_f, 0))),
        ],
        out_shape=[
            jax.ShapeDtypeStruct((slots, width), BF16),
            jax.ShapeDtypeStruct((n_f, cap, width), BF16),
            jax.ShapeDtypeStruct((width, hidden), BF16),
        ],
        scratch_shapes=[
            pltpu.VMEM((n_f, cap, width), BF16),
            pltpu.VMEM((slots, hidden), BF16),
            pltpu.SemaphoreType.DMA((n_f,)),
            pltpu.SemaphoreType.DMA((n_f,)),
            pltpu.SemaphoreType.DMA,
        ],
        compiler_params=params(collective_id=3, has_side_effects=True),
        cost_estimate=cost(6 * slots * width * hidden, 60e6),
        name="back_experts",
    )(b_there, g_there, act, slope, up, down, y0, db0, gu0)


def combine_rows(col_ref, slots_ref):
    slot_id = lax.broadcasted_iota(jnp.int32, (1, slots_ref.shape[0]), 1)
    chosen = (col_ref[...] == slot_id).astype(F32).astype(BF16)
    return dot(chosen, slots_ref[...])


def hidden_back_kernel(
    n_f, n_long, n_rows, h_ref, col_ref, db_ref, long_ref, short_ref, o_ref, w_ref, vec_ref, y_ref,
    dh_ref, do_ref, gp_ref, gv_ref, yb_ref, acc_ref, vec_scr, send, recv,
):
    i = pl.program_id(0)
    home = Homeward(n_f, range(1, 3 * n_f // 4), y_ref, yb_ref, send, recv)
    pl.when(i == 0)(home.begin)

    @pl.when(i == 0)
    def _():
        vec_scr[...] = vectors(vec_ref)
        acc_ref[...] = jnp.zeros_like(acc_ref)
        gv_ref[...] = jnp.zeros_like(gv_ref)

    def body(cot_ref):
        d_b = combine_rows(col_ref, db_ref)
        normed, inv_scale = norm_parts(h_ref[...])
        gv_ref[2:3, :] = gv_ref[2:3, :] + jnp.sum(d_b * normed, 0, keepdims=True)
        gv_ref[3:4, :] = gv_ref[3:4, :] + jnp.sum(d_b, 0, keepdims=True)
        d_h = cot_ref[...] + norm_back(d_b * vec_scr[2:3, :], normed, inv_scale)
        dh_ref[...] = d_h
        d_attn = d_h.astype(BF16)
        do_ref[...] = dot(d_attn, w_ref[...]).astype(BF16)
        acc_ref[...] = acc_ref[...] + dot(d_attn, o_ref[...], TN)

    pl.when(i < n_long)(lambda: body(long_ref))
    pl.when(i >= n_long)(lambda: body(short_ref))

    @pl.when(i == n_rows - 1)
    def _():
        gp_ref[...] = acc_ref[...].astype(BF16)
        home.end()


def hidden_back(h, slot_col, db_back, long_cot, short_cot, o, dense, y):
    n_f = y.shape[0]
    count, width = h.shape
    slots = db_back.shape[0]
    n_long, n_short = long_cot.shape[0] // ROWS, short_cot.shape[0] // ROWS
    n_rows = n_long + n_short
    row = pl.BlockSpec((ROWS, width), lambda i: (i, 0))
    return pl.pallas_call(
        functools.partial(hidden_back_kernel, n_f, n_long, n_rows),
        grid=(n_rows,),
        in_specs=[row, pl.BlockSpec((ROWS, 1), lambda i: (i, 0)), constant((slots, width))]
        + long_short(width, n_long)
        + [
            row,
            pl.BlockSpec((width, width), lambda i: (0, 3)),
            pl.BlockSpec((width, LANES), lambda i: (0, 4 * width // LANES)),
            pl.BlockSpec(memory_space=pl.ANY),
        ],
        out_specs=[
            row,
            row,
            pl.BlockSpec((width, width), lambda i: (0, 0)),
            pl.BlockSpec((LANES, width), lambda i: (0, 0)),
            pl.BlockSpec(memory_space=pl.ANY),
        ],
        out_shape=[
            jax.ShapeDtypeStruct((count, width), F32),
            jax.ShapeDtypeStruct((count, width), BF16),
            jax.ShapeDtypeStruct((width, width), BF16),
            jax.ShapeDtypeStruct((LANES, width), F32),
            jax.ShapeDtypeStruct(y.shape, BF16),
        ],
        scratch_shapes=[
            pltpu.VMEM((width, width), F32),
            pltpu.VMEM((8, width), F32),
            pltpu.SemaphoreType.DMA((n_f,)),
            pltpu.SemaphoreType.DMA((n_f,)),
        ],
        compiler_params=params(collective_id=6, has_side_effects=True),
        cost_estimate=cost(2 * (slots + 2 * width) * count * width, 16 * count * width),
        name="hidden_back",
    )(h, slot_col, db_back, long_cot, short_cot, o, dense, dense, y)


def grads_kernel(
    n_long, n_rows, width, long_ref, short_ref, d_ref, w_ref, vec_ref, gp_ref, gv_ref,
    out_ref, acc_ref, vec_scr, sum_scr,
):
    i = pl.program_id(0)

    @pl.when(i == 0)
    def _():
        vec_scr[...] = vectors(vec_ref)
        acc_ref[...] = jnp.zeros_like(acc_ref)
        sum_scr[...] = jnp.zeros_like(sum_scr)

    def body(x_ref):
        normed, _ = norm_parts(x_ref[...])
        rows = (normed * vec_scr[0:1, :] + vec_scr[1:2, :]).astype(BF16)
        for part in range(3):
            cut = slice(part * width, (part + 1) * width)
            acc_ref[:, cut] = acc_ref[:, cut] + dot(rows, d_ref[part], TN)
            sum_scr[:, cut] = sum_scr[:, cut] + jnp.sum(
                d_ref[part].astype(F32), 0, keepdims=True
            )

    pl.when(i < n_long)(lambda: body(long_ref))
    pl.when(i >= n_long)(lambda: body(short_ref))

    @pl.when(i == n_rows - 1)
    def _():
        out_ref[:, :width] = gp_ref[...]
        out_ref[:, width : 4 * width] = acc_ref[...].astype(BF16)
        weighted = jnp.zeros((width, 1), F32)
        bias_grad = jnp.zeros((width, 1), F32)
        for part in range(3):
            cut = slice(part * width, (part + 1) * width)
            weight = w_ref[:, cut].astype(F32)
            weighted = weighted + jnp.sum(weight * acc_ref[:, cut], 1, keepdims=True)
            bias_grad = bias_grad + jnp.sum(weight * sum_scr[:, cut], 1, keepdims=True)
        out_ref[:, 4 * width :] = norm1_grads(weighted, bias_grad, vec_ref, gv_ref)


def dense_grads(long_x, short_x, d_qkv, dense, grad_proj, grad_vec):
    count, width = d_qkv.shape[1:]
    n_long, n_short = long_x.shape[0] // ROWS, short_x.shape[0] // ROWS
    n_rows = n_long + n_short
    return pl.pallas_call(
        functools.partial(grads_kernel, n_long, n_rows, width),
        grid=(n_rows,),
        in_specs=long_short(width, n_long)
        + [
            pl.BlockSpec((3, ROWS, width), lambda i: (0, i, 0)),
            constant((width, 3 * width)),
            pl.BlockSpec((width, LANES), lambda i: (0, 4 * width // LANES)),
            constant((width, width)),
            constant((LANES, width)),
        ],
        out_specs=pl.BlockSpec((width, 4 * width + LANES), lambda i: (0, 0)),
        out_shape=jax.ShapeDtypeStruct((width, 4 * width + LANES), BF16),
        scratch_shapes=[
            pltpu.VMEM((width, 3 * width), F32),
            pltpu.VMEM((8, width), F32),
            pltpu.VMEM((1, 3 * width), F32),
        ],
        compiler_params=params(),
        cost_estimate=cost(6 * count * width * width, 16 * count * width),
        name="dense_grads",
    )(long_x, short_x, d_qkv, dense, dense, grad_proj, grad_vec)


class Reducer:
    def __init__(self, part_ref, out_ref, chunks, scratch):
        self.part, self.out, self.chunks = part_ref, out_ref, chunks
        self.got1, self.sum1, self.got2, self.sum2, self.got3 = scratch[:5]
        self.sems = scratch[5:]
        self.n_dp, self.n_f = part_ref.shape[:2]
        self.z = lax.axis_index("dp")
        self.f = lax.axis_index("fsdp")
        self.half = self.n_f // 2
        self.parity = lax.rem(self.f, 2)
        self.mine = self.f // 2
        self.partner = self.f + 1 - 2 * self.parity
        self.order = list(range(1, self.half)) + [0]
        self.barrier = pltpu.get_barrier_semaphore()

    def greet(self):
        z, f = self.z, self.f
        for k in range(1, self.n_dp):
            pl.semaphore_signal(
                self.barrier, 1, device_id=(lax.rem(z + k, self.n_dp), f), device_id_type=MESH
            )
        for k in range(1, self.half):
            pl.semaphore_signal(
                self.barrier, 1, device_id=(z, lax.rem(f + 2 * k, self.n_f)), device_id_type=MESH
            )
        pl.semaphore_signal(self.barrier, 1, device_id=(z, self.partner), device_id_type=MESH)

    def meet(self):
        pl.semaphore_wait(self.barrier, self.n_dp - 1 + self.half)

    def slot(self, k):
        return lax.rem(self.mine + k, self.half)

    def core_copy(self, c, k):
        cut, slot = self.chunks[c], self.slot(k)
        return pltpu.make_async_remote_copy(
            self.part.at[:, 2 * slot + 1 - self.parity, :, cut], self.got1.at[slot, :, :, cut],
            self.sems[0].at[c, k], self.sems[1].at[c, k],
            device_id=(self.z, self.partner), device_id_type=MESH,
        )

    def chip_copy(self, c, k):
        cut = self.chunks[c]
        return pltpu.make_async_remote_copy(
            self.sum1.at[self.slot(k), :, :, cut], self.got2.at[k, :, :, cut],
            self.sems[2].at[c, k], self.sems[3].at[c, k],
            device_id=(self.z, lax.rem(self.f + 2 * k, self.n_f)), device_id_type=MESH,
        )

    def plane_copy(self, c, k):
        cut, there = self.chunks[c], lax.rem(self.z + k, self.n_dp)
        return pltpu.make_async_remote_copy(
            self.sum2.at[there, :, cut], self.got3.at[k, :, cut],
            self.sems[4].at[c, k], self.sems[5].at[c, k],
            device_id=(there, self.f), device_id_type=MESH,
        )

    def start_core(self, c):
        for k in self.order:
            self.core_copy(c, k).start()

    def start_chip(self, c):
        cut = self.chunks[c]
        for k in self.order:
            slot = self.slot(k)
            self.core_copy(c, k).wait_recv()
            self.sum1[slot, :, :, cut] = (
                self.part[:, 2 * slot + self.parity, :, cut].astype(F32)
                + self.got1[slot, :, :, cut].astype(F32)
            ).astype(BF16)
            if k:
                self.chip_copy(c, k).start()

    def start_plane(self, c):
        cut = self.chunks[c]
        total = self.sum1[self.mine, :, :, cut].astype(F32)
        for k in range(1, self.half):
            self.chip_copy(c, k).wait_recv()
            total = total + self.got2[k, :, :, cut].astype(F32)
        self.sum2[:, :, cut] = total.astype(BF16)
        for k in range(1, self.n_dp):
            self.plane_copy(c, k).start()

    def close(self, c):
        cut = self.chunks[c]
        total = self.sum2[self.z, :, cut].astype(F32)
        for k in range(1, self.n_dp):
            self.plane_copy(c, k).wait_recv()
            total = total + self.got3[k, :, cut].astype(F32)
        self.out[:, cut] = total

    def drain(self):
        for c in range(len(self.chunks)):
            for k in range(self.half):
                self.core_copy(c, k).wait_send()
            for k in range(1, self.half):
                self.chip_copy(c, k).wait_send()
            for k in range(1, self.n_dp):
                self.plane_copy(c, k).wait_send()


def reducer_scratch(n_chunks, n_dp, n_f, share, columns):
    half = n_f // 2
    return [
        pltpu.VMEM((half, n_dp, share, columns), BF16),
        pltpu.VMEM((half, n_dp, share, columns), BF16),
        pltpu.VMEM((half, n_dp, share, columns), BF16),
        pltpu.VMEM((n_dp, share, columns), BF16),
        pltpu.VMEM((n_dp, share, columns), BF16),
        pltpu.SemaphoreType.DMA((n_chunks, half)),
        pltpu.SemaphoreType.DMA((n_chunks, half)),
        pltpu.SemaphoreType.DMA((n_chunks, half)),
        pltpu.SemaphoreType.DMA((n_chunks, half)),
        pltpu.SemaphoreType.DMA((n_chunks, n_dp)),
        pltpu.SemaphoreType.DMA((n_chunks, n_dp)),
    ]


def input_grad(x_ref, dh_ref, d_ref, w_ref, vec_scr, grad_ref):
    width = dh_ref.shape[1]
    normed, inv_scale = norm_parts(x_ref)
    entered = jnp.zeros_like(normed)
    for part in range(3):
        entered = entered + dot(d_ref[part], w_ref[:, part * width : (part + 1) * width], NT)
    grad_ref[...] = dh_ref[...] + norm_back(entered * vec_scr[0:1, :], normed, inv_scale)


def norm1_grads(weighted, bias_grad, vec_ref, gv_ref):
    gain, bias = vec_ref[:, 0:1].astype(F32), vec_ref[:, 1:2].astype(F32)
    lane = lax.broadcasted_iota(jnp.int32, (1, LANES), 1)
    found = jnp.transpose(gv_ref[...])
    found = jnp.where(lane == 0, (weighted - bias * bias_grad) / gain, found)
    return jnp.where(lane == 1, bias_grad, found).astype(BF16)


def last_kernel(
    n_long, n_rows, part_ref, long_ref, short_ref, dh_ref, d_ref, w_ref, vec_ref,
    h_ref, col_ref, y_ref, out_ref, lg_ref, sg_ref, lo_ref, so_ref, vec_scr, *scratch,
):
    i = pl.program_id(0)
    reducer = Reducer(part_ref, out_ref, column_chunks(part_ref.shape[3]), scratch)

    @pl.when(i == 0)
    def _():
        reducer.greet()
        vec_scr[...] = vectors(vec_ref)
        reducer.meet()
        for c in range(N_CHUNKS):
            reducer.start_core(c)

    def back(x_ref, grad_ref):
        input_grad(x_ref[...], dh_ref, d_ref, w_ref, vec_scr, grad_ref)

    pl.when(i < n_long)(lambda: back(long_ref, lg_ref))
    pl.when((i >= n_long) & (i < n_rows))(lambda: back(short_ref, sg_ref))

    @pl.when(i == 0)
    def _():
        for c in range(N_CHUNKS):
            reducer.start_chip(c)

    def finish(out):
        out[...] = h_ref[...] + combine_rows(col_ref, y_ref)

    pl.when((i >= n_rows) & (i < n_rows + n_long))(lambda: finish(lo_ref))
    pl.when((i >= n_rows + n_long) & (i < 2 * n_rows))(lambda: finish(so_ref))

    @pl.when(i == 2 * n_rows - 1)
    def _():
        for c in range(N_CHUNKS):
            reducer.start_plane(c)
        for c in range(N_CHUNKS):
            reducer.close(c)
        reducer.drain()


def last_stage(partial, long_x, short_x, d_h, d_qkv, dense, h, slot_col, y_back):
    n_dp, n_f, share, columns = partial.shape
    count, width = d_h.shape
    n_long, n_short = long_x.shape[0] // ROWS, short_x.shape[0] // ROWS
    n_rows = n_long + n_short
    slots = y_back.shape[0]
    row = pl.BlockSpec((ROWS, width), lambda i: (jnp.minimum(i, n_rows - 1), 0))
    late = lambda i: (jnp.clip(i - n_rows, 0, n_rows - 1), 0)
    return pl.pallas_call(
        functools.partial(last_kernel, n_long, n_rows),
        grid=(2 * n_rows,),
        in_specs=[
            constant(partial.shape),
            pl.BlockSpec((ROWS, width), lambda i: (jnp.minimum(i, n_long - 1), 0)),
            pl.BlockSpec((ROWS, width), lambda i: (jnp.clip(i - n_long, 0, n_short - 1), 0)),
            row,
            pl.BlockSpec((3, ROWS, width), lambda i: (0, jnp.minimum(i, n_rows - 1), 0)),
            constant((width, 3 * width)),
            pl.BlockSpec((width, LANES), lambda i: (0, 4 * width // LANES)),
            pl.BlockSpec((ROWS, width), late),
            pl.BlockSpec((ROWS, 1), late),
            constant((slots, width)),
        ],
        out_specs=[
            pl.BlockSpec((share, columns), lambda i: (0, 0)),
            pl.BlockSpec((ROWS, width), lambda i: (jnp.minimum(i, n_long - 1), 0)),
            pl.BlockSpec((ROWS, width), lambda i: (jnp.clip(i - n_long, 0, n_short - 1), 0)),
            pl.BlockSpec((ROWS, width), lambda i: (jnp.clip(i - n_rows, 0, n_long - 1), 0)),
            pl.BlockSpec(
                (ROWS, width), lambda i: (jnp.clip(i - n_rows - n_long, 0, n_short - 1), 0)
            ),
        ],
        out_shape=[
            jax.ShapeDtypeStruct((share, columns), F32),
            jax.ShapeDtypeStruct(long_x.shape, F32),
            jax.ShapeDtypeStruct(short_x.shape, F32),
            jax.ShapeDtypeStruct(long_x.shape, F32),
            jax.ShapeDtypeStruct(short_x.shape, F32),
        ],
        scratch_shapes=[pltpu.VMEM((8, width), F32)]
        + reducer_scratch(N_CHUNKS, n_dp, n_f, share, columns),
        compiler_params=params(collective_id=1, has_side_effects=True),
        cost_estimate=cost(2 * count * width * (3 * width + slots), 60e6),
        name="last_stage",
    )(partial, long_x, short_x, d_h, d_qkv, dense, dense, h, slot_col, y_back)


def close_kernel(
    n_long, n_rows, proj_ref, gv_ref, long_ref, short_ref, dp_ref, dh_ref, d_ref, w_ref, vec_ref,
    h_ref, col_ref, y_ref, out_ref, lg_ref, sg_ref, lo_ref, so_ref,
    vec_scr, rows_ref, part_ref, stat_ref, *scratch,
):
    i = pl.program_id(0)
    n_dp, n_f, share, columns = part_ref.shape
    width = dh_ref.shape[1]
    chunks = [slice(c * width, (c + 1) * width) for c in range(3)] + [slice(3 * width, columns)]
    reducer = Reducer(part_ref, out_ref, chunks, scratch)
    begin_back, begin_out = 3, 3 + n_rows

    def scatter(value, cut):
        for index in range(n_dp * n_f):
            part_ref[index // n_f, index % n_f, :, cut] = value[
                index * share : (index + 1) * share
            ].astype(BF16)

    @pl.when(i == 0)
    def _():
        reducer.greet()
        vec_scr[...] = vectors(vec_ref)
        part_ref[:, :, :, :width] = proj_ref[...]
        reducer.meet()
        reducer.start_core(0)
        n = long_ref.shape[0]
        for ref, first in ((long_ref, 0), (short_ref, n)):
            for start in range(0, ref.shape[0], ROWS):
                normed, _ = norm_parts(ref[start : start + ROWS, :])
                rows_ref[first + start : first + start + ROWS, :] = (
                    normed * vec_scr[0:1, :] + vec_scr[1:2, :]
                ).astype(BF16)
        stat_ref[...] = jnp.zeros_like(stat_ref)
        reducer.start_chip(0)

    for part in range(3):

        @pl.when(i == part)
        def _(part=part):
            value = dot(rows_ref[...], dp_ref[0], TN)
            scatter(value, slice((part + 1) * width, (part + 2) * width))
            weight = w_ref[:, part * width : (part + 1) * width].astype(F32)
            sums = jnp.sum(dp_ref[0].astype(F32), 0, keepdims=True)
            stat_ref[:, 0:1] = stat_ref[:, 0:1] + jnp.sum(weight * value, 1, keepdims=True)
            stat_ref[:, 1:2] = stat_ref[:, 1:2] + jnp.sum(weight * sums, 1, keepdims=True)
            if part == 2:
                found = norm1_grads(stat_ref[:, 0:1], stat_ref[:, 1:2], vec_ref, gv_ref)
                scatter(found.astype(F32), slice(4 * width, columns))
            reducer.start_core(part + 1)
            if part:
                reducer.start_chip(part)

    @pl.when(i == begin_back)
    def _():
        reducer.start_chip(3)

    def back(x_ref, index, grad_ref):
        rows = pl.ds(pl.multiple_of(index * ROWS, ROWS), ROWS)
        input_grad(x_ref[rows, :], dh_ref, d_ref, w_ref, vec_scr, grad_ref)

    j = i - begin_back
    pl.when((j >= 0) & (j < n_long))(lambda: back(long_ref, j, lg_ref))
    pl.when((j >= n_long) & (j < n_rows))(lambda: back(short_ref, j - n_long, sg_ref))

    def finish(out):
        out[...] = h_ref[...] + combine_rows(col_ref, y_ref)

    m = i - begin_out
    pl.when((m >= 0) & (m < n_long))(lambda: finish(lo_ref))
    pl.when((m >= n_long) & (m < n_rows))(lambda: finish(so_ref))

    pl.when(i == begin_back + 1)(lambda: reducer.start_plane(0))
    pl.when(i == begin_out - 1)(lambda: reducer.start_plane(1))
    pl.when(i == begin_out + n_rows - 2)(lambda: reducer.start_plane(2))

    @pl.when(i == begin_out + n_rows - 1)
    def _():
        reducer.start_plane(3)
        for c in range(4):
            reducer.close(c)
        reducer.drain()


def close_stage(grad_proj, grad_vec, long_x, short_x, d_h, d_qkv, dense, h, slot_col, y_back):
    n_dp, n_f, share = grad_proj.shape[:3]
    count, width = d_h.shape
    columns = 4 * width + LANES
    n_long, n_short = long_x.shape[0] // ROWS, short_x.shape[0] // ROWS
    n_rows = n_long + n_short
    slots = y_back.shape[0]
    step = lambda i, base, last: jnp.clip(i - base, 0, last)
    return pl.pallas_call(
        functools.partial(close_kernel, n_long, n_rows),
        grid=(3 + 2 * n_rows,),
        in_specs=[
            constant(grad_proj.shape),
            constant(grad_vec.shape),
            constant(long_x.shape),
            constant(short_x.shape),
            pl.BlockSpec((1, count, width), lambda i: (jnp.minimum(i, 2), 0, 0)),
            pl.BlockSpec((ROWS, width), lambda i: (step(i, 3, n_rows - 1), 0)),
            pl.BlockSpec((3, ROWS, width), lambda i: (0, step(i, 3, n_rows - 1), 0)),
            constant((width, 3 * width)),
            pl.BlockSpec((width, LANES), lambda i: (0, 4 * width // LANES)),
            pl.BlockSpec((ROWS, width), lambda i: (step(i, 3 + n_rows, n_rows - 1), 0)),
            pl.BlockSpec((ROWS, 1), lambda i: (step(i, 3 + n_rows, n_rows - 1), 0)),
            constant((slots, width)),
        ],
        out_specs=[
            pl.BlockSpec((share, columns), lambda i: (0, 0)),
            pl.BlockSpec((ROWS, width), lambda i: (step(i, 3, n_long - 1), 0)),
            pl.BlockSpec((ROWS, width), lambda i: (step(i, 3 + n_long, n_short - 1), 0)),
            pl.BlockSpec((ROWS, width), lambda i: (step(i, 3 + n_rows, n_long - 1), 0)),
            pl.BlockSpec((ROWS, width), lambda i: (step(i, 3 + n_rows + n_long, n_short - 1), 0)),
        ],
        out_shape=[
            jax.ShapeDtypeStruct((share, columns), F32),
            jax.ShapeDtypeStruct(long_x.shape, F32),
            jax.ShapeDtypeStruct(short_x.shape, F32),
            jax.ShapeDtypeStruct(long_x.shape, F32),
            jax.ShapeDtypeStruct(short_x.shape, F32),
        ],
        scratch_shapes=[
            pltpu.VMEM((8, width), F32),
            pltpu.VMEM((count, width), BF16),
            pltpu.VMEM((n_dp, n_f, share, columns), BF16),
            pltpu.VMEM((width, LANES), F32),
        ]
        + reducer_scratch(4, n_dp, n_f, share, columns),
        compiler_params=params(collective_id=4, has_side_effects=True),
        cost_estimate=cost(2 * count * width * (6 * width + slots), 60e6),
        name="close_stage",
    )(grad_proj, grad_vec, long_x, short_x, d_qkv, d_h, d_qkv, dense, dense, h, slot_col, y_back)


def ship_kernel(n_long, width, *refs):
    i = pl.program_id(0)
    arrays_in, (owned_ref, down_ref), rest = refs[:4], refs[4:6], refs[6:]
    arrays_out, (qkv_ref, proj_ref, vec_ref, grad_ref, pad_ref) = rest[:4], rest[4:]
    for first in (0, 2):

        @pl.when(i < n_long)
        def _():
            arrays_out[first][...] = arrays_in[first][...]

        @pl.when(i >= n_long)
        def _():
            arrays_out[first + 1][...] = arrays_in[first + 1][...]

    grad_ref[...] = down_ref[...].astype(F32)

    @pl.when(i == 0)
    def _():
        share = owned_ref.shape[0]
        qkv_ref[...] = owned_ref[:, width : 4 * width]
        pad_ref[...] = jnp.zeros_like(pad_ref)
        pad_ref[:share, :width] = owned_ref[:, :width]
        pad_ref[:share, width:] = owned_ref[:, 4 * width :]
        turned = jnp.transpose(pad_ref[...])
        proj_ref[...] = turned[:width, :share]
        vec_ref[...] = turned[width : width + 8, :share]


def ship(arrays, owned, grad_down):
    width = arrays[0].shape[1]
    n_long, n_short = arrays[0].shape[0] // ROWS, arrays[1].shape[0] // ROWS
    steps = n_long + n_short
    share = owned.shape[0]
    piece = pl.BlockSpec((grad_down.shape[0] // steps, width), lambda i: (i, 0))
    whole = lambda shape: pl.BlockSpec(shape, lambda i: (0, 0))
    return pl.pallas_call(
        functools.partial(ship_kernel, n_long, width),
        grid=(steps,),
        in_specs=long_short(width, n_long) * 2 + [constant(owned.shape), piece],
        out_specs=long_short(width, n_long) * 2
        + [whole((share, 3 * width)), whole((width, share)), whole((8, share)), piece],
        out_shape=[jax.ShapeDtypeStruct(a.shape, a.dtype) for a in arrays]
        + [
            jax.ShapeDtypeStruct((share, 3 * width), F32),
            jax.ShapeDtypeStruct((width, share), F32),
            jax.ShapeDtypeStruct((8, share), F32),
            jax.ShapeDtypeStruct(grad_down.shape, F32),
        ],
        scratch_shapes=[pltpu.VMEM((LANES, width + LANES), F32)],
        compiler_params=params(),
        cost_estimate=cost(0, sum(8 * a.size for a in arrays)),
        name="ship",
    )(*arrays, owned, grad_down)


def on_device(
    n_dp, n_f, long_x, short_x, long_len, short_len, expert_ids, ln1_gain, ln1_bias,
    w_qkv, w_proj, ln2_gain, ln2_bias, w_up, w_down, long_cot, short_cot,
):
    width = long_x.shape[2]
    share = w_qkv.shape[0]
    seqs = sequences(long_x.shape[:2], short_x.shape[:2])
    flat = lambda a: a.reshape(-1, width)
    xl, xs, gl, gs = flat(long_x), flat(short_x), flat(long_cot), flat(short_cot)
    n_long, n_short = xl.shape[0] // ROWS, xs.shape[0] // ROWS
    experts = n_f * w_up.shape[0]
    cap = 4 * expert_ids.shape[0] // (3 * experts)
    slots = experts * cap

    up = lax.all_gather(w_up, "dp", axis=2, tiled=True)[0]
    down = lax.all_gather(w_down, "dp", axis=1, tiled=True)[0]

    vec = jnp.stack([ln1_gain, ln1_bias, ln2_gain, ln2_bias], 1)
    own = jnp.concatenate(
        [w_qkv, w_proj.T, jnp.pad(vec, ((0, 0), (0, LANES - vec.shape[1])))], 1
    )
    dense, slot_col, slot_row, g_slots = gather_dense(
        own, expert_ids, gl, gs, n_dp, n_f, cap, slots
    )
    dense = dense.reshape(n_dp * n_f * share, own.shape[1])

    def exchange(rows):
        sent = lax.all_to_all(
            rows.reshape(n_f, cap, width), "fsdp", split_axis=0, concat_axis=0, tiled=True
        )
        return sent.reshape(slots, width)

    g_there = exchange(g_slots)
    qkv = make_qkv(xl, xs, dense)
    o, lse = attend(qkv, long_len, short_len, seqs)
    h, b_there, act, slope, grad_down = forward_experts(
        xl, xs, o, dense, slot_row, g_there, up, n_f, cap
    )
    grad_down = lax.psum_scatter(grad_down, "dp", scatter_dimension=0, tiled=True)
    y0, db0, gu0 = own_experts(
        lax.axis_index("dp").reshape(1), b_there, g_there, act, slope, up, w_down[0], n_f, cap
    )
    y, db_back, grad_up = back_experts(
        b_there, g_there, act, slope, up, down, y0, db0, gu0, n_dp, n_f, cap
    )
    db_back = db_back.reshape(slots, width)
    grad_up = lax.psum_scatter(grad_up, "dp", scatter_dimension=1, tiled=True).astype(F32)
    y = y.reshape(n_f, cap, width)
    d_h, d_o, grad_proj, grad_vec, y_back = hidden_back(
        h, slot_col, db_back, gl, gs, o, dense, y
    )
    d_qkv, y_back = attend_back(
        qkv, o, d_o, lse, long_len, short_len, seqs, y, y_back
    )
    y_back = y_back.reshape(slots, width)
    if share % 8 == 0:
        owned, long_grad, short_grad, long_out, short_out = close_stage(
            grad_proj.reshape(n_dp, n_f, share, width), grad_vec,
            xl, xs, d_h, d_qkv, dense, h, slot_col, y_back,
        )
    else:
        partial = dense_grads(xl, xs, d_qkv, dense, grad_proj, grad_vec)
        owned, long_grad, short_grad, long_out, short_out = last_stage(
            partial.reshape(n_dp, n_f, share, own.shape[1]),
            xl, xs, d_h, d_qkv, dense, h, slot_col, y_back,
        )
    (long_grad, short_grad, long_out, short_out, grad_qkv, grad_proj, grad_vec, grad_down) = ship(
        (long_grad, short_grad, long_out, short_out), owned, grad_down
    )
    return (
        long_out.reshape(long_x.shape),
        short_out.reshape(short_x.shape),
        long_grad.reshape(long_x.shape),
        short_grad.reshape(short_x.shape),
        grad_vec[0],
        grad_vec[1],
        grad_qkv,
        grad_proj,
        grad_vec[2],
        grad_vec[3],
        grad_up[None],
        grad_down[None],
    )


def solution(mesh):
    both = ("dp", "fsdp")
    return jax.shard_map(
        functools.partial(on_device, mesh.shape["dp"], mesh.shape["fsdp"]),
        mesh=mesh,
        in_specs=(
            P(both, None, None),
            P(both, None, None),
            P(both),
            P(both),
            P(both, None),
            P(both),
            P(both),
            P(both, None),
            P(None, both),
            P(both),
            P(both),
            P("fsdp", None, "dp"),
            P("fsdp", "dp", None),
            P(both, None, None),
            P(both, None, None),
        ),
        out_specs=(
            P(both, None, None),
            P(both, None, None),
            P(both, None, None),
            P(both, None, None),
            P(both),
            P(both),
            P(both, None),
            P(None, both),
            P(both),
            P(both),
            P("fsdp", None, "dp"),
            P("fsdp", "dp", None),
        ),
        check_vma=False,
    )
```

```python
import functools

import jax
import jax.numpy as jnp
from jax import lax
from jax.experimental import pallas as pl
from jax.experimental.pallas import tpu as pltpu
from jax.sharding import PartitionSpec as P

MESH = pl.DeviceIdType.MESH
HEAD_DIM = 64
EPSILON = 1e-05
MASKED = -1e30
BF16 = jnp.bfloat16
F32 = jnp.float32
LANES = 128
ROWS = 512
BLOCK = 256
ATTEND = 512
ATTEND_BACK = 512
VMEM_LIMIT = 60 * 2**20
N_CHUNKS = 3

NN = (((1,), (0,)), ((), ()))
NT = (((1,), (1,)), ((), ()))
TN = (((0,), (0,)), ((), ()))


def dot(a, b, dims=NN, precision=None):
    return lax.dot_general(a, b, dims, preferred_element_type=F32, precision=precision)


def params(**extra):
    return pltpu.CompilerParams(vmem_limit_bytes=VMEM_LIMIT, **extra)


def cost(flops, moved, exps=0):
    return pl.CostEstimate(flops=int(flops), bytes_accessed=int(moved), transcendentals=int(exps))


def constant(shape):
    return pl.BlockSpec(shape, lambda *_: (0,) * len(shape), pipeline_mode=pl.Buffered(1))


def norm_parts(inputs):
    average = jnp.mean(inputs, -1, keepdims=True)
    centred = inputs - average
    inv_scale = lax.rsqrt(jnp.mean(centred * centred, -1, keepdims=True) + EPSILON)
    return centred * inv_scale, inv_scale


def norm_back(grad_normed, normed, inv_scale):
    centre_term = jnp.mean(grad_normed, -1, keepdims=True)
    slope_term = jnp.mean(grad_normed * normed, -1, keepdims=True)
    return inv_scale * (grad_normed - centre_term - normed * slope_term)


def vectors(vec_ref):
    return jnp.transpose(vec_ref[...].astype(F32))[:8]


def long_short(width, n_long):
    return [
        pl.BlockSpec((ROWS, width), lambda i: (jnp.minimum(i, n_long - 1), 0)),
        pl.BlockSpec((ROWS, width), lambda i: (jnp.maximum(i - n_long, 0), 0)),
    ]


def column_chunks(columns):
    tiles = columns // LANES
    edges = [LANES * (tiles * c // N_CHUNKS) for c in range(N_CHUNKS + 1)]
    return [slice(lo, hi) for lo, hi in zip(edges, edges[1:])]


def gather_kernel(
    n_dp, n_f, cap, own_ref, ids_ref, long_ref, short_ref, out_ref, col_ref, row_ref, slots_ref,
    rows_ref, z_send, z_recv, p_send, p_recv, c_send, c_recv, l_sem,
):
    z = lax.axis_index("dp")
    f = lax.axis_index("fsdp")
    half = n_f // 2
    partner = f + 1 - 2 * lax.rem(f, 2)
    barrier = pltpu.get_barrier_semaphore()
    for k in range(1, n_dp):
        pl.semaphore_signal(barrier, 1, device_id=(lax.rem(z + k, n_dp), f), device_id_type=MESH)
    for k in range(1, half):
        pl.semaphore_signal(barrier, 1, device_id=(z, lax.rem(f + 2 * k, n_f)), device_id_type=MESH)
    pl.semaphore_signal(barrier, 1, device_id=(z, partner), device_id_type=MESH)
    local = pltpu.make_async_copy(own_ref, out_ref.at[z, f], l_sem)
    local.start()
    pl.semaphore_wait(barrier, n_dp - 1 + half)

    chunks = column_chunks(own_ref.shape[1])
    z_copies, p_copies, c_copies = [], [], []

    def send_z(c):
        for k in range(1, n_dp):
            copy = pltpu.make_async_remote_copy(
                own_ref.at[:, chunks[c]], out_ref.at[z, f, :, chunks[c]],
                z_send.at[c, k], z_recv.at[c, k],
                device_id=(lax.rem(z + k, n_dp), f), device_id_type=MESH,
            )
            copy.start()
            z_copies.append(copy)

    def send_p(c):
        for k in range(1, n_dp):
            z_copies[c * (n_dp - 1) + k - 1].wait_recv()
        for k in range(1, half):
            copy = pltpu.make_async_remote_copy(
                out_ref.at[:, f, :, chunks[c]], out_ref.at[:, f, :, chunks[c]],
                p_send.at[c, k], p_recv.at[c, k],
                device_id=(z, lax.rem(f + 2 * k, n_f)), device_id_type=MESH,
            )
            copy.start()
            p_copies.append(copy)

    def send_c(c):
        for k in range(half):
            if k:
                p_copies[c * (half - 1) + k - 1].wait_recv()
            column = lax.rem(f + n_f - 2 * k, n_f)
            copy = pltpu.make_async_remote_copy(
                out_ref.at[:, column, :, chunks[c]], out_ref.at[:, column, :, chunks[c]],
                c_send.at[c, k], c_recv.at[c, k],
                device_id=(z, partner), device_id_type=MESH,
            )
            copy.start()
            c_copies.append(copy)

    def fill(block, carry):
        start = pl.multiple_of(block * BLOCK, BLOCK)
        slots_ref[pl.ds(start, BLOCK), :] = dispatch_block(row_ref, rows_ref[...], start, BLOCK)
        return carry

    n_blocks = slots_ref.shape[0] // BLOCK
    for c in range(len(chunks)):
        send_z(c)
    number_slots(cap, ids_ref, col_ref, row_ref)
    n_long = long_ref.shape[0]
    rows_ref[:n_long, :] = long_ref[...].astype(BF16)
    rows_ref[n_long:, :] = short_ref[...].astype(BF16)
    local.wait()
    for c in range(len(chunks)):
        send_p(c)
        lax.fori_loop(c * n_blocks // len(chunks), (c + 1) * n_blocks // len(chunks), fill, 0)
    for c in range(len(chunks)):
        send_c(c)
    for copy in c_copies:
        copy.wait_recv()
    for copy in z_copies + p_copies + c_copies:
        copy.wait_send()


def gather_dense(own, ids, long_cot, short_cot, n_dp, n_f, cap, slots):
    count, width = ids.shape[0], long_cot.shape[1]
    vmem = pl.BlockSpec(memory_space=pltpu.VMEM)
    return pl.pallas_call(
        functools.partial(gather_kernel, n_dp, n_f, cap),
        out_shape=[
            jax.ShapeDtypeStruct((n_dp, n_f) + own.shape, own.dtype),
            jax.ShapeDtypeStruct((count, 1), jnp.int32),
            jax.ShapeDtypeStruct((8, count), jnp.int32),
            jax.ShapeDtypeStruct((slots, width), BF16),
        ],
        in_specs=[pl.BlockSpec(memory_space=pl.ANY), vmem, vmem, vmem],
        out_specs=[pl.BlockSpec(memory_space=pl.ANY), vmem, vmem, vmem],
        scratch_shapes=[
            pltpu.VMEM((count, width), BF16),
            pltpu.SemaphoreType.DMA((N_CHUNKS, n_dp)),
            pltpu.SemaphoreType.DMA((N_CHUNKS, n_dp)),
            pltpu.SemaphoreType.DMA((N_CHUNKS, n_f // 2)),
            pltpu.SemaphoreType.DMA((N_CHUNKS, n_f // 2)),
            pltpu.SemaphoreType.DMA((N_CHUNKS, n_f // 2)),
            pltpu.SemaphoreType.DMA((N_CHUNKS, n_f // 2)),
            pltpu.SemaphoreType.DMA,
        ],
        compiler_params=params(collective_id=0, has_side_effects=True),
        cost_estimate=cost(0, 100e6),
        name="gather_dense",
    )(own, ids, long_cot, short_cot)


def dispatch_block(slot_row_ref, rows, first, size):
    slot_id = first + lax.broadcasted_iota(jnp.int32, (size, 1), 0)
    chosen = (slot_row_ref[0:1, :] == slot_id).astype(F32).astype(BF16)
    return dot(chosen, rows).astype(BF16)


def number_slots(cap, ids_ref, col_ref, row_ref):
    count = ids_ref.shape[0]
    lane = lax.broadcasted_iota(jnp.int32, (1, LANES), 1)
    onehot = (ids_ref[...] == lane).astype(F32)
    onehot_low = onehot.astype(BF16)
    col = lax.broadcasted_iota(jnp.int32, (1, count), 1)
    base = (lane * cap).astype(F32)
    ones = jnp.ones((8, LANES), F32)
    for start in range(0, count, ROWS):
        row = start + lax.broadcasted_iota(jnp.int32, (ROWS, 1), 0)
        before = dot((col < row).astype(F32).astype(BF16), onehot_low)
        picked = (before + base) * onehot[start : start + ROWS]
        col_ref[start : start + ROWS, :] = jnp.sum(picked, 1, keepdims=True).astype(jnp.int32)
        row_ref[:, start : start + ROWS] = dot(
            ones, picked, NT, precision=lax.Precision.HIGHEST
        ).astype(jnp.int32)


def peers(n_f):
    f = lax.axis_index("fsdp")

    def partner(k):
        place, digit = 0, 1
        while digit < n_f:
            place = place + digit * lax.rem(f // digit + k // digit, 2)
            digit *= 2
        return place

    return f, partner


def greet(n_f, to):
    z = lax.axis_index("dp")
    barrier = pltpu.get_barrier_semaphore()
    for k in range(1, n_f):
        pl.semaphore_signal(barrier, 1, device_id=(z, to(k)), device_id_type=MESH)


class Homeward:
    def __init__(self, n_f, ks, y_ref, yb_ref, send, recv):
        self.f, self.to = peers(n_f)
        self.n_f, self.ks = n_f, ks
        self.z = lax.axis_index("dp")
        self.y, self.yb, self.send, self.recv = y_ref, yb_ref, send, recv

    def transfer(self, k):
        return pltpu.make_async_remote_copy(
            self.y.at[self.to(k)], self.yb.at[self.f], self.send.at[k], self.recv.at[k],
            device_id=(self.z, self.to(k)), device_id_type=MESH,
        )

    def begin(self):
        greet(self.n_f, self.to)

    def launch(self):
        pl.semaphore_wait(pltpu.get_barrier_semaphore(), self.n_f - 1)
        for k in self.ks:
            self.transfer(k).start()

    def end(self):
        for k in self.ks:
            self.transfer(k).wait_recv()
            self.transfer(k).wait_send()


def qkv_kernel(n_long, width, long_ref, short_ref, w_ref, vec_ref, qkv_ref, vec_scr):
    i = pl.program_id(0)

    @pl.when(i == 0)
    def _():
        vec_scr[...] = vectors(vec_ref)

    def body(x_ref):
        normed, _ = norm_parts(x_ref[...])
        rows = (normed * vec_scr[0:1, :] + vec_scr[1:2, :]).astype(BF16)
        for part in range(3):
            cut = slice(part * width, (part + 1) * width)
            out = dot(rows, w_ref[:, cut])
            if part == 0:
                out = out * HEAD_DIM ** (-0.5)
            qkv_ref[:, cut] = out.astype(BF16)

    pl.when(i < n_long)(lambda: body(long_ref))
    pl.when(i >= n_long)(lambda: body(short_ref))


def make_qkv(long_x, short_x, dense):
    width = long_x.shape[1]
    n_long, n_short = long_x.shape[0] // ROWS, short_x.shape[0] // ROWS
    count = long_x.shape[0] + short_x.shape[0]
    return pl.pallas_call(
        functools.partial(qkv_kernel, n_long, width),
        grid=(n_long + n_short,),
        in_specs=long_short(width, n_long)
        + [
            constant((width, 3 * width)),
            pl.BlockSpec((width, LANES), lambda i: (0, 4 * width // LANES)),
        ],
        out_specs=pl.BlockSpec((ROWS, 3 * width), lambda i: (i, 0)),
        out_shape=jax.ShapeDtypeStruct((count, 3 * width), BF16),
        scratch_shapes=[pltpu.VMEM((8, width), F32)],
        compiler_params=params(),
        cost_estimate=cost(6 * count * width * width, count * width * 10 + 6 * width * width),
        name="make_qkv",
    )(long_x, short_x, dense, dense)


def sequences(long_shape, short_shape):
    found = []
    start = 0
    for which, (number, length) in enumerate((long_shape, short_shape)):
        for index in range(number):
            found.append((start, length, which, index))
            start += length
    return found


def head_masks():
    lane = lax.broadcasted_iota(jnp.int32, (1, LANES), 1)
    return (lane < HEAD_DIM, lane >= HEAD_DIM)


def marked(q, k, valid, first, masks, lane):
    key_pos = first + lax.broadcasted_iota(jnp.int32, (k.shape[0], 1), 0)
    bias = jnp.where(key_pos < valid, 0.0, MASKED).astype(BF16)
    found = []
    for head in range(2):
        spare = HEAD_DIM * (1 - head)
        qh = jnp.where(masks[head], q, jnp.where(lane == spare, 1.0, 0.0).astype(BF16))
        kh = jnp.where(masks[head], k, jnp.where(lane == spare, bias, jnp.zeros_like(bias)))
        found.append((qh, kh))
    return found


def attend_kernel(seqs, long_len, short_len, q_ref, k_ref, v_ref, o_ref, lse_ref):
    pair = pl.program_id(0)
    masks = head_masks()
    lane = lax.broadcasted_iota(jnp.int32, (1, LANES), 1)

    @pl.when(pair == 0)
    def _():
        lse_ref[...] = jnp.zeros_like(lse_ref)

    causal = lax.broadcasted_iota(jnp.int32, (ATTEND, ATTEND), 0) <= lax.broadcasted_iota(
        jnp.int32, (ATTEND, ATTEND), 1
    )
    upper = lax.broadcasted_iota(jnp.int32, (LANES, 1), 0) < HEAD_DIM
    for start, length, which, index in seqs:
        valid = (short_len if which else long_len)[index]
        rows = slice(start, start + length)
        heads = marked(q_ref[rows, :], k_ref[rows, :], valid, 0, masks, lane)
        v = jnp.transpose(v_ref[rows, :].astype(F32))
        values = [
            jnp.where(upper, v, 1.0).astype(BF16),
            jnp.where(upper, 1.0, v).astype(BF16),
        ]
        for first in range(0, length, ATTEND):
            last = first + ATTEND
            outs = []
            for head, (qh, kh) in enumerate(heads):
                qb = qh[first:last]
                near = dot(kh[first:last], qb, NT)
                near = jnp.where(causal, near, MASKED)
                top = jnp.max(near, 0, keepdims=True)
                if first:
                    far = dot(kh[:first], qb, NT)
                    top = jnp.maximum(top, jnp.max(far, 0, keepdims=True))
                out = dot(values[head][:, first:last], jnp.exp(near - top).astype(BF16))
                if first:
                    out = out + dot(values[head][:, :first], jnp.exp(far - top).astype(BF16))
                total = out[LANES - 1 : LANES] if head == 0 else out[0:1]
                outs.append(out * (1.0 / total))
                lse_ref[pl.ds(2 * pair + head, 1), start + first : start + last] = top + jnp.log(
                    total
                )
            o_ref[start + first : start + last, :] = jnp.transpose(
                jnp.where(upper, outs[0], outs[1])
            ).astype(BF16)


def attend(qkv, long_len, short_len, seqs):
    count, width = qkv.shape[0], qkv.shape[1] // 3
    pairs = width // LANES
    return pl.pallas_call(
        functools.partial(attend_kernel, seqs),
        grid=(pairs,),
        in_specs=[pl.BlockSpec(memory_space=pltpu.SMEM)] * 2
        + [
            pl.BlockSpec((count, LANES), lambda i: (0, i)),
            pl.BlockSpec((count, LANES), lambda i: (0, i + pairs)),
            pl.BlockSpec((count, LANES), lambda i: (0, i + 2 * pairs)),
        ],
        out_specs=[
            pl.BlockSpec((count, LANES), lambda i: (0, i)),
            pl.BlockSpec((LANES, count), lambda i: (0, 0)),
        ],
        out_shape=[
            jax.ShapeDtypeStruct((count, width), BF16),
            jax.ShapeDtypeStruct((LANES, count), F32),
        ],
        compiler_params=params(),
        cost_estimate=cost(16e9, 8 * count * width, 10e6),
        name="attend",
    )(long_len, short_len, qkv, qkv, qkv)


def attend_back_kernel(
    seqs, n_f, long_len, short_len, q_ref, k_ref, v_ref, o_ref, do_ref, lse_ref, y_ref, _,
    d_ref, yb_ref, dkt_ref, dvt_ref, lse_scr, send, recv, l_sem,
):
    pair = pl.program_id(0)
    masks = head_masks()
    lane = lax.broadcasted_iota(jnp.int32, (1, LANES), 1)

    home = Homeward(n_f, range(3 * n_f // 4, n_f), y_ref, yb_ref, send, recv)
    keep = pltpu.make_async_copy(y_ref.at[home.f], yb_ref.at[home.f], l_sem)

    @pl.when(pair == 0)
    def _():
        home.begin()
        keep.start()
        lse_scr[...] = jnp.transpose(lse_ref[...])
        home.launch()

    causal = lax.broadcasted_iota(jnp.int32, (ATTEND_BACK, ATTEND_BACK), 1) <= (
        lax.broadcasted_iota(jnp.int32, (ATTEND_BACK, ATTEND_BACK), 0)
    )
    for start, length, which, index in seqs:
        valid = (short_len if which else long_len)[index]
        rows = slice(start, start + length)
        q, k, v, do = q_ref[rows, :], k_ref[rows, :], v_ref[rows, :], do_ref[rows, :]
        heads = marked(q, k, valid, 0, masks, lane)
        q_t = jnp.transpose(q.astype(F32)).astype(BF16)
        do_t = jnp.transpose(do.astype(F32)).astype(BF16)
        both = do.astype(F32) * o_ref[rows, :].astype(F32)
        lse_all = lse_scr[rows, :]
        dkt_ref[...] = jnp.zeros_like(dkt_ref)
        dvt_ref[...] = jnp.zeros_like(dvt_ref)
        for first in range(0, length, ATTEND_BACK):
            last = first + ATTEND_BACK
            dqs = []
            for head, (qh, kh) in enumerate(heads):
                part = slice(HEAD_DIM * head, HEAD_DIM * (head + 1))
                doh = jnp.where(masks[head], do[first:last], jnp.zeros_like(do[first:last]))
                lse = jnp.sum(
                    jnp.where(lane == 2 * pair + head, lse_all[first:last], 0.0), 1, keepdims=True
                )
                delta = jnp.sum(jnp.where(masks[head], both[first:last], 0.0), 1, keepdims=True)
                dq = jnp.zeros((ATTEND_BACK, LANES), F32)
                for keys in (slice(0, first), slice(first, last)):
                    if keys.stop == keys.start:
                        continue
                    p = jnp.exp(dot(qh[first:last], kh[keys], NT) - lse)
                    if keys.start == first:
                        p = jnp.where(causal, p, 0.0)
                    dp = dot(doh, v[keys], NT)
                    ds = (p * (dp - delta)).astype(BF16)
                    dvt_ref[part, keys] = dvt_ref[part, keys] + dot(
                        do_t[part, first:last], p.astype(BF16)
                    )
                    dkt_ref[part, keys] = dkt_ref[part, keys] + dot(q_t[part, first:last], ds)
                    dq = dq + dot(ds, k[keys])
                dqs.append(dq)
            d_ref[0, start + first : start + last, :] = (
                jnp.where(masks[0], dqs[0], dqs[1]) * HEAD_DIM ** (-0.5)
            ).astype(BF16)
        d_ref[1, rows, :] = jnp.transpose(dkt_ref[:, :length]).astype(BF16)
        d_ref[2, rows, :] = jnp.transpose(dvt_ref[:, :length]).astype(BF16)

    @pl.when(pair == pl.num_programs(0) - 1)
    def _():
        keep.wait()
        home.end()


def attend_back(qkv, o, d_o, lse, long_len, short_len, seqs, y, y_back):
    count, width = o.shape
    n_f = y.shape[0]
    pairs = width // LANES
    longest = max(length for _, length, _, _ in seqs)
    one = pl.BlockSpec((count, LANES), lambda i: (0, i))
    return pl.pallas_call(
        functools.partial(attend_back_kernel, seqs, n_f),
        grid=(pairs,),
        in_specs=[pl.BlockSpec(memory_space=pltpu.SMEM)] * 2
        + [
            one,
            pl.BlockSpec((count, LANES), lambda i: (0, i + pairs)),
            pl.BlockSpec((count, LANES), lambda i: (0, i + 2 * pairs)),
            one,
            one,
            constant((LANES, count)),
            pl.BlockSpec(memory_space=pl.ANY),
            pl.BlockSpec(memory_space=pl.ANY),
        ],
        out_specs=[
            pl.BlockSpec((3, count, LANES), lambda i: (0, 0, i)),
            pl.BlockSpec(memory_space=pl.ANY),
        ],
        input_output_aliases={9: 1},
        out_shape=[
            jax.ShapeDtypeStruct((3, count, width), BF16),
            jax.ShapeDtypeStruct(y.shape, BF16),
        ],
        scratch_shapes=[
            pltpu.VMEM((LANES, longest), F32),
            pltpu.VMEM((LANES, longest), F32),
            pltpu.VMEM((count, LANES), F32),
            pltpu.SemaphoreType.DMA((n_f,)),
            pltpu.SemaphoreType.DMA((n_f,)),
            pltpu.SemaphoreType.DMA,
        ],
        compiler_params=params(collective_id=5, has_side_effects=True),
        cost_estimate=cost(40e9, 16 * count * width, 10e6),
        name="attend_back",
    )(long_len, short_len, qkv, qkv, qkv, o, d_o, lse, y, y_back)


def gelu_parts(pre):
    scale = 0.7978845608028654
    square = pre * pre
    flat = jnp.tanh(scale * pre * (1.0 + 0.044715 * square))
    half = 0.5 * (1.0 + flat)
    slope = half + (0.5 * scale) * pre * (1.0 - flat * flat) * (1.0 + 0.134145 * square)
    return half * pre, slope


def forward_kernel(
    n_f, n_long, n_rows, long_ref, short_ref, o_ref, w_ref, vec_ref, row_ref, g_ref, up_ref,
    h_ref, there_ref, act_ref, slope_ref, gd_ref,
    rows_ref, vec_scr, out_buf, in_buf, all_ref, send, recv,
):
    i = pl.program_id(0)
    z = lax.axis_index("dp")
    f, partner = peers(n_f)
    cap, width = out_buf.shape[1:]
    n_up = n_rows + n_f
    n_down = n_up + n_f
    barrier = pltpu.get_barrier_semaphore()

    def transfer(k):
        return pltpu.make_async_remote_copy(
            out_buf.at[k], in_buf.at[f], send.at[k], recv.at[k],
            device_id=(z, partner(k)), device_id_type=MESH,
        )

    @pl.when(i == 0)
    def _():
        greet(n_f, partner)
        vec_scr[...] = vectors(vec_ref)

    def body(x_ref):
        hidden = x_ref[...] + dot(o_ref[...], w_ref[...], NT)
        h_ref[...] = hidden
        normed, _ = norm_parts(hidden)
        rows_ref[pl.ds(pl.multiple_of(i * ROWS, ROWS), ROWS), :] = (
            normed * vec_scr[2:3, :] + vec_scr[3:4, :]
        ).astype(BF16)

    pl.when(i < n_long)(lambda: body(long_ref))
    pl.when((i >= n_long) & (i < n_rows))(lambda: body(short_ref))

    @pl.when(i == n_rows)
    def _():
        pl.semaphore_wait(barrier, n_f - 1)

    @pl.when((i >= n_rows) & (i < n_up - 1))
    def _():
        k = i - n_rows + 1
        out_buf[k] = dispatch_block(row_ref, rows_ref[...], partner(k) * cap, cap)
        transfer(k).start()

    @pl.when(i == n_up - 1)
    def _():
        in_buf[f] = dispatch_block(row_ref, rows_ref[...], f * cap, cap)

    @pl.when((i > n_up) & (i < n_down))
    def _():
        transfer(i - n_up).wait_recv()

    @pl.when((i >= n_up) & (i < n_down))
    def _():
        origin = partner(i - n_up)
        rows = in_buf[origin]
        here = pl.ds(pl.multiple_of(origin * cap, cap), cap)
        for first in range(0, up_ref.shape[1], width):
            cut = slice(first, first + width)
            act, slope = gelu_parts(dot(rows, up_ref[:, cut]))
            act = act.astype(BF16)
            act_ref[:, cut] = act
            slope_ref[:, cut] = slope.astype(BF16)
            all_ref[here, cut] = act
        there_ref[here, :] = rows

    @pl.when(i >= n_down)
    def _():
        cut = pl.ds(pl.multiple_of((i - n_down) * width, width), width)
        gd_ref[...] = dot(all_ref[:, cut], g_ref[...], TN).astype(BF16)

    @pl.when(i == pl.num_programs(0) - 1)
    def _():
        for k in range(1, n_f):
            transfer(k).wait_send()


def forward_experts(long_x, short_x, o, dense, slot_row, g_there, up, n_f, cap):
    width = long_x.shape[1]
    hidden = up.shape[1]
    n_long, n_short = long_x.shape[0] // ROWS, short_x.shape[0] // ROWS
    n_rows = n_long + n_short
    n_up = n_rows + n_f
    n_down = n_up + n_f
    n_hidden = hidden // width
    slots = n_f * cap
    count = o.shape[0]
    tile = pl.BlockSpec((cap, hidden), lambda i: (jnp.clip(i - n_up, 0, n_f - 1), 0))
    return pl.pallas_call(
        functools.partial(forward_kernel, n_f, n_long, n_rows),
        grid=(n_down + n_hidden,),
        in_specs=[
            pl.BlockSpec((ROWS, width), lambda i: (jnp.minimum(i, n_long - 1), 0)),
            pl.BlockSpec((ROWS, width), lambda i: (jnp.clip(i - n_long, 0, n_short - 1), 0)),
            pl.BlockSpec((ROWS, width), lambda i: (jnp.minimum(i, n_rows - 1), 0)),
            pl.BlockSpec((width, width), lambda i: (0, 3), pipeline_mode=pl.Buffered(1)),
            pl.BlockSpec((width, LANES), lambda i: (0, 4 * width // LANES)),
            constant((8, count)),
            constant((slots, width)),
            constant((width, hidden)),
        ],
        out_specs=[
            pl.BlockSpec((ROWS, width), lambda i: (jnp.minimum(i, n_rows - 1), 0)),
            pl.BlockSpec((slots, width), lambda i: (0, 0)),
            tile,
            tile,
            pl.BlockSpec((width, width), lambda i: (jnp.clip(i - n_down, 0, n_hidden - 1), 0)),
        ],
        out_shape=[
            jax.ShapeDtypeStruct((count, width), F32),
            jax.ShapeDtypeStruct((slots, width), BF16),
            jax.ShapeDtypeStruct((slots, hidden), BF16),
            jax.ShapeDtypeStruct((slots, hidden), BF16),
            jax.ShapeDtypeStruct((hidden, width), BF16),
        ],
        scratch_shapes=[
            pltpu.VMEM((count, width), BF16),
            pltpu.VMEM((8, width), F32),
            pltpu.VMEM((n_f, cap, width), BF16),
            pltpu.VMEM((n_f, cap, width), BF16),
            pltpu.VMEM((slots, hidden), BF16),
            pltpu.SemaphoreType.DMA((n_f,)),
            pltpu.SemaphoreType.DMA((n_f,)),
        ],
        compiler_params=params(collective_id=2, has_side_effects=True),
        cost_estimate=cost(
            2 * slots * width * (count + 2 * hidden), 60e6, slots * hidden
        ),
        name="forward_experts",
    )(long_x, short_x, o, dense, dense, slot_row, g_there, up)


def own_kernel(
    n_f, z_ref, b_ref, g_ref, act_ref, slope_ref, up_ref, down_ref, y_ref, db_ref, gu_ref, all_ref
):
    i = pl.program_id(0)
    _, partner = peers(n_f)
    cap = y_ref.shape[0]

    @pl.when(i < n_f)
    def _():
        here = pl.ds(pl.multiple_of(partner(i) * cap, cap), cap)
        d_act = dot(g_ref[here, :], down_ref[...], NT)
        d_pre = (d_act * slope_ref[...].astype(F32)).astype(BF16)
        all_ref[here, :] = d_pre
        db_ref[...] = dot(d_pre, up_ref[...], NT)
        y_ref[...] = dot(act_ref[...], down_ref[...])

    @pl.when(i >= n_f)
    def _():
        gu_ref[...] = dot(b_ref[...], all_ref[...], TN).astype(BF16)


def own_experts(z, b_there, g_there, act, slope, up, own_down, n_f, cap):
    slots, width = b_there.shape
    piece = own_down.shape[0]
    tile = pl.BlockSpec((cap, piece), lambda i, z: (jnp.minimum(i, n_f - 1), z[0]))
    out = pl.BlockSpec((cap, width), lambda i, z: (jnp.minimum(i, n_f - 1), 0))
    return pl.pallas_call(
        functools.partial(own_kernel, n_f),
        grid_spec=pltpu.PrefetchScalarGridSpec(
            num_scalar_prefetch=1,
            grid=(n_f + 1,),
            in_specs=[
                constant((slots, width)),
                constant((slots, width)),
                tile,
                tile,
                pl.BlockSpec((width, piece), lambda i, z: (0, z[0])),
                constant((piece, width)),
            ],
            out_specs=[out, out, pl.BlockSpec((width, piece), lambda i, z: (0, 0))],
            scratch_shapes=[pltpu.VMEM((slots, piece), BF16)],
        ),
        out_shape=[
            jax.ShapeDtypeStruct((slots, width), F32),
            jax.ShapeDtypeStruct((slots, width), F32),
            jax.ShapeDtypeStruct((width, piece), BF16),
        ],
        compiler_params=params(),
        cost_estimate=cost(8 * slots * width * piece, 30e6),
        name="own_experts",
    )(z, b_there, g_there, act, slope, up, own_down)


def back_kernel(
    n_dp, n_f, b_ref, g_ref, act_ref, slope_ref, up_ref, down_ref, y0_ref, db0_ref, gu0_ref,
    y_ref, db_ref, gu_ref, out_buf, all_ref, send, recv, l_sem,
):
    i = pl.program_id(0)
    z = lax.axis_index("dp")
    f, partner = peers(n_f)
    cap, width = out_buf.shape[1:]
    piece = gu_ref.shape[1]
    barrier = pltpu.get_barrier_semaphore()

    def transfer(k):
        return pltpu.make_async_remote_copy(
            out_buf.at[k], db_ref.at[f], send.at[k], recv.at[k],
            device_id=(z, partner(k)), device_id_type=MESH,
        )

    def other(m):
        return pl.ds(pl.multiple_of(lax.rem(z + m, n_dp) * piece, piece), piece)

    keep = pltpu.make_async_copy(out_buf.at[0], db_ref.at[f], l_sem)

    @pl.when(i == 0)
    def _():
        greet(n_f, partner)

    @pl.when(i < n_f)
    def _():
        k = n_f - 1 - i
        here = pl.ds(pl.multiple_of(partner(k) * cap, cap), cap)
        g = g_ref[here, :]
        d_b = db0_ref[...]
        for m in range(1, n_dp):
            d_act = dot(g, down_ref[other(m), :], NT)
            d_pre = (d_act * slope_ref[:, other(m)].astype(F32)).astype(BF16)
            all_ref[here, other(m)] = d_pre
            d_b = d_b + dot(d_pre, up_ref[:, other(m)], NT)
        out_buf[k] = d_b.astype(BF16)

    @pl.when(i == 0)
    def _():
        pl.semaphore_wait(barrier, n_f - 1)

    @pl.when(i < n_f - 1)
    def _():
        transfer(n_f - 1 - i).start()

    @pl.when(i == n_f - 1)
    def _():
        keep.start()

    @pl.when(i < n_f)
    def _():
        here = pl.ds(pl.multiple_of(partner(n_f - 1 - i) * cap, cap), cap)
        y = y0_ref[...]
        for m in range(1, n_dp):
            y = y + dot(act_ref[:, other(m)], down_ref[other(m), :])
        y_ref[here, :] = y.astype(BF16)

    @pl.when((i >= n_f) & (i - n_f == z))
    def _():
        gu_ref[...] = gu0_ref[...]

    @pl.when((i >= n_f) & (i - n_f != z))
    def _():
        cut = pl.ds(pl.multiple_of((i - n_f) * piece, piece), piece)
        gu_ref[...] = dot(b_ref[...], all_ref[:, cut], TN).astype(BF16)

    @pl.when(i == pl.num_programs(0) - 1)
    def _():
        keep.wait()
        for k in range(1, n_f):
            transfer(k).wait_recv()
        for k in range(1, n_f):
            transfer(k).wait_send()


def back_experts(b_there, g_there, act, slope, up, down, y0, db0, gu0, n_dp, n_f, cap):
    slots, width = b_there.shape
    hidden = up.shape[1]
    piece = hidden // n_dp
    tile = pl.BlockSpec((cap, hidden), lambda i: (jnp.maximum(n_f - 1 - i, 0), 0))
    begun = pl.BlockSpec((cap, width), lambda i: (jnp.maximum(n_f - 1 - i, 0), 0))
    return pl.pallas_call(
        functools.partial(back_kernel, n_dp, n_f),
        grid=(n_f + n_dp,),
        in_specs=[
            constant((slots, width)),
            constant((slots, width)),
            tile,
            tile,
            constant((width, hidden)),
            constant((hidden, width)),
            begun,
            begun,
            constant((width, piece)),
        ],
        out_specs=[
            pl.BlockSpec((slots, width), lambda i: (0, 0)),
            pl.BlockSpec(memory_space=pl.ANY),
            pl.BlockSpec((width, piece), lambda i: (0, jnp.maximum(i - n_f, 0))),
        ],
        out_shape=[
            jax.ShapeDtypeStruct((slots, width), BF16),
            jax.ShapeDtypeStruct((n_f, cap, width), BF16),
            jax.ShapeDtypeStruct((width, hidden), BF16),
        ],
        scratch_shapes=[
            pltpu.VMEM((n_f, cap, width), BF16),
            pltpu.VMEM((slots, hidden), BF16),
            pltpu.SemaphoreType.DMA((n_f,)),
            pltpu.SemaphoreType.DMA((n_f,)),
            pltpu.SemaphoreType.DMA,
        ],
        compiler_params=params(collective_id=3, has_side_effects=True),
        cost_estimate=cost(6 * slots * width * hidden, 60e6),
        name="back_experts",
    )(b_there, g_there, act, slope, up, down, y0, db0, gu0)


def combine_rows(col_ref, slots_ref):
    slot_id = lax.broadcasted_iota(jnp.int32, (1, slots_ref.shape[0]), 1)
    chosen = (col_ref[...] == slot_id).astype(F32).astype(BF16)
    return dot(chosen, slots_ref[...])


def hidden_back_kernel(
    n_f, n_long, n_rows, h_ref, col_ref, db_ref, long_ref, short_ref, o_ref, w_ref, vec_ref, y_ref,
    dh_ref, do_ref, gp_ref, gv_ref, yb_ref, acc_ref, vec_scr, send, recv,
):
    i = pl.program_id(0)
    home = Homeward(n_f, range(1, 3 * n_f // 4), y_ref, yb_ref, send, recv)
    pl.when(i == 0)(home.begin)

    @pl.when(i == 0)
    def _():
        vec_scr[...] = vectors(vec_ref)
        acc_ref[...] = jnp.zeros_like(acc_ref)
        gv_ref[...] = jnp.zeros_like(gv_ref)
        home.launch()

    def body(cot_ref):
        d_b = combine_rows(col_ref, db_ref)
        normed, inv_scale = norm_parts(h_ref[...])
        gv_ref[2:3, :] = gv_ref[2:3, :] + jnp.sum(d_b * normed, 0, keepdims=True)
        gv_ref[3:4, :] = gv_ref[3:4, :] + jnp.sum(d_b, 0, keepdims=True)
        d_h = cot_ref[...] + norm_back(d_b * vec_scr[2:3, :], normed, inv_scale)
        dh_ref[...] = d_h
        d_attn = d_h.astype(BF16)
        do_ref[...] = dot(d_attn, w_ref[...]).astype(BF16)
        acc_ref[...] = acc_ref[...] + dot(d_attn, o_ref[...], TN)

    pl.when(i < n_long)(lambda: body(long_ref))
    pl.when(i >= n_long)(lambda: body(short_ref))

    @pl.when(i == n_rows - 1)
    def _():
        gp_ref[...] = acc_ref[...].astype(BF16)
        home.end()


def hidden_back(h, slot_col, db_back, long_cot, short_cot, o, dense, y):
    n_f = y.shape[0]
    count, width = h.shape
    slots = db_back.shape[0]
    n_long, n_short = long_cot.shape[0] // ROWS, short_cot.shape[0] // ROWS
    n_rows = n_long + n_short
    row = pl.BlockSpec((ROWS, width), lambda i: (i, 0))
    return pl.pallas_call(
        functools.partial(hidden_back_kernel, n_f, n_long, n_rows),
        grid=(n_rows,),
        in_specs=[row, pl.BlockSpec((ROWS, 1), lambda i: (i, 0)), constant((slots, width))]
        + long_short(width, n_long)
        + [
            row,
            pl.BlockSpec((width, width), lambda i: (0, 3)),
            pl.BlockSpec((width, LANES), lambda i: (0, 4 * width // LANES)),
            pl.BlockSpec(memory_space=pl.ANY),
        ],
        out_specs=[
            row,
            row,
            pl.BlockSpec((width, width), lambda i: (0, 0)),
            pl.BlockSpec((LANES, width), lambda i: (0, 0)),
            pl.BlockSpec(memory_space=pl.ANY),
        ],
        out_shape=[
            jax.ShapeDtypeStruct((count, width), F32),
            jax.ShapeDtypeStruct((count, width), BF16),
            jax.ShapeDtypeStruct((width, width), BF16),
            jax.ShapeDtypeStruct((LANES, width), F32),
            jax.ShapeDtypeStruct(y.shape, BF16),
        ],
        scratch_shapes=[
            pltpu.VMEM((width, width), F32),
            pltpu.VMEM((8, width), F32),
            pltpu.SemaphoreType.DMA((n_f,)),
            pltpu.SemaphoreType.DMA((n_f,)),
        ],
        compiler_params=params(collective_id=6, has_side_effects=True),
        cost_estimate=cost(2 * (slots + 2 * width) * count * width, 16 * count * width),
        name="hidden_back",
    )(h, slot_col, db_back, long_cot, short_cot, o, dense, dense, y)


def grads_kernel(
    n_long, n_rows, width, long_ref, short_ref, d_ref, w_ref, vec_ref, gp_ref, gv_ref,
    out_ref, acc_ref, vec_scr, sum_scr,
):
    i = pl.program_id(0)

    @pl.when(i == 0)
    def _():
        vec_scr[...] = vectors(vec_ref)
        acc_ref[...] = jnp.zeros_like(acc_ref)
        sum_scr[...] = jnp.zeros_like(sum_scr)

    def body(x_ref):
        normed, _ = norm_parts(x_ref[...])
        rows = (normed * vec_scr[0:1, :] + vec_scr[1:2, :]).astype(BF16)
        for part in range(3):
            cut = slice(part * width, (part + 1) * width)
            acc_ref[:, cut] = acc_ref[:, cut] + dot(rows, d_ref[part], TN)
            sum_scr[:, cut] = sum_scr[:, cut] + jnp.sum(
                d_ref[part].astype(F32), 0, keepdims=True
            )

    pl.when(i < n_long)(lambda: body(long_ref))
    pl.when(i >= n_long)(lambda: body(short_ref))

    @pl.when(i == n_rows - 1)
    def _():
        out_ref[:, :width] = gp_ref[...]
        out_ref[:, width : 4 * width] = acc_ref[...].astype(BF16)
        weighted = jnp.zeros((width, 1), F32)
        bias_grad = jnp.zeros((width, 1), F32)
        for part in range(3):
            cut = slice(part * width, (part + 1) * width)
            weight = w_ref[:, cut].astype(F32)
            weighted = weighted + jnp.sum(weight * acc_ref[:, cut], 1, keepdims=True)
            bias_grad = bias_grad + jnp.sum(weight * sum_scr[:, cut], 1, keepdims=True)
        out_ref[:, 4 * width :] = norm1_grads(weighted, bias_grad, vec_ref, gv_ref)


def dense_grads(long_x, short_x, d_qkv, dense, grad_proj, grad_vec):
    count, width = d_qkv.shape[1:]
    n_long, n_short = long_x.shape[0] // ROWS, short_x.shape[0] // ROWS
    n_rows = n_long + n_short
    return pl.pallas_call(
        functools.partial(grads_kernel, n_long, n_rows, width),
        grid=(n_rows,),
        in_specs=long_short(width, n_long)
        + [
            pl.BlockSpec((3, ROWS, width), lambda i: (0, i, 0)),
            constant((width, 3 * width)),
            pl.BlockSpec((width, LANES), lambda i: (0, 4 * width // LANES)),
            constant((width, width)),
            constant((LANES, width)),
        ],
        out_specs=pl.BlockSpec((width, 4 * width + LANES), lambda i: (0, 0)),
        out_shape=jax.ShapeDtypeStruct((width, 4 * width + LANES), BF16),
        scratch_shapes=[
            pltpu.VMEM((width, 3 * width), F32),
            pltpu.VMEM((8, width), F32),
            pltpu.VMEM((1, 3 * width), F32),
        ],
        compiler_params=params(),
        cost_estimate=cost(6 * count * width * width, 16 * count * width),
        name="dense_grads",
    )(long_x, short_x, d_qkv, dense, dense, grad_proj, grad_vec)


class Reducer:
    def __init__(self, part_ref, out_ref, chunks, scratch):
        self.part, self.out, self.chunks = part_ref, out_ref, chunks
        self.got1, self.sum1, self.got2, self.sum2, self.got3 = scratch[:5]
        self.sems = scratch[5:]
        self.n_dp, self.n_f = part_ref.shape[:2]
        self.z = lax.axis_index("dp")
        self.f = lax.axis_index("fsdp")
        self.half = self.n_f // 2
        self.parity = lax.rem(self.f, 2)
        self.mine = self.f // 2
        self.partner = self.f + 1 - 2 * self.parity
        self.order = list(range(1, self.half)) + [0]
        self.barrier = pltpu.get_barrier_semaphore()

    def greet(self):
        z, f = self.z, self.f
        for k in range(1, self.n_dp):
            pl.semaphore_signal(
                self.barrier, 1, device_id=(lax.rem(z + k, self.n_dp), f), device_id_type=MESH
            )
        for k in range(1, self.half):
            pl.semaphore_signal(
                self.barrier, 1, device_id=(z, lax.rem(f + 2 * k, self.n_f)), device_id_type=MESH
            )
        pl.semaphore_signal(self.barrier, 1, device_id=(z, self.partner), device_id_type=MESH)

    def meet(self):
        pl.semaphore_wait(self.barrier, self.n_dp - 1 + self.half)

    def slot(self, k):
        return lax.rem(self.mine + k, self.half)

    def core_copy(self, c, k):
        cut, slot = self.chunks[c], self.slot(k)
        return pltpu.make_async_remote_copy(
            self.part.at[:, 2 * slot + 1 - self.parity, :, cut], self.got1.at[slot, :, :, cut],
            self.sems[0].at[c, k], self.sems[1].at[c, k],
            device_id=(self.z, self.partner), device_id_type=MESH,
        )

    def chip_copy(self, c, k):
        cut = self.chunks[c]
        return pltpu.make_async_remote_copy(
            self.sum1.at[self.slot(k), :, :, cut], self.got2.at[k, :, :, cut],
            self.sems[2].at[c, k], self.sems[3].at[c, k],
            device_id=(self.z, lax.rem(self.f + 2 * k, self.n_f)), device_id_type=MESH,
        )

    def plane_copy(self, c, k):
        cut, there = self.chunks[c], lax.rem(self.z + k, self.n_dp)
        return pltpu.make_async_remote_copy(
            self.sum2.at[there, :, cut], self.got3.at[k, :, cut],
            self.sems[4].at[c, k], self.sems[5].at[c, k],
            device_id=(there, self.f), device_id_type=MESH,
        )

    def start_core(self, c):
        for k in self.order:
            self.core_copy(c, k).start()

    def start_chip(self, c):
        cut = self.chunks[c]
        for k in self.order:
            slot = self.slot(k)
            self.core_copy(c, k).wait_recv()
            self.sum1[slot, :, :, cut] = (
                self.part[:, 2 * slot + self.parity, :, cut].astype(F32)
                + self.got1[slot, :, :, cut].astype(F32)
            ).astype(BF16)
            if k:
                self.chip_copy(c, k).start()

    def start_plane(self, c):
        cut = self.chunks[c]
        total = self.sum1[self.mine, :, :, cut].astype(F32)
        for k in range(1, self.half):
            self.chip_copy(c, k).wait_recv()
            total = total + self.got2[k, :, :, cut].astype(F32)
        self.sum2[:, :, cut] = total.astype(BF16)
        for k in range(1, self.n_dp):
            self.plane_copy(c, k).start()

    def close(self, c):
        cut = self.chunks[c]
        total = self.sum2[self.z, :, cut].astype(F32)
        for k in range(1, self.n_dp):
            self.plane_copy(c, k).wait_recv()
            total = total + self.got3[k, :, cut].astype(F32)
        self.out[:, cut] = total

    def drain(self):
        for c in range(len(self.chunks)):
            for k in range(self.half):
                self.core_copy(c, k).wait_send()
            for k in range(1, self.half):
                self.chip_copy(c, k).wait_send()
            for k in range(1, self.n_dp):
                self.plane_copy(c, k).wait_send()


def reducer_scratch(n_chunks, n_dp, n_f, share, columns):
    half = n_f // 2
    return [
        pltpu.VMEM((half, n_dp, share, columns), BF16),
        pltpu.VMEM((half, n_dp, share, columns), BF16),
        pltpu.VMEM((half, n_dp, share, columns), BF16),
        pltpu.VMEM((n_dp, share, columns), BF16),
        pltpu.VMEM((n_dp, share, columns), BF16),
        pltpu.SemaphoreType.DMA((n_chunks, half)),
        pltpu.SemaphoreType.DMA((n_chunks, half)),
        pltpu.SemaphoreType.DMA((n_chunks, half)),
        pltpu.SemaphoreType.DMA((n_chunks, half)),
        pltpu.SemaphoreType.DMA((n_chunks, n_dp)),
        pltpu.SemaphoreType.DMA((n_chunks, n_dp)),
    ]


def input_grad(x_ref, dh_ref, d_ref, w_ref, vec_scr, grad_ref):
    width = dh_ref.shape[1]
    normed, inv_scale = norm_parts(x_ref)
    entered = jnp.zeros_like(normed)
    for part in range(3):
        entered = entered + dot(d_ref[part], w_ref[:, part * width : (part + 1) * width], NT)
    grad_ref[...] = dh_ref[...] + norm_back(entered * vec_scr[0:1, :], normed, inv_scale)


def norm1_grads(weighted, bias_grad, vec_ref, gv_ref):
    gain, bias = vec_ref[:, 0:1].astype(F32), vec_ref[:, 1:2].astype(F32)
    lane = lax.broadcasted_iota(jnp.int32, (1, LANES), 1)
    found = jnp.transpose(gv_ref[...])
    found = jnp.where(lane == 0, (weighted - bias * bias_grad) / gain, found)
    return jnp.where(lane == 1, bias_grad, found).astype(BF16)


def last_kernel(
    n_long, n_rows, part_ref, long_ref, short_ref, dh_ref, d_ref, w_ref, vec_ref,
    h_ref, col_ref, y_ref, out_ref, lg_ref, sg_ref, lo_ref, so_ref, vec_scr, *scratch,
):
    i = pl.program_id(0)
    reducer = Reducer(part_ref, out_ref, column_chunks(part_ref.shape[3]), scratch)

    @pl.when(i == 0)
    def _():
        reducer.greet()
        vec_scr[...] = vectors(vec_ref)
        reducer.meet()
        for c in range(N_CHUNKS):
            reducer.start_core(c)

    def back(x_ref, grad_ref):
        input_grad(x_ref[...], dh_ref, d_ref, w_ref, vec_scr, grad_ref)

    pl.when(i < n_long)(lambda: back(long_ref, lg_ref))
    pl.when((i >= n_long) & (i < n_rows))(lambda: back(short_ref, sg_ref))

    @pl.when(i == 0)
    def _():
        for c in range(N_CHUNKS):
            reducer.start_chip(c)

    def finish(out):
        out[...] = h_ref[...] + combine_rows(col_ref, y_ref)

    pl.when((i >= n_rows) & (i < n_rows + n_long))(lambda: finish(lo_ref))
    pl.when((i >= n_rows + n_long) & (i < 2 * n_rows))(lambda: finish(so_ref))

    @pl.when(i == 2 * n_rows - 1)
    def _():
        for c in range(N_CHUNKS):
            reducer.start_plane(c)
        for c in range(N_CHUNKS):
            reducer.close(c)
        reducer.drain()


def last_stage(partial, long_x, short_x, d_h, d_qkv, dense, h, slot_col, y_back):
    n_dp, n_f, share, columns = partial.shape
    count, width = d_h.shape
    n_long, n_short = long_x.shape[0] // ROWS, short_x.shape[0] // ROWS
    n_rows = n_long + n_short
    slots = y_back.shape[0]
    row = pl.BlockSpec((ROWS, width), lambda i: (jnp.minimum(i, n_rows - 1), 0))
    late = lambda i: (jnp.clip(i - n_rows, 0, n_rows - 1), 0)
    return pl.pallas_call(
        functools.partial(last_kernel, n_long, n_rows),
        grid=(2 * n_rows,),
        in_specs=[
            constant(partial.shape),
            pl.BlockSpec((ROWS, width), lambda i: (jnp.minimum(i, n_long - 1), 0)),
            pl.BlockSpec((ROWS, width), lambda i: (jnp.clip(i - n_long, 0, n_short - 1), 0)),
            row,
            pl.BlockSpec((3, ROWS, width), lambda i: (0, jnp.minimum(i, n_rows - 1), 0)),
            constant((width, 3 * width)),
            pl.BlockSpec((width, LANES), lambda i: (0, 4 * width // LANES)),
            pl.BlockSpec((ROWS, width), late),
            pl.BlockSpec((ROWS, 1), late),
            constant((slots, width)),
        ],
        out_specs=[
            pl.BlockSpec((share, columns), lambda i: (0, 0)),
            pl.BlockSpec((ROWS, width), lambda i: (jnp.minimum(i, n_long - 1), 0)),
            pl.BlockSpec((ROWS, width), lambda i: (jnp.clip(i - n_long, 0, n_short - 1), 0)),
            pl.BlockSpec((ROWS, width), lambda i: (jnp.clip(i - n_rows, 0, n_long - 1), 0)),
            pl.BlockSpec(
                (ROWS, width), lambda i: (jnp.clip(i - n_rows - n_long, 0, n_short - 1), 0)
            ),
        ],
        out_shape=[
            jax.ShapeDtypeStruct((share, columns), F32),
            jax.ShapeDtypeStruct(long_x.shape, F32),
            jax.ShapeDtypeStruct(short_x.shape, F32),
            jax.ShapeDtypeStruct(long_x.shape, F32),
            jax.ShapeDtypeStruct(short_x.shape, F32),
        ],
        scratch_shapes=[pltpu.VMEM((8, width), F32)]
        + reducer_scratch(N_CHUNKS, n_dp, n_f, share, columns),
        compiler_params=params(collective_id=1, has_side_effects=True),
        cost_estimate=cost(2 * count * width * (3 * width + slots), 60e6),
        name="last_stage",
    )(partial, long_x, short_x, d_h, d_qkv, dense, dense, h, slot_col, y_back)


def close_kernel(
    n_long, n_rows, proj_ref, gv_ref, long_ref, short_ref, dp_ref, dh_ref, d_ref, w_ref, vec_ref,
    h_ref, col_ref, y_ref, out_ref, lg_ref, sg_ref, lo_ref, so_ref,
    vec_scr, rows_ref, part_ref, stat_ref, *scratch,
):
    i = pl.program_id(0)
    n_dp, n_f, share, columns = part_ref.shape
    width = dh_ref.shape[1]
    chunks = [slice(c * width, (c + 1) * width) for c in range(3)] + [slice(3 * width, columns)]
    reducer = Reducer(part_ref, out_ref, chunks, scratch)
    begin_back, begin_out = 3, 3 + n_rows

    def scatter(value, cut):
        for index in range(n_dp * n_f):
            part_ref[index // n_f, index % n_f, :, cut] = value[
                index * share : (index + 1) * share
            ].astype(BF16)

    @pl.when(i == 0)
    def _():
        reducer.greet()
        vec_scr[...] = vectors(vec_ref)
        part_ref[:, :, :, :width] = proj_ref[...]
        reducer.meet()
        reducer.start_core(0)
        n = long_ref.shape[0]
        for ref, first in ((long_ref, 0), (short_ref, n)):
            for start in range(0, ref.shape[0], ROWS):
                normed, _ = norm_parts(ref[start : start + ROWS, :])
                rows_ref[first + start : first + start + ROWS, :] = (
                    normed * vec_scr[0:1, :] + vec_scr[1:2, :]
                ).astype(BF16)
        stat_ref[...] = jnp.zeros_like(stat_ref)
        reducer.start_chip(0)

    for part in range(3):

        @pl.when(i == part)
        def _(part=part):
            value = dot(rows_ref[...], dp_ref[0], TN)
            scatter(value, slice((part + 1) * width, (part + 2) * width))
            weight = w_ref[:, part * width : (part + 1) * width].astype(F32)
            sums = jnp.sum(dp_ref[0].astype(F32), 0, keepdims=True)
            stat_ref[:, 0:1] = stat_ref[:, 0:1] + jnp.sum(weight * value, 1, keepdims=True)
            stat_ref[:, 1:2] = stat_ref[:, 1:2] + jnp.sum(weight * sums, 1, keepdims=True)
            if part == 2:
                found = norm1_grads(stat_ref[:, 0:1], stat_ref[:, 1:2], vec_ref, gv_ref)
                scatter(found.astype(F32), slice(4 * width, columns))
            reducer.start_core(part + 1)
            if part:
                reducer.start_chip(part)

    @pl.when(i == begin_back)
    def _():
        reducer.start_chip(3)

    def back(x_ref, index, grad_ref):
        rows = pl.ds(pl.multiple_of(index * ROWS, ROWS), ROWS)
        input_grad(x_ref[rows, :], dh_ref, d_ref, w_ref, vec_scr, grad_ref)

    j = i - begin_back
    pl.when((j >= 0) & (j < n_long))(lambda: back(long_ref, j, lg_ref))
    pl.when((j >= n_long) & (j < n_rows))(lambda: back(short_ref, j - n_long, sg_ref))

    def finish(out):
        out[...] = h_ref[...] + combine_rows(col_ref, y_ref)

    m = i - begin_out
    pl.when((m >= 0) & (m < n_long))(lambda: finish(lo_ref))
    pl.when((m >= n_long) & (m < n_rows))(lambda: finish(so_ref))

    pl.when(i == begin_back + 1)(lambda: reducer.start_plane(0))
    pl.when(i == begin_out - 1)(lambda: reducer.start_plane(1))
    pl.when(i == begin_out + n_rows - 2)(lambda: reducer.start_plane(2))

    @pl.when(i == begin_out + n_rows - 1)
    def _():
        reducer.start_plane(3)
        for c in range(4):
            reducer.close(c)
        reducer.drain()


def close_stage(grad_proj, grad_vec, long_x, short_x, d_h, d_qkv, dense, h, slot_col, y_back):
    n_dp, n_f, share = grad_proj.shape[:3]
    count, width = d_h.shape
    columns = 4 * width + LANES
    n_long, n_short = long_x.shape[0] // ROWS, short_x.shape[0] // ROWS
    n_rows = n_long + n_short
    slots = y_back.shape[0]
    step = lambda i, base, last: jnp.clip(i - base, 0, last)
    return pl.pallas_call(
        functools.partial(close_kernel, n_long, n_rows),
        grid=(3 + 2 * n_rows,),
        in_specs=[
            constant(grad_proj.shape),
            constant(grad_vec.shape),
            constant(long_x.shape),
            constant(short_x.shape),
            pl.BlockSpec((1, count, width), lambda i: (jnp.minimum(i, 2), 0, 0)),
            pl.BlockSpec((ROWS, width), lambda i: (step(i, 3, n_rows - 1), 0)),
            pl.BlockSpec((3, ROWS, width), lambda i: (0, step(i, 3, n_rows - 1), 0)),
            constant((width, 3 * width)),
            pl.BlockSpec((width, LANES), lambda i: (0, 4 * width // LANES)),
            pl.BlockSpec((ROWS, width), lambda i: (step(i, 3 + n_rows, n_rows - 1), 0)),
            pl.BlockSpec((ROWS, 1), lambda i: (step(i, 3 + n_rows, n_rows - 1), 0)),
            constant((slots, width)),
        ],
        out_specs=[
            pl.BlockSpec((share, columns), lambda i: (0, 0)),
            pl.BlockSpec((ROWS, width), lambda i: (step(i, 3, n_long - 1), 0)),
            pl.BlockSpec((ROWS, width), lambda i: (step(i, 3 + n_long, n_short - 1), 0)),
            pl.BlockSpec((ROWS, width), lambda i: (step(i, 3 + n_rows, n_long - 1), 0)),
            pl.BlockSpec((ROWS, width), lambda i: (step(i, 3 + n_rows + n_long, n_short - 1), 0)),
        ],
        out_shape=[
            jax.ShapeDtypeStruct((share, columns), F32),
            jax.ShapeDtypeStruct(long_x.shape, F32),
            jax.ShapeDtypeStruct(short_x.shape, F32),
            jax.ShapeDtypeStruct(long_x.shape, F32),
            jax.ShapeDtypeStruct(short_x.shape, F32),
        ],
        scratch_shapes=[
            pltpu.VMEM((8, width), F32),
            pltpu.VMEM((count, width), BF16),
            pltpu.VMEM((n_dp, n_f, share, columns), BF16),
            pltpu.VMEM((width, LANES), F32),
        ]
        + reducer_scratch(4, n_dp, n_f, share, columns),
        compiler_params=params(collective_id=4, has_side_effects=True),
        cost_estimate=cost(2 * count * width * (6 * width + slots), 60e6),
        name="close_stage",
    )(grad_proj, grad_vec, long_x, short_x, d_qkv, d_h, d_qkv, dense, dense, h, slot_col, y_back)


def ship_kernel(n_long, width, *refs):
    i = pl.program_id(0)
    arrays_in, (owned_ref, down_ref), rest = refs[:4], refs[4:6], refs[6:]
    arrays_out, (qkv_ref, proj_ref, grad_ref), vec_refs, pad_ref = rest[:4], rest[4:7], rest[7:11], rest[11]
    for first in (0, 2):

        @pl.when(i < n_long)
        def _():
            arrays_out[first][...] = arrays_in[first][...]

        @pl.when(i >= n_long)
        def _():
            arrays_out[first + 1][...] = arrays_in[first + 1][...]

    grad_ref[...] = down_ref[...].astype(F32)

    @pl.when(i == 0)
    def _():
        share = owned_ref.shape[0]
        qkv_ref[...] = owned_ref[:, width : 4 * width]
        pad_ref[...] = jnp.zeros_like(pad_ref)
        pad_ref[:share, :] = owned_ref[:, 4 * width :]
        proj_ref[...] = owned_ref[:, :width]
        turned = jnp.transpose(pad_ref[...])
        for row, vec_ref in enumerate(vec_refs):
            vec_ref[...] = turned[row : row + 1, :share]


def ship(arrays, owned, grad_down):
    width = arrays[0].shape[1]
    n_long, n_short = arrays[0].shape[0] // ROWS, arrays[1].shape[0] // ROWS
    steps = n_long + n_short
    share = owned.shape[0]
    piece = pl.BlockSpec((grad_down.shape[0] // steps, width), lambda i: (i, 0))
    whole = lambda shape: pl.BlockSpec(shape, lambda i: (0, 0))
    return pl.pallas_call(
        functools.partial(ship_kernel, n_long, width),
        grid=(steps,),
        in_specs=long_short(width, n_long) * 2 + [constant(owned.shape), piece],
        out_specs=long_short(width, n_long) * 2
        + [whole((share, 3 * width)), whole((share, width)), piece]
        + [whole((1, share))] * 4,
        out_shape=[jax.ShapeDtypeStruct(a.shape, a.dtype) for a in arrays]
        + [
            jax.ShapeDtypeStruct((share, 3 * width), F32),
            jax.ShapeDtypeStruct((share, width), F32),
            jax.ShapeDtypeStruct(grad_down.shape, F32),
        ]
        + [jax.ShapeDtypeStruct((1, share), F32)] * 4,
        scratch_shapes=[pltpu.VMEM((LANES, LANES), F32)],
        compiler_params=params(),
        cost_estimate=cost(0, sum(8 * a.size for a in arrays)),
        name="ship",
    )(*arrays, owned, grad_down)


def on_device(
    n_dp, n_f, long_x, short_x, long_len, short_len, expert_ids, ln1_gain, ln1_bias,
    w_qkv, w_proj, ln2_gain, ln2_bias, w_up, w_down, long_cot, short_cot,
):
    width = long_x.shape[2]
    share = w_qkv.shape[0]
    seqs = sequences(long_x.shape[:2], short_x.shape[:2])
    flat = lambda a: a.reshape(-1, width)
    xl, xs, gl, gs = flat(long_x), flat(short_x), flat(long_cot), flat(short_cot)
    n_long, n_short = xl.shape[0] // ROWS, xs.shape[0] // ROWS
    experts = n_f * w_up.shape[0]
    cap = 4 * expert_ids.shape[0] // (3 * experts)
    slots = experts * cap

    up = lax.all_gather(w_up, "dp", axis=2, tiled=True)[0]
    down = lax.all_gather(w_down, "dp", axis=1, tiled=True)[0]

    vec = jnp.stack([ln1_gain, ln1_bias, ln2_gain, ln2_bias], 1)
    own = jnp.concatenate(
        [w_qkv, w_proj.T, jnp.pad(vec, ((0, 0), (0, LANES - vec.shape[1])))], 1
    )
    dense, slot_col, slot_row, g_slots = gather_dense(
        own, expert_ids, gl, gs, n_dp, n_f, cap, slots
    )
    dense = dense.reshape(n_dp * n_f * share, own.shape[1])

    def exchange(rows):
        sent = lax.all_to_all(
            rows.reshape(n_f, cap, width), "fsdp", split_axis=0, concat_axis=0, tiled=True
        )
        return sent.reshape(slots, width)

    g_there = exchange(g_slots)
    qkv = make_qkv(xl, xs, dense)
    o, lse = attend(qkv, long_len, short_len, seqs)
    h, b_there, act, slope, grad_down = forward_experts(
        xl, xs, o, dense, slot_row, g_there, up, n_f, cap
    )
    grad_down = lax.psum_scatter(grad_down, "dp", scatter_dimension=0, tiled=True)
    y0, db0, gu0 = own_experts(
        lax.axis_index("dp").reshape(1), b_there, g_there, act, slope, up, w_down[0], n_f, cap
    )
    y, db_back, grad_up = back_experts(
        b_there, g_there, act, slope, up, down, y0, db0, gu0, n_dp, n_f, cap
    )
    db_back = db_back.reshape(slots, width)
    grad_up = lax.psum_scatter(grad_up, "dp", scatter_dimension=1, tiled=True)
    y = y.reshape(n_f, cap, width)
    d_h, d_o, grad_proj, grad_vec, y_back = hidden_back(
        h, slot_col, db_back, gl, gs, o, dense, y
    )
    d_qkv, y_back = attend_back(
        qkv, o, d_o, lse, long_len, short_len, seqs, y, y_back
    )
    y_back = y_back.reshape(slots, width)
    if share % 8 == 0:
        owned, long_grad, short_grad, long_out, short_out = close_stage(
            grad_proj.reshape(n_dp, n_f, share, width), grad_vec,
            xl, xs, d_h, d_qkv, dense, h, slot_col, y_back,
        )
    else:
        partial = dense_grads(xl, xs, d_qkv, dense, grad_proj, grad_vec)
        owned, long_grad, short_grad, long_out, short_out = last_stage(
            partial.reshape(n_dp, n_f, share, own.shape[1]),
            xl, xs, d_h, d_qkv, dense, h, slot_col, y_back,
        )
    (long_grad, short_grad, long_out, short_out, grad_qkv, grad_proj, grad_down, *grad_vec) = ship(
        (long_grad, short_grad, long_out, short_out), owned, grad_down
    )
    grad_up, grad_down = lax.optimization_barrier((grad_up, grad_down))
    grad_up = grad_up.astype(F32)
    return (
        long_out.reshape(long_x.shape),
        short_out.reshape(short_x.shape),
        long_grad.reshape(long_x.shape),
        short_grad.reshape(short_x.shape),
        grad_vec[0].reshape(-1),
        grad_vec[1].reshape(-1),
        grad_qkv,
        grad_proj.T,
        grad_vec[2].reshape(-1),
        grad_vec[3].reshape(-1),
        grad_up[None],
        grad_down[None],
    )


def solution(mesh):
    both = ("dp", "fsdp")
    return jax.shard_map(
        functools.partial(on_device, mesh.shape["dp"], mesh.shape["fsdp"]),
        mesh=mesh,
        in_specs=(
            P(both, None, None),
            P(both, None, None),
            P(both),
            P(both),
            P(both, None),
            P(both),
            P(both),
            P(both, None),
            P(None, both),
            P(both),
            P(both),
            P("fsdp", None, "dp"),
            P("fsdp", "dp", None),
            P(both, None, None),
            P(both, None, None),
        ),
        out_specs=(
            P(both, None, None),
            P(both, None, None),
            P(both, None, None),
            P(both, None, None),
            P(both),
            P(both),
            P(both, None),
            P(None, both),
            P(both),
            P(both),
            P("fsdp", None, "dp"),
            P("fsdp", "dp", None),
        ),
        check_vma=False,
    )
```

```python
import functools

import jax
import jax.numpy as jnp
from jax import lax
from jax.experimental import pallas as pl
from jax.experimental.pallas import tpu as pltpu
from jax.sharding import PartitionSpec as P

MESH = pl.DeviceIdType.MESH
HEAD_DIM = 64
EPSILON = 1e-05
MASKED = -1e30
BF16 = jnp.bfloat16
F32 = jnp.float32
LANES = 128
ROWS = 512
BLOCK = 256
ATTEND = 512
ATTEND_BACK = 512
VMEM_LIMIT = 60 * 2**20
N_CHUNKS = 3

NN = (((1,), (0,)), ((), ()))
NT = (((1,), (1,)), ((), ()))
TN = (((0,), (0,)), ((), ()))


def dot(a, b, dims=NN, precision=None):
    return lax.dot_general(a, b, dims, preferred_element_type=F32, precision=precision)


def params(**extra):
    return pltpu.CompilerParams(vmem_limit_bytes=VMEM_LIMIT, **extra)


def cost(flops, moved, exps=0):
    return pl.CostEstimate(flops=int(flops), bytes_accessed=int(moved), transcendentals=int(exps))


def constant(shape):
    return pl.BlockSpec(shape, lambda *_: (0,) * len(shape), pipeline_mode=pl.Buffered(1))


def norm_parts(inputs):
    average = jnp.mean(inputs, -1, keepdims=True)
    centred = inputs - average
    inv_scale = lax.rsqrt(jnp.mean(centred * centred, -1, keepdims=True) + EPSILON)
    return centred * inv_scale, inv_scale


def norm_back(grad_normed, normed, inv_scale):
    centre_term = jnp.mean(grad_normed, -1, keepdims=True)
    slope_term = jnp.mean(grad_normed * normed, -1, keepdims=True)
    return inv_scale * (grad_normed - centre_term - normed * slope_term)


def vectors(vec_ref):
    return jnp.transpose(vec_ref[...].astype(F32))[:8]


def long_short(width, n_long):
    return [
        pl.BlockSpec((ROWS, width), lambda i: (jnp.minimum(i, n_long - 1), 0)),
        pl.BlockSpec((ROWS, width), lambda i: (jnp.maximum(i - n_long, 0), 0)),
    ]


def column_chunks(columns):
    tiles = columns // LANES
    edges = [LANES * (tiles * c // N_CHUNKS) for c in range(N_CHUNKS + 1)]
    return [slice(lo, hi) for lo, hi in zip(edges, edges[1:])]


def gather_kernel(
    n_dp, n_f, cap, own_ref, ids_ref, long_ref, short_ref, out_ref, col_ref, row_ref, slots_ref,
    rows_ref, z_send, z_recv, p_send, p_recv, c_send, c_recv, l_sem,
):
    z = lax.axis_index("dp")
    f = lax.axis_index("fsdp")
    half = n_f // 2
    partner = f + 1 - 2 * lax.rem(f, 2)
    barrier = pltpu.get_barrier_semaphore()
    for k in range(1, n_dp):
        pl.semaphore_signal(barrier, 1, device_id=(lax.rem(z + k, n_dp), f), device_id_type=MESH)
    for k in range(1, half):
        pl.semaphore_signal(barrier, 1, device_id=(z, lax.rem(f + 2 * k, n_f)), device_id_type=MESH)
    pl.semaphore_signal(barrier, 1, device_id=(z, partner), device_id_type=MESH)
    local = pltpu.make_async_copy(own_ref, out_ref.at[z, f], l_sem)
    local.start()
    pl.semaphore_wait(barrier, n_dp - 1 + half)

    chunks = column_chunks(own_ref.shape[1])
    z_copies, p_copies, c_copies = [], [], []

    def send_z(c):
        for k in range(1, n_dp):
            copy = pltpu.make_async_remote_copy(
                own_ref.at[:, chunks[c]], out_ref.at[z, f, :, chunks[c]],
                z_send.at[c, k], z_recv.at[c, k],
                device_id=(lax.rem(z + k, n_dp), f), device_id_type=MESH,
            )
            copy.start()
            z_copies.append(copy)

    def send_p(c):
        for k in range(1, n_dp):
            z_copies[c * (n_dp - 1) + k - 1].wait_recv()
        for k in range(1, half):
            copy = pltpu.make_async_remote_copy(
                out_ref.at[:, f, :, chunks[c]], out_ref.at[:, f, :, chunks[c]],
                p_send.at[c, k], p_recv.at[c, k],
                device_id=(z, lax.rem(f + 2 * k, n_f)), device_id_type=MESH,
            )
            copy.start()
            p_copies.append(copy)

    def send_c(c):
        for k in range(half):
            if k:
                p_copies[c * (half - 1) + k - 1].wait_recv()
            column = lax.rem(f + n_f - 2 * k, n_f)
            copy = pltpu.make_async_remote_copy(
                out_ref.at[:, column, :, chunks[c]], out_ref.at[:, column, :, chunks[c]],
                c_send.at[c, k], c_recv.at[c, k],
                device_id=(z, partner), device_id_type=MESH,
            )
            copy.start()
            c_copies.append(copy)

    def fill(block, carry):
        start = pl.multiple_of(block * BLOCK, BLOCK)
        slots_ref[pl.ds(start, BLOCK), :] = dispatch_block(row_ref, rows_ref[...], start, BLOCK)
        return carry

    n_blocks = slots_ref.shape[0] // BLOCK
    for c in range(len(chunks)):
        send_z(c)
    number_slots(cap, ids_ref, col_ref, row_ref)
    n_long = long_ref.shape[0]
    rows_ref[:n_long, :] = long_ref[...].astype(BF16)
    rows_ref[n_long:, :] = short_ref[...].astype(BF16)
    local.wait()
    for c in range(len(chunks)):
        send_p(c)
        lax.fori_loop(c * n_blocks // len(chunks), (c + 1) * n_blocks // len(chunks), fill, 0)
    for c in range(len(chunks)):
        send_c(c)
    for copy in c_copies:
        copy.wait_recv()
    for copy in z_copies + p_copies + c_copies:
        copy.wait_send()


def gather_dense(own, ids, long_cot, short_cot, n_dp, n_f, cap, slots):
    count, width = ids.shape[0], long_cot.shape[1]
    vmem = pl.BlockSpec(memory_space=pltpu.VMEM)
    return pl.pallas_call(
        functools.partial(gather_kernel, n_dp, n_f, cap),
        out_shape=[
            jax.ShapeDtypeStruct((n_dp, n_f) + own.shape, own.dtype),
            jax.ShapeDtypeStruct((count, 1), jnp.int32),
            jax.ShapeDtypeStruct((8, count), jnp.int32),
            jax.ShapeDtypeStruct((slots, width), BF16),
        ],
        in_specs=[pl.BlockSpec(memory_space=pl.ANY), vmem, vmem, vmem],
        out_specs=[pl.BlockSpec(memory_space=pl.ANY), vmem, vmem, vmem],
        scratch_shapes=[
            pltpu.VMEM((count, width), BF16),
            pltpu.SemaphoreType.DMA((N_CHUNKS, n_dp)),
            pltpu.SemaphoreType.DMA((N_CHUNKS, n_dp)),
            pltpu.SemaphoreType.DMA((N_CHUNKS, n_f // 2)),
            pltpu.SemaphoreType.DMA((N_CHUNKS, n_f // 2)),
            pltpu.SemaphoreType.DMA((N_CHUNKS, n_f // 2)),
            pltpu.SemaphoreType.DMA((N_CHUNKS, n_f // 2)),
            pltpu.SemaphoreType.DMA,
        ],
        compiler_params=params(collective_id=0, has_side_effects=True),
        cost_estimate=cost(0, 100e6),
        name="gather_dense",
    )(own, ids, long_cot, short_cot)


def dispatch_block(slot_row_ref, rows, first, size):
    slot_id = first + lax.broadcasted_iota(jnp.int32, (size, 1), 0)
    chosen = (slot_row_ref[0:1, :] == slot_id).astype(F32).astype(BF16)
    return dot(chosen, rows).astype(BF16)


def number_slots(cap, ids_ref, col_ref, row_ref):
    count = ids_ref.shape[0]
    lane = lax.broadcasted_iota(jnp.int32, (1, LANES), 1)
    onehot = (ids_ref[...] == lane).astype(F32)
    onehot_low = onehot.astype(BF16)
    col = lax.broadcasted_iota(jnp.int32, (1, count), 1)
    base = (lane * cap).astype(F32)
    ones = jnp.ones((8, LANES), F32)
    for start in range(0, count, ROWS):
        row = start + lax.broadcasted_iota(jnp.int32, (ROWS, 1), 0)
        before = dot((col < row).astype(F32).astype(BF16), onehot_low)
        picked = (before + base) * onehot[start : start + ROWS]
        col_ref[start : start + ROWS, :] = jnp.sum(picked, 1, keepdims=True).astype(jnp.int32)
        row_ref[:, start : start + ROWS] = dot(
            ones, picked, NT, precision=lax.Precision.HIGHEST
        ).astype(jnp.int32)


def peers(n_f):
    f = lax.axis_index("fsdp")

    def partner(k):
        place, digit = 0, 1
        while digit < n_f:
            place = place + digit * lax.rem(f // digit + k // digit, 2)
            digit *= 2
        return place

    return f, partner


def greet(n_f, to):
    z = lax.axis_index("dp")
    barrier = pltpu.get_barrier_semaphore()
    for k in range(1, n_f):
        pl.semaphore_signal(barrier, 1, device_id=(z, to(k)), device_id_type=MESH)


def early_blocks(n_f):
    return [k for k in range(1, n_f) if k & (k - 1) == 0]


def late_blocks(n_f):
    return [k for k in range(1, n_f) if k & (k - 1) != 0]


class Homeward:
    def __init__(self, n_f, ks, y_ref, yb_ref, send, recv):
        self.f, self.to = peers(n_f)
        self.n_f, self.ks = n_f, ks
        self.z = lax.axis_index("dp")
        self.y, self.yb, self.send, self.recv = y_ref, yb_ref, send, recv

    def transfer(self, k):
        return pltpu.make_async_remote_copy(
            self.y.at[self.to(k)], self.yb.at[self.f], self.send.at[k], self.recv.at[k],
            device_id=(self.z, self.to(k)), device_id_type=MESH,
        )

    def begin(self):
        greet(self.n_f, self.to)

    def launch(self):
        pl.semaphore_wait(pltpu.get_barrier_semaphore(), self.n_f - 1)
        for k in self.ks:
            self.transfer(k).start()

    def end(self):
        for k in self.ks:
            self.transfer(k).wait_recv()
            self.transfer(k).wait_send()


def qkv_kernel(n_long, width, long_ref, short_ref, w_ref, vec_ref, qkv_ref, vec_scr):
    i = pl.program_id(0)

    @pl.when(i == 0)
    def _():
        vec_scr[...] = vectors(vec_ref)

    def body(x_ref):
        normed, _ = norm_parts(x_ref[...])
        rows = (normed * vec_scr[0:1, :] + vec_scr[1:2, :]).astype(BF16)
        for part in range(3):
            cut = slice(part * width, (part + 1) * width)
            out = dot(rows, w_ref[:, cut])
            if part == 0:
                out = out * HEAD_DIM ** (-0.5)
            qkv_ref[:, cut] = out.astype(BF16)

    pl.when(i < n_long)(lambda: body(long_ref))
    pl.when(i >= n_long)(lambda: body(short_ref))


def make_qkv(long_x, short_x, dense):
    width = long_x.shape[1]
    n_long, n_short = long_x.shape[0] // ROWS, short_x.shape[0] // ROWS
    count = long_x.shape[0] + short_x.shape[0]
    return pl.pallas_call(
        functools.partial(qkv_kernel, n_long, width),
        grid=(n_long + n_short,),
        in_specs=long_short(width, n_long)
        + [
            constant((width, 3 * width)),
            pl.BlockSpec((width, LANES), lambda i: (0, 4 * width // LANES)),
        ],
        out_specs=pl.BlockSpec((ROWS, 3 * width), lambda i: (i, 0)),
        out_shape=jax.ShapeDtypeStruct((count, 3 * width), BF16),
        scratch_shapes=[pltpu.VMEM((8, width), F32)],
        compiler_params=params(),
        cost_estimate=cost(6 * count * width * width, count * width * 10 + 6 * width * width),
        name="make_qkv",
    )(long_x, short_x, dense, dense)


def sequences(long_shape, short_shape):
    found = []
    start = 0
    for which, (number, length) in enumerate((long_shape, short_shape)):
        for index in range(number):
            found.append((start, length, which, index))
            start += length
    return found


def head_masks():
    lane = lax.broadcasted_iota(jnp.int32, (1, LANES), 1)
    return (lane < HEAD_DIM, lane >= HEAD_DIM)


def marked(q, k, valid, first, masks, lane):
    key_pos = first + lax.broadcasted_iota(jnp.int32, (k.shape[0], 1), 0)
    bias = jnp.where(key_pos < valid, 0.0, MASKED).astype(BF16)
    found = []
    for head in range(2):
        spare = HEAD_DIM * (1 - head)
        qh = jnp.where(masks[head], q, jnp.where(lane == spare, 1.0, 0.0).astype(BF16))
        kh = jnp.where(masks[head], k, jnp.where(lane == spare, bias, jnp.zeros_like(bias)))
        found.append((qh, kh))
    return found


def attend_kernel(seqs, long_len, short_len, q_ref, k_ref, v_ref, o_ref, lse_ref):
    pair = pl.program_id(0)
    masks = head_masks()
    lane = lax.broadcasted_iota(jnp.int32, (1, LANES), 1)

    @pl.when(pair == 0)
    def _():
        lse_ref[...] = jnp.zeros_like(lse_ref)

    causal = lax.broadcasted_iota(jnp.int32, (ATTEND, ATTEND), 0) <= lax.broadcasted_iota(
        jnp.int32, (ATTEND, ATTEND), 1
    )
    upper = lax.broadcasted_iota(jnp.int32, (LANES, 1), 0) < HEAD_DIM
    for start, length, which, index in seqs:
        valid = (short_len if which else long_len)[index]
        rows = slice(start, start + length)
        heads = marked(q_ref[rows, :], k_ref[rows, :], valid, 0, masks, lane)
        v = jnp.transpose(v_ref[rows, :].astype(F32))
        values = [
            jnp.where(upper, v, 1.0).astype(BF16),
            jnp.where(upper, 1.0, v).astype(BF16),
        ]
        for first in range(0, length, ATTEND):
            last = first + ATTEND
            outs = []
            for head, (qh, kh) in enumerate(heads):
                qb = qh[first:last]
                near = dot(kh[first:last], qb, NT)
                near = jnp.where(causal, near, MASKED)
                top = jnp.max(near, 0, keepdims=True)
                if first:
                    far = dot(kh[:first], qb, NT)
                    top = jnp.maximum(top, jnp.max(far, 0, keepdims=True))
                out = dot(values[head][:, first:last], jnp.exp(near - top).astype(BF16))
                if first:
                    out = out + dot(values[head][:, :first], jnp.exp(far - top).astype(BF16))
                total = out[LANES - 1 : LANES] if head == 0 else out[0:1]
                outs.append(out * (1.0 / total))
                lse_ref[pl.ds(2 * pair + head, 1), start + first : start + last] = top + jnp.log(
                    total
                )
            o_ref[start + first : start + last, :] = jnp.transpose(
                jnp.where(upper, outs[0], outs[1])
            ).astype(BF16)


def attend(qkv, long_len, short_len, seqs):
    count, width = qkv.shape[0], qkv.shape[1] // 3
    pairs = width // LANES
    return pl.pallas_call(
        functools.partial(attend_kernel, seqs),
        grid=(pairs,),
        in_specs=[pl.BlockSpec(memory_space=pltpu.SMEM)] * 2
        + [
            pl.BlockSpec((count, LANES), lambda i: (0, i)),
            pl.BlockSpec((count, LANES), lambda i: (0, i + pairs)),
            pl.BlockSpec((count, LANES), lambda i: (0, i + 2 * pairs)),
        ],
        out_specs=[
            pl.BlockSpec((count, LANES), lambda i: (0, i)),
            pl.BlockSpec((LANES, count), lambda i: (0, 0)),
        ],
        out_shape=[
            jax.ShapeDtypeStruct((count, width), BF16),
            jax.ShapeDtypeStruct((LANES, count), F32),
        ],
        compiler_params=params(),
        cost_estimate=cost(16e9, 8 * count * width, 10e6),
        name="attend",
    )(long_len, short_len, qkv, qkv, qkv)


def attend_back_kernel(
    seqs, n_f, long_len, short_len, q_ref, k_ref, v_ref, o_ref, do_ref, lse_ref, y_ref, _,
    d_ref, yb_ref, dkt_ref, dvt_ref, lse_scr, send, recv, l_sem,
):
    pair = pl.program_id(0)
    masks = head_masks()
    lane = lax.broadcasted_iota(jnp.int32, (1, LANES), 1)

    home = Homeward(n_f, late_blocks(n_f), y_ref, yb_ref, send, recv)
    keep = pltpu.make_async_copy(y_ref.at[home.f], yb_ref.at[home.f], l_sem)

    @pl.when(pair == 0)
    def _():
        home.begin()
        keep.start()
        lse_scr[...] = jnp.transpose(lse_ref[...])
        home.launch()

    causal = lax.broadcasted_iota(jnp.int32, (ATTEND_BACK, ATTEND_BACK), 1) <= (
        lax.broadcasted_iota(jnp.int32, (ATTEND_BACK, ATTEND_BACK), 0)
    )
    for start, length, which, index in seqs:
        valid = (short_len if which else long_len)[index]
        rows = slice(start, start + length)
        q, k, v, do = q_ref[rows, :], k_ref[rows, :], v_ref[rows, :], do_ref[rows, :]
        heads = marked(q, k, valid, 0, masks, lane)
        q_t = jnp.transpose(q.astype(F32)).astype(BF16)
        do_t = jnp.transpose(do.astype(F32)).astype(BF16)
        both = do.astype(F32) * o_ref[rows, :].astype(F32)
        lse_all = lse_scr[rows, :]
        dkt_ref[...] = jnp.zeros_like(dkt_ref)
        dvt_ref[...] = jnp.zeros_like(dvt_ref)
        for first in range(0, length, ATTEND_BACK):
            last = first + ATTEND_BACK
            dqs = []
            for head, (qh, kh) in enumerate(heads):
                part = slice(HEAD_DIM * head, HEAD_DIM * (head + 1))
                doh = jnp.where(masks[head], do[first:last], jnp.zeros_like(do[first:last]))
                lse = jnp.sum(
                    jnp.where(lane == 2 * pair + head, lse_all[first:last], 0.0), 1, keepdims=True
                )
                delta = jnp.sum(jnp.where(masks[head], both[first:last], 0.0), 1, keepdims=True)
                dq = jnp.zeros((ATTEND_BACK, LANES), F32)
                for keys in (slice(0, first), slice(first, last)):
                    if keys.stop == keys.start:
                        continue
                    p = jnp.exp(dot(qh[first:last], kh[keys], NT) - lse)
                    if keys.start == first:
                        p = jnp.where(causal, p, 0.0)
                    dp = dot(doh, v[keys], NT)
                    ds = (p * (dp - delta)).astype(BF16)
                    dvt_ref[part, keys] = dvt_ref[part, keys] + dot(
                        do_t[part, first:last], p.astype(BF16)
                    )
                    dkt_ref[part, keys] = dkt_ref[part, keys] + dot(q_t[part, first:last], ds)
                    dq = dq + dot(ds, k[keys])
                dqs.append(dq)
            d_ref[0, start + first : start + last, :] = (
                jnp.where(masks[0], dqs[0], dqs[1]) * HEAD_DIM ** (-0.5)
            ).astype(BF16)
        d_ref[1, rows, :] = jnp.transpose(dkt_ref[:, :length]).astype(BF16)
        d_ref[2, rows, :] = jnp.transpose(dvt_ref[:, :length]).astype(BF16)

    @pl.when(pair == pl.num_programs(0) - 1)
    def _():
        keep.wait()
        home.end()


def attend_back(qkv, o, d_o, lse, long_len, short_len, seqs, y, y_back):
    count, width = o.shape
    n_f = y.shape[0]
    pairs = width // LANES
    longest = max(length for _, length, _, _ in seqs)
    one = pl.BlockSpec((count, LANES), lambda i: (0, i))
    return pl.pallas_call(
        functools.partial(attend_back_kernel, seqs, n_f),
        grid=(pairs,),
        in_specs=[pl.BlockSpec(memory_space=pltpu.SMEM)] * 2
        + [
            one,
            pl.BlockSpec((count, LANES), lambda i: (0, i + pairs)),
            pl.BlockSpec((count, LANES), lambda i: (0, i + 2 * pairs)),
            one,
            one,
            constant((LANES, count)),
            pl.BlockSpec(memory_space=pl.ANY),
            pl.BlockSpec(memory_space=pl.ANY),
        ],
        out_specs=[
            pl.BlockSpec((3, count, LANES), lambda i: (0, 0, i)),
            pl.BlockSpec(memory_space=pl.ANY),
        ],
        input_output_aliases={9: 1},
        out_shape=[
            jax.ShapeDtypeStruct((3, count, width), BF16),
            jax.ShapeDtypeStruct(y.shape, BF16),
        ],
        scratch_shapes=[
            pltpu.VMEM((LANES, longest), F32),
            pltpu.VMEM((LANES, longest), F32),
            pltpu.VMEM((count, LANES), F32),
            pltpu.SemaphoreType.DMA((n_f,)),
            pltpu.SemaphoreType.DMA((n_f,)),
            pltpu.SemaphoreType.DMA,
        ],
        compiler_params=params(collective_id=5, has_side_effects=True),
        cost_estimate=cost(40e9, 16 * count * width, 10e6),
        name="attend_back",
    )(long_len, short_len, qkv, qkv, qkv, o, d_o, lse, y, y_back)


class Line:
    def __init__(self, own_ref, all_ref, send, recv, l_sem):
        self.own, self.all, self.send, self.recv = own_ref, all_ref, send, recv
        self.n = all_ref.shape[0]
        self.z = lax.axis_index("dp")
        self.f = lax.axis_index("fsdp")
        self.barrier = pltpu.get_barrier_semaphore()
        self.keep = pltpu.make_async_copy(own_ref, all_ref.at[self.z], l_sem)
        half = all_ref.shape[1] // 2
        self.chunks = (pl.ds(0, half), pl.ds(half, half))
        self.sides = (1, -1)

    def exists(self, place):
        return (place >= 0) & (place < self.n)

    def copy(self, hop, index, chunk, plane):
        side, rows = self.sides[index], self.chunks[chunk]
        src = self.own.at[rows] if hop == 1 else self.all.at[plane, rows]
        return pltpu.make_async_remote_copy(
            src, self.all.at[plane, rows],
            self.send.at[hop - 1, index, chunk], self.recv.at[hop - 1, index, chunk],
            device_id=(self.z + side, self.f), device_id_type=MESH,
        )

    def greet(self):
        for side in self.sides:

            @pl.when(self.exists(self.z + side))
            def _(side=side):
                pl.semaphore_signal(
                    self.barrier, 1, device_id=(self.z + side, self.f), device_id_type=MESH
                )

    def neighbours(self):
        return jnp.minimum(self.z, 1) + jnp.minimum(self.n - 1 - self.z, 1)

    def pass_on(self, hop, chunk):
        for index, side in enumerate(self.sides):
            plane = self.z - side * (hop - 1)

            @pl.when(self.exists(self.z + side) & self.exists(plane))
            def _(index=index, plane=plane):
                self.copy(hop, index, chunk, plane).start()

    def arrive(self, hop, chunk):
        for index, side in enumerate(self.sides):
            plane = self.z - side * hop

            @pl.when(self.exists(plane))
            def _(index=index, plane=plane):
                self.copy(hop, index, chunk, plane).wait_recv()

    def begin(self):
        self.keep.start()
        for chunk in range(2):
            self.pass_on(1, chunk)

    def event(self, number):
        hop, chunk = 1 + number // 2, number % 2
        self.arrive(hop, chunk)
        self.pass_on(hop + 1, chunk)

    def end(self):
        self.keep.wait()
        for chunk in range(2):
            self.arrive(self.n - 1, chunk)
            for hop in range(1, self.n):
                for index, side in enumerate(self.sides):
                    plane = self.z - side * (hop - 1)

                    @pl.when(self.exists(self.z + side) & self.exists(plane))
                    def _(index=index, plane=plane, hop=hop, chunk=chunk):
                        self.copy(hop, index, chunk, plane).wait_send()


def gelu_parts(pre):
    scale = 0.7978845608028654
    square = pre * pre
    flat = jnp.tanh(scale * pre * (1.0 + 0.044715 * square))
    half = 0.5 * (1.0 + flat)
    slope = half + (0.5 * scale) * pre * (1.0 - flat * flat) * (1.0 + 0.134145 * square)
    return half * pre, slope


def forward_kernel(
    n_f, n_long, n_rows, long_ref, short_ref, o_ref, w_ref, vec_ref, row_ref, g_ref, up_ref,
    own_ref, h_ref, there_ref, act_ref, slope_ref, gd_ref, down_ref,
    rows_ref, vec_scr, out_buf, in_buf, all_ref, send, recv, line_send, line_recv, line_sem,
):
    i = pl.program_id(0)
    z = lax.axis_index("dp")
    f, partner = peers(n_f)
    cap, width = out_buf.shape[1:]
    n_up = n_rows + n_f
    n_down = n_up + n_f
    barrier = pltpu.get_barrier_semaphore()
    line = Line(own_ref, down_ref, line_send, line_recv, line_sem)
    n_events = 2 * (line.n - 2)

    def transfer(k):
        return pltpu.make_async_remote_copy(
            out_buf.at[k], in_buf.at[f], send.at[k], recv.at[k],
            device_id=(z, partner(k)), device_id_type=MESH,
        )

    @pl.when(i == 0)
    def _():
        greet(n_f, partner)
        line.greet()
        vec_scr[...] = vectors(vec_ref)
        pl.semaphore_wait(barrier, n_f - 1 + line.neighbours())
        line.begin()

    def body(x_ref):
        hidden = x_ref[...] + dot(o_ref[...], w_ref[...], NT)
        h_ref[...] = hidden
        normed, _ = norm_parts(hidden)
        rows_ref[pl.ds(pl.multiple_of(i * ROWS, ROWS), ROWS), :] = (
            normed * vec_scr[2:3, :] + vec_scr[3:4, :]
        ).astype(BF16)

    pl.when(i < n_long)(lambda: body(long_ref))
    pl.when((i >= n_long) & (i < n_rows))(lambda: body(short_ref))

    @pl.when((i >= n_rows) & (i < n_up - 1))
    def _():
        k = i - n_rows + 1
        out_buf[k] = dispatch_block(row_ref, rows_ref[...], partner(k) * cap, cap)
        transfer(k).start()

    @pl.when(i == n_up - 1)
    def _():
        in_buf[f] = dispatch_block(row_ref, rows_ref[...], f * cap, cap)

    @pl.when((i > n_up) & (i < n_down))
    def _():
        transfer(i - n_up).wait_recv()

    for number in range(n_events):
        at = n_up + 1 + number * (n_f - 1) // (n_events - 1)
        pl.when(i == at)(functools.partial(line.event, number))

    @pl.when((i >= n_up) & (i < n_down))
    def _():
        origin = partner(i - n_up)
        rows = in_buf[origin]
        here = pl.ds(pl.multiple_of(origin * cap, cap), cap)
        for first in range(0, up_ref.shape[1], width):
            cut = slice(first, first + width)
            act, slope = gelu_parts(dot(rows, up_ref[:, cut]))
            act = act.astype(BF16)
            act_ref[:, cut] = act
            slope_ref[:, cut] = slope.astype(BF16)
            all_ref[here, cut] = act
        there_ref[here, :] = rows

    @pl.when(i >= n_down)
    def _():
        cut = pl.ds(pl.multiple_of((i - n_down) * width, width), width)
        gd_ref[...] = dot(all_ref[:, cut], g_ref[...], TN).astype(BF16)

    @pl.when(i == pl.num_programs(0) - 1)
    def _():
        for k in range(1, n_f):
            transfer(k).wait_send()
        line.end()


def forward_experts(long_x, short_x, o, dense, slot_row, g_there, up, own_down, n_dp, n_f, cap):
    width = long_x.shape[1]
    hidden = up.shape[1]
    n_long, n_short = long_x.shape[0] // ROWS, short_x.shape[0] // ROWS
    n_rows = n_long + n_short
    n_up = n_rows + n_f
    n_down = n_up + n_f
    n_hidden = hidden // width
    slots = n_f * cap
    count = o.shape[0]
    tile = pl.BlockSpec((cap, hidden), lambda i: (jnp.clip(i - n_up, 0, n_f - 1), 0))
    return pl.pallas_call(
        functools.partial(forward_kernel, n_f, n_long, n_rows),
        grid=(n_down + n_hidden,),
        in_specs=[
            pl.BlockSpec((ROWS, width), lambda i: (jnp.minimum(i, n_long - 1), 0)),
            pl.BlockSpec((ROWS, width), lambda i: (jnp.clip(i - n_long, 0, n_short - 1), 0)),
            pl.BlockSpec((ROWS, width), lambda i: (jnp.minimum(i, n_rows - 1), 0)),
            pl.BlockSpec((width, width), lambda i: (0, 3), pipeline_mode=pl.Buffered(1)),
            pl.BlockSpec((width, LANES), lambda i: (0, 4 * width // LANES)),
            constant((8, count)),
            constant((slots, width)),
            constant((width, hidden)),
            pl.BlockSpec(memory_space=pl.ANY),
        ],
        out_specs=[
            pl.BlockSpec((ROWS, width), lambda i: (jnp.minimum(i, n_rows - 1), 0)),
            pl.BlockSpec((slots, width), lambda i: (0, 0)),
            tile,
            tile,
            pl.BlockSpec((width, width), lambda i: (jnp.clip(i - n_down, 0, n_hidden - 1), 0)),
            pl.BlockSpec(memory_space=pl.ANY),
        ],
        out_shape=[
            jax.ShapeDtypeStruct((count, width), F32),
            jax.ShapeDtypeStruct((slots, width), BF16),
            jax.ShapeDtypeStruct((slots, hidden), BF16),
            jax.ShapeDtypeStruct((slots, hidden), BF16),
            jax.ShapeDtypeStruct((hidden, width), BF16),
            jax.ShapeDtypeStruct((n_dp,) + own_down.shape, BF16),
        ],
        scratch_shapes=[
            pltpu.VMEM((count, width), BF16),
            pltpu.VMEM((8, width), F32),
            pltpu.VMEM((n_f, cap, width), BF16),
            pltpu.VMEM((n_f, cap, width), BF16),
            pltpu.VMEM((slots, hidden), BF16),
            pltpu.SemaphoreType.DMA((n_f,)),
            pltpu.SemaphoreType.DMA((n_f,)),
            pltpu.SemaphoreType.DMA((n_dp - 1, 2, 2)),
            pltpu.SemaphoreType.DMA((n_dp - 1, 2, 2)),
            pltpu.SemaphoreType.DMA,
        ],
        compiler_params=params(collective_id=2, has_side_effects=True),
        cost_estimate=cost(
            2 * slots * width * (count + 2 * hidden), 60e6, slots * hidden
        ),
        name="forward_experts",
    )(long_x, short_x, o, dense, dense, slot_row, g_there, up, own_down)


def back_kernel(
    n_f, b_ref, g_ref, act_ref, slope_ref, up_ref, down_ref, y_ref, db_ref, gu_ref,
    out_buf, all_ref, send, recv, l_sem,
):
    i = pl.program_id(0)
    z = lax.axis_index("dp")
    f, partner = peers(n_f)
    cap, width = out_buf.shape[1:]
    barrier = pltpu.get_barrier_semaphore()

    def transfer(k):
        return pltpu.make_async_remote_copy(
            out_buf.at[k], db_ref.at[f], send.at[k], recv.at[k],
            device_id=(z, partner(k)), device_id_type=MESH,
        )

    keep = pltpu.make_async_copy(out_buf.at[0], db_ref.at[f], l_sem)

    @pl.when(i == 0)
    def _():
        greet(n_f, partner)

    @pl.when(i < n_f)
    def _():
        k = n_f - 1 - i
        here = pl.ds(pl.multiple_of(partner(k) * cap, cap), cap)
        g = g_ref[here, :]
        d_b = jnp.zeros((cap, width), F32)
        for first in range(0, up_ref.shape[1], width):
            cut = slice(first, first + width)
            d_act = dot(g, down_ref[cut, :], NT)
            d_pre = (d_act * slope_ref[:, cut].astype(F32)).astype(BF16)
            all_ref[here, cut] = d_pre
            d_b = d_b + dot(d_pre, up_ref[:, cut], NT)
        out_buf[k] = d_b.astype(BF16)

    @pl.when(i == 0)
    def _():
        pl.semaphore_wait(barrier, n_f - 1)

    @pl.when(i < n_f - 1)
    def _():
        transfer(n_f - 1 - i).start()

    @pl.when(i == n_f - 1)
    def _():
        keep.start()

    @pl.when(i < n_f)
    def _():
        here = pl.ds(pl.multiple_of(partner(n_f - 1 - i) * cap, cap), cap)
        y_ref[here, :] = dot(act_ref[...], down_ref[...]).astype(BF16)

    @pl.when(i >= n_f)
    def _():
        cut = pl.ds(pl.multiple_of((i - n_f) * width, width), width)
        gu_ref[...] = dot(b_ref[...], all_ref[:, cut], TN).astype(BF16)

    @pl.when(i == pl.num_programs(0) - 1)
    def _():
        keep.wait()
        for k in range(1, n_f):
            transfer(k).wait_recv()
        for k in range(1, n_f):
            transfer(k).wait_send()


def back_experts(b_there, g_there, act, slope, up, down, n_f, cap):
    slots, width = b_there.shape
    hidden = up.shape[1]
    n_hidden = hidden // width
    tile = pl.BlockSpec((cap, hidden), lambda i: (jnp.maximum(n_f - 1 - i, 0), 0))
    return pl.pallas_call(
        functools.partial(back_kernel, n_f),
        grid=(n_f + n_hidden,),
        in_specs=[
            constant((slots, width)),
            constant((slots, width)),
            tile,
            tile,
            constant((width, hidden)),
            constant((hidden, width)),
        ],
        out_specs=[
            pl.BlockSpec((slots, width), lambda i: (0, 0)),
            pl.BlockSpec(memory_space=pl.ANY),
            pl.BlockSpec((width, width), lambda i: (0, jnp.maximum(i - n_f, 0))),
        ],
        out_shape=[
            jax.ShapeDtypeStruct((slots, width), BF16),
            jax.ShapeDtypeStruct((n_f, cap, width), BF16),
            jax.ShapeDtypeStruct((width, hidden), BF16),
        ],
        scratch_shapes=[
            pltpu.VMEM((n_f, cap, width), BF16),
            pltpu.VMEM((slots, hidden), BF16),
            pltpu.SemaphoreType.DMA((n_f,)),
            pltpu.SemaphoreType.DMA((n_f,)),
            pltpu.SemaphoreType.DMA,
        ],
        compiler_params=params(collective_id=3, has_side_effects=True),
        cost_estimate=cost(8 * slots * width * hidden, 60e6),
        name="back_experts",
    )(b_there, g_there, act, slope, up, down)


def combine_rows(col_ref, slots_ref):
    slot_id = lax.broadcasted_iota(jnp.int32, (1, slots_ref.shape[0]), 1)
    chosen = (col_ref[...] == slot_id).astype(F32).astype(BF16)
    return dot(chosen, slots_ref[...])


def hidden_back_kernel(
    n_f, n_long, n_rows, h_ref, col_ref, db_ref, long_ref, short_ref, o_ref, w_ref, vec_ref, y_ref,
    dh_ref, do_ref, gp_ref, gv_ref, yb_ref, acc_ref, vec_scr, send, recv,
):
    i = pl.program_id(0)
    home = Homeward(n_f, early_blocks(n_f), y_ref, yb_ref, send, recv)
    pl.when(i == 0)(home.begin)

    @pl.when(i == 0)
    def _():
        vec_scr[...] = vectors(vec_ref)
        acc_ref[...] = jnp.zeros_like(acc_ref)
        gv_ref[...] = jnp.zeros_like(gv_ref)
        home.launch()

    def body(cot_ref):
        d_b = combine_rows(col_ref, db_ref)
        normed, inv_scale = norm_parts(h_ref[...])
        gv_ref[2:3, :] = gv_ref[2:3, :] + jnp.sum(d_b * normed, 0, keepdims=True)
        gv_ref[3:4, :] = gv_ref[3:4, :] + jnp.sum(d_b, 0, keepdims=True)
        d_h = cot_ref[...] + norm_back(d_b * vec_scr[2:3, :], normed, inv_scale)
        dh_ref[...] = d_h
        d_attn = d_h.astype(BF16)
        do_ref[...] = dot(d_attn, w_ref[...]).astype(BF16)
        acc_ref[...] = acc_ref[...] + dot(d_attn, o_ref[...], TN)

    pl.when(i < n_long)(lambda: body(long_ref))
    pl.when(i >= n_long)(lambda: body(short_ref))

    @pl.when(i == n_rows - 1)
    def _():
        gp_ref[...] = acc_ref[...].astype(BF16)
        home.end()


def hidden_back(h, slot_col, db_back, long_cot, short_cot, o, dense, y):
    n_f = y.shape[0]
    count, width = h.shape
    slots = db_back.shape[0]
    n_long, n_short = long_cot.shape[0] // ROWS, short_cot.shape[0] // ROWS
    n_rows = n_long + n_short
    row = pl.BlockSpec((ROWS, width), lambda i: (i, 0))
    return pl.pallas_call(
        functools.partial(hidden_back_kernel, n_f, n_long, n_rows),
        grid=(n_rows,),
        in_specs=[row, pl.BlockSpec((ROWS, 1), lambda i: (i, 0)), constant((slots, width))]
        + long_short(width, n_long)
        + [
            row,
            pl.BlockSpec((width, width), lambda i: (0, 3)),
            pl.BlockSpec((width, LANES), lambda i: (0, 4 * width // LANES)),
            pl.BlockSpec(memory_space=pl.ANY),
        ],
        out_specs=[
            row,
            row,
            pl.BlockSpec((width, width), lambda i: (0, 0)),
            pl.BlockSpec((LANES, width), lambda i: (0, 0)),
            pl.BlockSpec(memory_space=pl.ANY),
        ],
        out_shape=[
            jax.ShapeDtypeStruct((count, width), F32),
            jax.ShapeDtypeStruct((count, width), BF16),
            jax.ShapeDtypeStruct((width, width), BF16),
            jax.ShapeDtypeStruct((LANES, width), F32),
            jax.ShapeDtypeStruct(y.shape, BF16),
        ],
        scratch_shapes=[
            pltpu.VMEM((width, width), F32),
            pltpu.VMEM((8, width), F32),
            pltpu.SemaphoreType.DMA((n_f,)),
            pltpu.SemaphoreType.DMA((n_f,)),
        ],
        compiler_params=params(collective_id=6, has_side_effects=True),
        cost_estimate=cost(2 * (slots + 2 * width) * count * width, 16 * count * width),
        name="hidden_back",
    )(h, slot_col, db_back, long_cot, short_cot, o, dense, dense, y)


def grads_kernel(
    n_long, n_rows, width, long_ref, short_ref, d_ref, w_ref, vec_ref, gp_ref, gv_ref,
    out_ref, acc_ref, vec_scr, sum_scr,
):
    i = pl.program_id(0)

    @pl.when(i == 0)
    def _():
        vec_scr[...] = vectors(vec_ref)
        acc_ref[...] = jnp.zeros_like(acc_ref)
        sum_scr[...] = jnp.zeros_like(sum_scr)

    def body(x_ref):
        normed, _ = norm_parts(x_ref[...])
        rows = (normed * vec_scr[0:1, :] + vec_scr[1:2, :]).astype(BF16)
        for part in range(3):
            cut = slice(part * width, (part + 1) * width)
            acc_ref[:, cut] = acc_ref[:, cut] + dot(rows, d_ref[part], TN)
            sum_scr[:, cut] = sum_scr[:, cut] + jnp.sum(
                d_ref[part].astype(F32), 0, keepdims=True
            )

    pl.when(i < n_long)(lambda: body(long_ref))
    pl.when(i >= n_long)(lambda: body(short_ref))

    @pl.when(i == n_rows - 1)
    def _():
        out_ref[:, :width] = gp_ref[...]
        out_ref[:, width : 4 * width] = acc_ref[...].astype(BF16)
        weighted = jnp.zeros((width, 1), F32)
        bias_grad = jnp.zeros((width, 1), F32)
        for part in range(3):
            cut = slice(part * width, (part + 1) * width)
            weight = w_ref[:, cut].astype(F32)
            weighted = weighted + jnp.sum(weight * acc_ref[:, cut], 1, keepdims=True)
            bias_grad = bias_grad + jnp.sum(weight * sum_scr[:, cut], 1, keepdims=True)
        out_ref[:, 4 * width :] = norm1_grads(weighted, bias_grad, vec_ref, gv_ref)


def dense_grads(long_x, short_x, d_qkv, dense, grad_proj, grad_vec):
    count, width = d_qkv.shape[1:]
    n_long, n_short = long_x.shape[0] // ROWS, short_x.shape[0] // ROWS
    n_rows = n_long + n_short
    return pl.pallas_call(
        functools.partial(grads_kernel, n_long, n_rows, width),
        grid=(n_rows,),
        in_specs=long_short(width, n_long)
        + [
            pl.BlockSpec((3, ROWS, width), lambda i: (0, i, 0)),
            constant((width, 3 * width)),
            pl.BlockSpec((width, LANES), lambda i: (0, 4 * width // LANES)),
            constant((width, width)),
            constant((LANES, width)),
        ],
        out_specs=pl.BlockSpec((width, 4 * width + LANES), lambda i: (0, 0)),
        out_shape=jax.ShapeDtypeStruct((width, 4 * width + LANES), BF16),
        scratch_shapes=[
            pltpu.VMEM((width, 3 * width), F32),
            pltpu.VMEM((8, width), F32),
            pltpu.VMEM((1, 3 * width), F32),
        ],
        compiler_params=params(),
        cost_estimate=cost(6 * count * width * width, 16 * count * width),
        name="dense_grads",
    )(long_x, short_x, d_qkv, dense, dense, grad_proj, grad_vec)


class Reducer:
    def __init__(self, part_ref, out_ref, chunks, scratch):
        self.part, self.out, self.chunks = part_ref, out_ref, chunks
        self.got1, self.sum1, self.got2, self.sum2, self.got3 = scratch[:5]
        self.sems = scratch[5:]
        self.n_dp, self.n_f = part_ref.shape[:2]
        self.z = lax.axis_index("dp")
        self.f = lax.axis_index("fsdp")
        self.half = self.n_f // 2
        self.parity = lax.rem(self.f, 2)
        self.mine = self.f // 2
        self.partner = self.f + 1 - 2 * self.parity
        self.order = list(range(1, self.half)) + [0]
        self.barrier = pltpu.get_barrier_semaphore()

    def greet(self):
        z, f = self.z, self.f
        for k in range(1, self.n_dp):
            pl.semaphore_signal(
                self.barrier, 1, device_id=(lax.rem(z + k, self.n_dp), f), device_id_type=MESH
            )
        for k in range(1, self.half):
            pl.semaphore_signal(
                self.barrier, 1, device_id=(z, lax.rem(f + 2 * k, self.n_f)), device_id_type=MESH
            )
        pl.semaphore_signal(self.barrier, 1, device_id=(z, self.partner), device_id_type=MESH)

    def meet(self):
        pl.semaphore_wait(self.barrier, self.n_dp - 1 + self.half)

    def slot(self, k):
        return lax.rem(self.mine + k, self.half)

    def core_copy(self, c, k):
        cut, slot = self.chunks[c], self.slot(k)
        return pltpu.make_async_remote_copy(
            self.part.at[:, 2 * slot + 1 - self.parity, :, cut], self.got1.at[slot, :, :, cut],
            self.sems[0].at[c, k], self.sems[1].at[c, k],
            device_id=(self.z, self.partner), device_id_type=MESH,
        )

    def chip_copy(self, c, k):
        cut = self.chunks[c]
        return pltpu.make_async_remote_copy(
            self.sum1.at[self.slot(k), :, :, cut], self.got2.at[k, :, :, cut],
            self.sems[2].at[c, k], self.sems[3].at[c, k],
            device_id=(self.z, lax.rem(self.f + 2 * k, self.n_f)), device_id_type=MESH,
        )

    def plane_copy(self, c, k):
        cut, there = self.chunks[c], lax.rem(self.z + k, self.n_dp)
        return pltpu.make_async_remote_copy(
            self.sum2.at[there, :, cut], self.got3.at[k, :, cut],
            self.sems[4].at[c, k], self.sems[5].at[c, k],
            device_id=(there, self.f), device_id_type=MESH,
        )

    def start_core(self, c):
        for k in self.order:
            self.core_copy(c, k).start()

    def start_chip(self, c):
        cut = self.chunks[c]
        for k in self.order:
            slot = self.slot(k)
            self.core_copy(c, k).wait_recv()
            self.sum1[slot, :, :, cut] = (
                self.part[:, 2 * slot + self.parity, :, cut].astype(F32)
                + self.got1[slot, :, :, cut].astype(F32)
            ).astype(BF16)
            if k:
                self.chip_copy(c, k).start()

    def start_plane(self, c):
        cut = self.chunks[c]
        total = self.sum1[self.mine, :, :, cut].astype(F32)
        for k in range(1, self.half):
            self.chip_copy(c, k).wait_recv()
            total = total + self.got2[k, :, :, cut].astype(F32)
        self.sum2[:, :, cut] = total.astype(BF16)
        for k in range(1, self.n_dp):
            self.plane_copy(c, k).start()

    def close(self, c):
        cut = self.chunks[c]
        total = self.sum2[self.z, :, cut].astype(F32)
        for k in range(1, self.n_dp):
            self.plane_copy(c, k).wait_recv()
            total = total + self.got3[k, :, cut].astype(F32)
        self.out[:, cut] = total

    def drain(self):
        for c in range(len(self.chunks)):
            for k in range(self.half):
                self.core_copy(c, k).wait_send()
            for k in range(1, self.half):
                self.chip_copy(c, k).wait_send()
            for k in range(1, self.n_dp):
                self.plane_copy(c, k).wait_send()


def reducer_scratch(n_chunks, n_dp, n_f, share, columns):
    half = n_f // 2
    return [
        pltpu.VMEM((half, n_dp, share, columns), BF16),
        pltpu.VMEM((half, n_dp, share, columns), BF16),
        pltpu.VMEM((half, n_dp, share, columns), BF16),
        pltpu.VMEM((n_dp, share, columns), BF16),
        pltpu.VMEM((n_dp, share, columns), BF16),
        pltpu.SemaphoreType.DMA((n_chunks, half)),
        pltpu.SemaphoreType.DMA((n_chunks, half)),
        pltpu.SemaphoreType.DMA((n_chunks, half)),
        pltpu.SemaphoreType.DMA((n_chunks, half)),
        pltpu.SemaphoreType.DMA((n_chunks, n_dp)),
        pltpu.SemaphoreType.DMA((n_chunks, n_dp)),
    ]


def input_grad(x_ref, dh_ref, d_ref, w_ref, vec_scr, grad_ref):
    width = dh_ref.shape[1]
    normed, inv_scale = norm_parts(x_ref)
    entered = jnp.zeros_like(normed)
    for part in range(3):
        entered = entered + dot(d_ref[part], w_ref[:, part * width : (part + 1) * width], NT)
    grad_ref[...] = dh_ref[...] + norm_back(entered * vec_scr[0:1, :], normed, inv_scale)


def norm1_grads(weighted, bias_grad, vec_ref, gv_ref):
    gain, bias = vec_ref[:, 0:1].astype(F32), vec_ref[:, 1:2].astype(F32)
    lane = lax.broadcasted_iota(jnp.int32, (1, LANES), 1)
    found = jnp.transpose(gv_ref[...])
    found = jnp.where(lane == 0, (weighted - bias * bias_grad) / gain, found)
    return jnp.where(lane == 1, bias_grad, found).astype(BF16)


def last_kernel(
    n_long, n_rows, part_ref, long_ref, short_ref, dh_ref, d_ref, w_ref, vec_ref,
    h_ref, col_ref, y_ref, out_ref, lg_ref, sg_ref, lo_ref, so_ref, vec_scr, *scratch,
):
    i = pl.program_id(0)
    reducer = Reducer(part_ref, out_ref, column_chunks(part_ref.shape[3]), scratch)

    @pl.when(i == 0)
    def _():
        reducer.greet()
        vec_scr[...] = vectors(vec_ref)
        reducer.meet()
        for c in range(N_CHUNKS):
            reducer.start_core(c)

    def back(x_ref, grad_ref):
        input_grad(x_ref[...], dh_ref, d_ref, w_ref, vec_scr, grad_ref)

    pl.when(i < n_long)(lambda: back(long_ref, lg_ref))
    pl.when((i >= n_long) & (i < n_rows))(lambda: back(short_ref, sg_ref))

    @pl.when(i == 0)
    def _():
        for c in range(N_CHUNKS):
            reducer.start_chip(c)

    def finish(out):
        out[...] = h_ref[...] + combine_rows(col_ref, y_ref)

    pl.when((i >= n_rows) & (i < n_rows + n_long))(lambda: finish(lo_ref))
    pl.when((i >= n_rows + n_long) & (i < 2 * n_rows))(lambda: finish(so_ref))

    @pl.when(i == 2 * n_rows - 1)
    def _():
        for c in range(N_CHUNKS):
            reducer.start_plane(c)
        for c in range(N_CHUNKS):
            reducer.close(c)
        reducer.drain()


def last_stage(partial, long_x, short_x, d_h, d_qkv, dense, h, slot_col, y_back):
    n_dp, n_f, share, columns = partial.shape
    count, width = d_h.shape
    n_long, n_short = long_x.shape[0] // ROWS, short_x.shape[0] // ROWS
    n_rows = n_long + n_short
    slots = y_back.shape[0]
    row = pl.BlockSpec((ROWS, width), lambda i: (jnp.minimum(i, n_rows - 1), 0))
    late = lambda i: (jnp.clip(i - n_rows, 0, n_rows - 1), 0)
    return pl.pallas_call(
        functools.partial(last_kernel, n_long, n_rows),
        grid=(2 * n_rows,),
        in_specs=[
            constant(partial.shape),
            pl.BlockSpec((ROWS, width), lambda i: (jnp.minimum(i, n_long - 1), 0)),
            pl.BlockSpec((ROWS, width), lambda i: (jnp.clip(i - n_long, 0, n_short - 1), 0)),
            row,
            pl.BlockSpec((3, ROWS, width), lambda i: (0, jnp.minimum(i, n_rows - 1), 0)),
            constant((width, 3 * width)),
            pl.BlockSpec((width, LANES), lambda i: (0, 4 * width // LANES)),
            pl.BlockSpec((ROWS, width), late),
            pl.BlockSpec((ROWS, 1), late),
            constant((slots, width)),
        ],
        out_specs=[
            pl.BlockSpec((share, columns), lambda i: (0, 0)),
            pl.BlockSpec((ROWS, width), lambda i: (jnp.minimum(i, n_long - 1), 0)),
            pl.BlockSpec((ROWS, width), lambda i: (jnp.clip(i - n_long, 0, n_short - 1), 0)),
            pl.BlockSpec((ROWS, width), lambda i: (jnp.clip(i - n_rows, 0, n_long - 1), 0)),
            pl.BlockSpec(
                (ROWS, width), lambda i: (jnp.clip(i - n_rows - n_long, 0, n_short - 1), 0)
            ),
        ],
        out_shape=[
            jax.ShapeDtypeStruct((share, columns), F32),
            jax.ShapeDtypeStruct(long_x.shape, F32),
            jax.ShapeDtypeStruct(short_x.shape, F32),
            jax.ShapeDtypeStruct(long_x.shape, F32),
            jax.ShapeDtypeStruct(short_x.shape, F32),
        ],
        scratch_shapes=[pltpu.VMEM((8, width), F32)]
        + reducer_scratch(N_CHUNKS, n_dp, n_f, share, columns),
        compiler_params=params(collective_id=1, has_side_effects=True),
        cost_estimate=cost(2 * count * width * (3 * width + slots), 60e6),
        name="last_stage",
    )(partial, long_x, short_x, d_h, d_qkv, dense, dense, h, slot_col, y_back)


def close_kernel(
    n_long, n_rows, proj_ref, gv_ref, long_ref, short_ref, dp_ref, dh_ref, d_ref, w_ref, vec_ref,
    h_ref, col_ref, y_ref, out_ref, lg_ref, sg_ref, lo_ref, so_ref,
    vec_scr, rows_ref, part_ref, stat_ref, *scratch,
):
    i = pl.program_id(0)
    n_dp, n_f, share, columns = part_ref.shape
    width = dh_ref.shape[1]
    chunks = [slice(c * width, (c + 1) * width) for c in range(3)] + [slice(3 * width, columns)]
    reducer = Reducer(part_ref, out_ref, chunks, scratch)
    begin_back, begin_out = 3, 3 + n_rows

    def scatter(value, cut):
        for index in range(n_dp * n_f):
            part_ref[index // n_f, index % n_f, :, cut] = value[
                index * share : (index + 1) * share
            ].astype(BF16)

    @pl.when(i == 0)
    def _():
        reducer.greet()
        vec_scr[...] = vectors(vec_ref)
        part_ref[:, :, :, :width] = proj_ref[...]
        reducer.meet()
        reducer.start_core(0)
        n = long_ref.shape[0]
        for ref, first in ((long_ref, 0), (short_ref, n)):
            for start in range(0, ref.shape[0], ROWS):
                normed, _ = norm_parts(ref[start : start + ROWS, :])
                rows_ref[first + start : first + start + ROWS, :] = (
                    normed * vec_scr[0:1, :] + vec_scr[1:2, :]
                ).astype(BF16)
        stat_ref[...] = jnp.zeros_like(stat_ref)
        reducer.start_chip(0)

    for part in range(3):

        @pl.when(i == part)
        def _(part=part):
            value = dot(rows_ref[...], dp_ref[0], TN)
            scatter(value, slice((part + 1) * width, (part + 2) * width))
            weight = w_ref[:, part * width : (part + 1) * width].astype(F32)
            sums = jnp.sum(dp_ref[0].astype(F32), 0, keepdims=True)
            stat_ref[:, 0:1] = stat_ref[:, 0:1] + jnp.sum(weight * value, 1, keepdims=True)
            stat_ref[:, 1:2] = stat_ref[:, 1:2] + jnp.sum(weight * sums, 1, keepdims=True)
            if part == 2:
                found = norm1_grads(stat_ref[:, 0:1], stat_ref[:, 1:2], vec_ref, gv_ref)
                scatter(found.astype(F32), slice(4 * width, columns))
            reducer.start_core(part + 1)
            if part:
                reducer.start_chip(part)

    @pl.when(i == begin_back)
    def _():
        reducer.start_chip(3)

    def back(x_ref, index, grad_ref):
        rows = pl.ds(pl.multiple_of(index * ROWS, ROWS), ROWS)
        input_grad(x_ref[rows, :], dh_ref, d_ref, w_ref, vec_scr, grad_ref)

    j = i - begin_back
    pl.when((j >= 0) & (j < n_long))(lambda: back(long_ref, j, lg_ref))
    pl.when((j >= n_long) & (j < n_rows))(lambda: back(short_ref, j - n_long, sg_ref))

    def finish(out):
        out[...] = h_ref[...] + combine_rows(col_ref, y_ref)

    m = i - begin_out
    pl.when((m >= 0) & (m < n_long))(lambda: finish(lo_ref))
    pl.when((m >= n_long) & (m < n_rows))(lambda: finish(so_ref))

    pl.when(i == begin_back + 1)(lambda: reducer.start_plane(0))
    pl.when(i == begin_out - 1)(lambda: reducer.start_plane(1))
    pl.when(i == begin_out + n_rows - 2)(lambda: reducer.start_plane(2))

    @pl.when(i == begin_out + n_rows - 1)
    def _():
        reducer.start_plane(3)
        for c in range(4):
            reducer.close(c)
        reducer.drain()


def close_stage(grad_proj, grad_vec, long_x, short_x, d_h, d_qkv, dense, h, slot_col, y_back):
    n_dp, n_f, share = grad_proj.shape[:3]
    count, width = d_h.shape
    columns = 4 * width + LANES
    n_long, n_short = long_x.shape[0] // ROWS, short_x.shape[0] // ROWS
    n_rows = n_long + n_short
    slots = y_back.shape[0]
    step = lambda i, base, last: jnp.clip(i - base, 0, last)
    return pl.pallas_call(
        functools.partial(close_kernel, n_long, n_rows),
        grid=(3 + 2 * n_rows,),
        in_specs=[
            constant(grad_proj.shape),
            constant(grad_vec.shape),
            constant(long_x.shape),
            constant(short_x.shape),
            pl.BlockSpec((1, count, width), lambda i: (jnp.minimum(i, 2), 0, 0)),
            pl.BlockSpec((ROWS, width), lambda i: (step(i, 3, n_rows - 1), 0)),
            pl.BlockSpec((3, ROWS, width), lambda i: (0, step(i, 3, n_rows - 1), 0)),
            constant((width, 3 * width)),
            pl.BlockSpec((width, LANES), lambda i: (0, 4 * width // LANES)),
            pl.BlockSpec((ROWS, width), lambda i: (step(i, 3 + n_rows, n_rows - 1), 0)),
            pl.BlockSpec((ROWS, 1), lambda i: (step(i, 3 + n_rows, n_rows - 1), 0)),
            constant((slots, width)),
        ],
        out_specs=[
            pl.BlockSpec((share, columns), lambda i: (0, 0)),
            pl.BlockSpec((ROWS, width), lambda i: (step(i, 3, n_long - 1), 0)),
            pl.BlockSpec((ROWS, width), lambda i: (step(i, 3 + n_long, n_short - 1), 0)),
            pl.BlockSpec((ROWS, width), lambda i: (step(i, 3 + n_rows, n_long - 1), 0)),
            pl.BlockSpec((ROWS, width), lambda i: (step(i, 3 + n_rows + n_long, n_short - 1), 0)),
        ],
        out_shape=[
            jax.ShapeDtypeStruct((share, columns), F32),
            jax.ShapeDtypeStruct(long_x.shape, F32),
            jax.ShapeDtypeStruct(short_x.shape, F32),
            jax.ShapeDtypeStruct(long_x.shape, F32),
            jax.ShapeDtypeStruct(short_x.shape, F32),
        ],
        scratch_shapes=[
            pltpu.VMEM((8, width), F32),
            pltpu.VMEM((count, width), BF16),
            pltpu.VMEM((n_dp, n_f, share, columns), BF16),
            pltpu.VMEM((width, LANES), F32),
        ]
        + reducer_scratch(4, n_dp, n_f, share, columns),
        compiler_params=params(collective_id=4, has_side_effects=True),
        cost_estimate=cost(2 * count * width * (6 * width + slots), 60e6),
        name="close_stage",
    )(grad_proj, grad_vec, long_x, short_x, d_qkv, d_h, d_qkv, dense, dense, h, slot_col, y_back)


def ship_kernel(n_long, width, *refs):
    i = pl.program_id(0)
    arrays_in, (owned_ref, down_ref), rest = refs[:4], refs[4:6], refs[6:]
    arrays_out, (qkv_ref, proj_ref, grad_ref), vec_refs, pad_ref = rest[:4], rest[4:7], rest[7:11], rest[11]
    for first in (0, 2):

        @pl.when(i < n_long)
        def _():
            arrays_out[first][...] = arrays_in[first][...]

        @pl.when(i >= n_long)
        def _():
            arrays_out[first + 1][...] = arrays_in[first + 1][...]

    grad_ref[...] = down_ref[...].astype(F32)

    @pl.when(i == 0)
    def _():
        share = owned_ref.shape[0]
        qkv_ref[...] = owned_ref[:, width : 4 * width]
        pad_ref[...] = jnp.zeros_like(pad_ref)
        pad_ref[:share, :] = owned_ref[:, 4 * width :]
        proj_ref[...] = owned_ref[:, :width]
        turned = jnp.transpose(pad_ref[...])
        for row, vec_ref in enumerate(vec_refs):
            vec_ref[...] = turned[row : row + 1, :share]


def ship(arrays, owned, grad_down):
    width = arrays[0].shape[1]
    n_long, n_short = arrays[0].shape[0] // ROWS, arrays[1].shape[0] // ROWS
    steps = n_long + n_short
    share = owned.shape[0]
    piece = pl.BlockSpec((grad_down.shape[0] // steps, width), lambda i: (i, 0))
    whole = lambda shape: pl.BlockSpec(shape, lambda i: (0, 0))
    return pl.pallas_call(
        functools.partial(ship_kernel, n_long, width),
        grid=(steps,),
        in_specs=long_short(width, n_long) * 2 + [constant(owned.shape), piece],
        out_specs=long_short(width, n_long) * 2
        + [whole((share, 3 * width)), whole((share, width)), piece]
        + [whole((1, share))] * 4,
        out_shape=[jax.ShapeDtypeStruct(a.shape, a.dtype) for a in arrays]
        + [
            jax.ShapeDtypeStruct((share, 3 * width), F32),
            jax.ShapeDtypeStruct((share, width), F32),
            jax.ShapeDtypeStruct(grad_down.shape, F32),
        ]
        + [jax.ShapeDtypeStruct((1, share), F32)] * 4,
        scratch_shapes=[pltpu.VMEM((LANES, LANES), F32)],
        compiler_params=params(),
        cost_estimate=cost(0, sum(8 * a.size for a in arrays)),
        name="ship",
    )(*arrays, owned, grad_down)


def on_device(
    n_dp, n_f, long_x, short_x, long_len, short_len, expert_ids, ln1_gain, ln1_bias,
    w_qkv, w_proj, ln2_gain, ln2_bias, w_up, w_down, long_cot, short_cot,
):
    width = long_x.shape[2]
    share = w_qkv.shape[0]
    seqs = sequences(long_x.shape[:2], short_x.shape[:2])
    flat = lambda a: a.reshape(-1, width)
    xl, xs, gl, gs = flat(long_x), flat(short_x), flat(long_cot), flat(short_cot)
    n_long, n_short = xl.shape[0] // ROWS, xs.shape[0] // ROWS
    experts = n_f * w_up.shape[0]
    cap = 4 * expert_ids.shape[0] // (3 * experts)
    slots = experts * cap

    up = lax.all_gather(w_up, "dp", axis=2, tiled=True)[0]

    vec = jnp.stack([ln1_gain, ln1_bias, ln2_gain, ln2_bias], 1)
    own = jnp.concatenate(
        [w_qkv, w_proj.T, jnp.pad(vec, ((0, 0), (0, LANES - vec.shape[1])))], 1
    )
    dense, slot_col, slot_row, g_slots = gather_dense(
        own, expert_ids, gl, gs, n_dp, n_f, cap, slots
    )
    dense = dense.reshape(n_dp * n_f * share, own.shape[1])

    def exchange(rows):
        sent = lax.all_to_all(
            rows.reshape(n_f, cap, width), "fsdp", split_axis=0, concat_axis=0, tiled=True
        )
        return sent.reshape(slots, width)

    g_there = exchange(g_slots)
    qkv = make_qkv(xl, xs, dense)
    o, lse = attend(qkv, long_len, short_len, seqs)
    h, b_there, act, slope, grad_down, down = forward_experts(
        xl, xs, o, dense, slot_row, g_there, up, w_down[0], n_dp, n_f, cap
    )
    down = down.reshape(-1, width)
    grad_down = lax.psum_scatter(grad_down, "dp", scatter_dimension=0, tiled=True)
    y, db_back, grad_up = back_experts(b_there, g_there, act, slope, up, down, n_f, cap)
    db_back = db_back.reshape(slots, width)
    grad_up = lax.psum_scatter(grad_up, "dp", scatter_dimension=1, tiled=True)
    y = y.reshape(n_f, cap, width)
    d_h, d_o, grad_proj, grad_vec, y_back = hidden_back(
        h, slot_col, db_back, gl, gs, o, dense, y
    )
    d_qkv, y_back = attend_back(
        qkv, o, d_o, lse, long_len, short_len, seqs, y, y_back
    )
    y_back = y_back.reshape(slots, width)
    if share % 8 == 0:
        owned, long_grad, short_grad, long_out, short_out = close_stage(
            grad_proj.reshape(n_dp, n_f, share, width), grad_vec,
            xl, xs, d_h, d_qkv, dense, h, slot_col, y_back,
        )
    else:
        partial = dense_grads(xl, xs, d_qkv, dense, grad_proj, grad_vec)
        owned, long_grad, short_grad, long_out, short_out = last_stage(
            partial.reshape(n_dp, n_f, share, own.shape[1]),
            xl, xs, d_h, d_qkv, dense, h, slot_col, y_back,
        )
    (long_grad, short_grad, long_out, short_out, grad_qkv, grad_proj, grad_down, *grad_vec) = ship(
        (long_grad, short_grad, long_out, short_out), owned, grad_down
    )
    grad_up, grad_down = lax.optimization_barrier((grad_up, grad_down))
    grad_up = grad_up.astype(F32)
    return (
        long_out.reshape(long_x.shape),
        short_out.reshape(short_x.shape),
        long_grad.reshape(long_x.shape),
        short_grad.reshape(short_x.shape),
        grad_vec[0].reshape(-1),
        grad_vec[1].reshape(-1),
        grad_qkv,
        grad_proj.T,
        grad_vec[2].reshape(-1),
        grad_vec[3].reshape(-1),
        grad_up[None],
        grad_down[None],
    )


def solution(mesh):
    both = ("dp", "fsdp")
    return jax.shard_map(
        functools.partial(on_device, mesh.shape["dp"], mesh.shape["fsdp"]),
        mesh=mesh,
        in_specs=(
            P(both, None, None),
            P(both, None, None),
            P(both),
            P(both),
            P(both, None),
            P(both),
            P(both),
            P(both, None),
            P(None, both),
            P(both),
            P(both),
            P("fsdp", None, "dp"),
            P("fsdp", "dp", None),
            P(both, None, None),
            P(both, None, None),
        ),
        out_specs=(
            P(both, None, None),
            P(both, None, None),
            P(both, None, None),
            P(both, None, None),
            P(both),
            P(both),
            P(both, None),
            P(None, both),
            P(both),
            P(both),
            P("fsdp", None, "dp"),
            P("fsdp", "dp", None),
        ),
        check_vma=False,
    )
```
